32 devices in a mesh: img: 4 (over y, x), ha: 4 (over z), wa: 2 (over core).
Axes of the slice: x: 2, y: 2, z: 4, core: 2. Of those that a mesh axis runs over, the one named last changes fastest.
Arguments:
- images: bfloat16 [16, 64, 32, 512], P('img', 'ha', 'wa'), may hold values from -32 to 32
- cot_shared: bfloat16 [16, 32, 16, 512], P('img', 'ha', 'wa'), may hold values from -32 to 32
- cot_tasks: bfloat16 [16, 32, 16, 1536], P('img', 'ha', 'wa'), may hold values from -32 to 32
- depth_mask: int32 [16, 32, 16], P('img', 'ha', 'wa'), may hold values 0 or 1
- nash_weights: float32 [3], replicated, may hold values from 0.5 to 2
- conv_weight: float32 [16, 45, 128, 128], P(('img', 'ha')), may hold values from -0.09375 to 0.09375
- conv_left: float32 [16, 45, 128, 128], P(('img', 'ha')), as said below
- conv_right: float32 [16, 45, 128, 128], P(('img', 'ha')), as said below
- conv_left_root: float32 [16, 45, 128, 128], P(('img', 'ha')), as said below
- conv_right_root: float32 [16, 45, 128, 128], P(('img', 'ha')), as said below
- proj_weight: float32 [3, 2, 4, 128, 128], replicated
- proj_left: float32 [3, 2, 4, 128, 128], replicated, as said below
- proj_right: float32 [3, 2, 4, 128, 128], replicated, as said below
- proj_left_root: float32 [3, 2, 4, 128, 128], replicated, as said below
- proj_right_root: float32 [3, 2, 4, 128, 128], replicated, as said below
- norm_params: float32 [2, 2944], replicated
- norm_moment: float32 [2, 2944], replicated, as said below
Outputs:
- shared_out: bfloat16 [16, 32, 16, 512], P('img', 'ha', 'wa')
- task_out: bfloat16 [16, 32, 16, 1536], P('img', 'ha', 'wa')
- image_grad: bfloat16 [16, 64, 32, 512], P('img', 'ha', 'wa')
- gram: float32 [3, 3], replicated
- conv_grad: float32 [16, 45, 128, 128], P(('img', 'ha'))
- conv_left_new: float32 [16, 45, 128, 128], P(('img', 'ha'))
- conv_right_new: float32 [16, 45, 128, 128], P(('img', 'ha'))
- conv_weight_new: float32 [16, 45, 128, 128], P(('img', 'ha'))
- proj_grad: float32 [3, 2, 4, 128, 128], replicated
- proj_left_new: float32 [3, 2, 4, 128, 128], replicated
- proj_right_new: float32 [3, 2, 4, 128, 128], replicated
- proj_weight_new: float32 [3, 2, 4, 128, 128], replicated
- norm_grad: float32 [2, 2944], replicated
- norm_moment_new: float32 [2, 2944], replicated
- norm_new: float32 [2, 2944], replicated
The draws below stay inside these ranges and needn't reach their ends.
Inputs may be any that keep to these rules, and one draw needn't show every extreme that they name: `conv_left`: symmetric. `conv_right`: symmetric. `conv_left_root`: symmetric. `conv_right_root`: symmetric. `proj_left`: symmetric. `proj_right`: symmetric. `proj_left_root`: symmetric. `proj_right_root`: symmetric. `norm_moment`: positive.
All inputs are finite; a program needn't handle non-finite values. No bound on the sum of `depth_mask` on one device may be relied on, other than what follows from the above.
Results may differ from the reference program's by a relative error of at most 0.015.
Values may be sent and summed in bfloat16 or wider, within the bound.
No kernel may reach another device: no remote copies, remote signals or barrier semaphores. Data moves between devices by JAX's collectives and lax.ppermute only.
A program may use at most 384 MiB of HBM per device.

```python
import math
import jax
import jax.numpy as jnp
from jax import lax

C = 512
CA = 128
TASKS = 3
BLK = 128
NBLK = 4
MATS = 45
NBN = 2944
BATCH = 16
HEIGHT = 64
WIDTH = 32


def ramped(key, batch_count, height, width, depth):
    shape_full = (batch_count, height, width, depth)
    base = jnp.clip(jax.random.normal(key, shape_full, jnp.float32), -6.0, 6.0)
    growth = 3.0
    level_batch = jnp.arange(batch_count, dtype=jnp.float32) / (batch_count - 1)
    level_rows = jnp.arange(height, dtype=jnp.float32) / (height - 1)
    level_cols = jnp.arange(width, dtype=jnp.float32) / (width - 1)
    level = level_batch[:, None, None] + level_rows[None, :, None] + level_cols[None, None, :]
    return base * jnp.exp((level - 1.5) * math.log(growth))[..., None]


def symmetric_blocks(key, leading, factor):
    upper_end = 4.0
    key_diag, key_off = jax.random.split(key)
    diagonal = jnp.exp(jax.random.uniform(key_diag, leading + (BLK,), jnp.float32, 0.0, math.log(upper_end)))
    noise = jax.random.uniform(key_off, leading + (BLK, BLK), jnp.float32, -0.1, 0.1)
    noise = 0.5 * (noise + jnp.swapaxes(noise, -1, -2))
    identity = jnp.eye(BLK, dtype=jnp.float32)
    return factor * (noise * (1.0 - identity) + diagonal[..., None] * identity)


def stat_level(grad_size):
    pixels = BATCH * HEIGHT * WIDTH
    return 1.0 / 9.0 * BLK * grad_size * grad_size * pixels


def draw_images(key, part):
    return ramped(jax.random.fold_in(key, 1), BATCH, HEIGHT, WIDTH, C).astype(jnp.bfloat16)


def draw_cot_shared(key, part):
    return ramped(jax.random.fold_in(key, 2), BATCH, HEIGHT // 2, WIDTH // 2, C).astype(jnp.bfloat16)


def draw_cot_tasks(key, part):
    return ramped(jax.random.fold_in(key, 3), BATCH, HEIGHT // 2, WIDTH // 2, TASKS * C).astype(jnp.bfloat16)


def draw_conv_left(key, part):
    return symmetric_blocks(jax.random.fold_in(key, 11), (NBLK * NBLK, MATS), stat_level(0.1))


def draw_conv_right(key, part):
    return symmetric_blocks(jax.random.fold_in(key, 12), (NBLK * NBLK, MATS), stat_level(0.1))


def draw_conv_left_root(key, part):
    return symmetric_blocks(jax.random.fold_in(key, 13), (NBLK * NBLK, MATS), (2.5 * stat_level(0.1)) ** (-0.25))


def draw_conv_right_root(key, part):
    return symmetric_blocks(jax.random.fold_in(key, 14), (NBLK * NBLK, MATS), (2.5 * stat_level(0.1)) ** (-0.25))


def draw_proj_weight(key, part):
    noise = jnp.clip(jax.random.normal(jax.random.fold_in(key, 5), (TASKS, 2, NBLK, BLK, BLK), jnp.float32), -6.0, 6.0)
    factor = jnp.array([C ** (-0.5), CA ** (-0.5)], jnp.float32)
    return noise * factor[None, :, None, None, None]


def draw_proj_left(key, part):
    return symmetric_blocks(jax.random.fold_in(key, 21), (TASKS, 2, NBLK), stat_level(0.4))


def draw_proj_right(key, part):
    return symmetric_blocks(jax.random.fold_in(key, 22), (TASKS, 2, NBLK), stat_level(0.4))


def draw_proj_left_root(key, part):
    return symmetric_blocks(jax.random.fold_in(key, 23), (TASKS, 2, NBLK), (2.5 * stat_level(0.05)) ** (-0.25))


def draw_proj_right_root(key, part):
    return symmetric_blocks(jax.random.fold_in(key, 24), (TASKS, 2, NBLK), (2.5 * stat_level(0.05)) ** (-0.25))


def draw_norm_params(key, part):
    gains = 1.0 + jax.random.uniform(jax.random.fold_in(key, 7), (NBN,), jnp.float32, -0.4, 0.4)
    biases = 0.3 * jnp.clip(jax.random.normal(jax.random.fold_in(key, 8), (NBN,), jnp.float32), -6.0, 6.0)
    return jnp.stack([gains, biases])


def draw_norm_moment(key, part):
    pixels = BATCH * HEIGHT * WIDTH
    spread_factor = jnp.exp(jax.random.uniform(jax.random.fold_in(key, 9), (2, NBN), jnp.float32, math.log(0.1), math.log(10.0)))
    return 0.05 / 0.95 * 0.01 * pixels * spread_factor


def set_ends(result, rng, low, high):
    longest = result.shape.index(max(result.shape))
    spots = []
    for shift in (0, 1):
        where = [jax.random.randint(jax.random.fold_in(rng, axis), (), 0, length) for axis, length in enumerate(result.shape)]
        where[longest] = (where[longest] + shift) % result.shape[longest]
        spots.append(tuple(where))
    return result.at[spots[0]].set(low).at[spots[1]].set(high)


def steps_of(key, shape, cuts, smallest, largest):
    loudness = 1.0
    for position, shards_of in cuts:
        draws = jax.random.uniform(jax.random.fold_in(jax.random.fold_in(key, 6), position), (shards_of,), jnp.float32, smallest / len(cuts), largest / len(cuts))
        loudness = loudness * jnp.repeat(jnp.exp(draws), shape[position] // shards_of).reshape((-1,) + (1,) * (len(shape) - 1 - position))
    return loudness


def centred(rng, extent, deviation, limit, cuts=(), held_as=jnp.bfloat16):
    values = deviation * jax.random.normal(rng, extent, jnp.float32)
    if cuts:
        values = values * steps_of(rng, extent, cuts, -0.22, 0.18)
    return jnp.clip(values, -limit, limit).astype(held_as)


def setup_inputs(seed: int = 0) -> dict:
    streams_of = jax.random.split(jax.random.key(seed), 18)
    images = draw_images(jax.random.fold_in(streams_of[17], 71), 0)
    cot_shared = draw_cot_shared(jax.random.fold_in(streams_of[17], 71), 0)
    cot_tasks = draw_cot_tasks(jax.random.fold_in(streams_of[17], 71), 0)
    depth_mask = set_ends((jax.random.randint(streams_of[3], (BATCH, HEIGHT // 2, WIDTH // 2), 0, 4) < 3).astype(jnp.int32), jax.random.fold_in(streams_of[3], 1), 0, 1)
    nash_weights = jnp.clip(jnp.exp(jax.random.uniform(streams_of[4], (TASKS,), jnp.float32, math.log(0.5), math.log(2.0))), 0.5, 2.0)
    conv_weight = centred(streams_of[5], (NBLK * NBLK, MATS, BLK, BLK), (9 * C) ** -0.5, 0.09375, ((0, 16),), jnp.float32)
    conv_left = draw_conv_left(jax.random.fold_in(streams_of[17], 71), 0)
    conv_right = draw_conv_right(jax.random.fold_in(streams_of[17], 71), 0)
    conv_left_root = draw_conv_left_root(jax.random.fold_in(streams_of[17], 71), 0)
    conv_right_root = draw_conv_right_root(jax.random.fold_in(streams_of[17], 71), 0)
    proj_weight = draw_proj_weight(jax.random.fold_in(streams_of[17], 71), 0)
    proj_left = draw_proj_left(jax.random.fold_in(streams_of[17], 71), 0)
    proj_right = draw_proj_right(jax.random.fold_in(streams_of[17], 71), 0)
    proj_left_root = draw_proj_left_root(jax.random.fold_in(streams_of[17], 71), 0)
    proj_right_root = draw_proj_right_root(jax.random.fold_in(streams_of[17], 71), 0)
    norm_params = draw_norm_params(jax.random.fold_in(streams_of[17], 71), 0)
    norm_moment = draw_norm_moment(jax.random.fold_in(streams_of[17], 71), 0)
    return {"images": images, "cot_shared": cot_shared, "cot_tasks": cot_tasks, "depth_mask": depth_mask, "nash_weights": nash_weights, "conv_weight": conv_weight, "conv_left": conv_left, "conv_right": conv_right, "conv_left_root": conv_left_root, "conv_right_root": conv_right_root, "proj_weight": proj_weight, "proj_left": proj_left, "proj_right": proj_right, "proj_left_root": proj_left_root, "proj_right_root": proj_right_root, "norm_params": norm_params, "norm_moment": norm_moment}


eps_norm = 1e-05
conv_rate = 0.08
proj_rate = 0.2
norm_rate = 0.1
stat_decay = 0.9
moment_decay = 0.95
highest = lax.Precision.HIGHEST

@jax.custom_vjp
def low(v):
    return lax.optimization_barrier(v.astype(jnp.bfloat16)).astype(jnp.float32)

@jax.custom_vjp
def low_back(v):
    return v

def low_keep(v):
    return (low(v), None)

def low_pass(kept, grad):
    return (grad,)

def back_keep(v):
    return (v, None)

def back_low(kept, grad):
    return (low(grad),)
low.defvjp(low_keep, low_pass)
low_back.defvjp(back_keep, back_low)

def full_matrices(master):
    block_count = C // BLK
    shaped = master.reshape(block_count, block_count, -1, BLK, BLK)
    return jnp.transpose(shaped, (2, 0, 3, 1, 4)).reshape(-1, C, C)

@jax.checkpoint
def conv_three(field, matrices):
    padded = jnp.pad(field, ((0, 0), (1, 1), (1, 1), (0, 0)))
    height = field.shape[1]
    width = field.shape[2]
    total = jnp.zeros(field.shape[:3] + (matrices.shape[2],), jnp.float32)
    for row_shift in range(3):
        for col_shift in range(3):
            window = padded[:, row_shift:row_shift + height, col_shift:col_shift + width, :]
            total = total + jnp.einsum('bhwc,cd->bhwd', window, matrices[3 * row_shift + col_shift], precision=highest)
    return total

def batch_norm(field, gain, bias):
    average = lax.optimization_barrier(jnp.mean(field, axis=(0, 1, 2)))
    variance = lax.optimization_barrier(jnp.mean(field * field, axis=(0, 1, 2))) - average * average
    return gain * ((field - average) * lax.rsqrt(variance + eps_norm)) + bias

def pool_mean(field):
    count, height, width, depth = field.shape
    return lax.optimization_barrier(jnp.mean(field.reshape(count, height // 2, 2, width // 2, 2, depth), axis=(2, 4)))

def forward(images32, conv_master, proj_master, norm_master, probe):
    matrices = full_matrices(low(conv_master))
    proj_low = low(proj_master)
    gains = norm_master[0]
    biases = norm_master[1]
    off_down = 2 * C
    off_up = 2 * C + TASKS * CA
    first = low_back(conv_three(images32, matrices[0:9]))
    shared_low = low(jax.nn.silu(batch_norm(first, gains[0:C], biases[0:C])))
    second = low_back(conv_three(shared_low, matrices[9:18]))
    shared_field = jax.nn.silu(batch_norm(second, gains[C:2 * C], biases[C:2 * C]))
    pooled = []
    masks = []
    for task_index in range(TASKS):
        down_matrix = proj_low[task_index, 0].reshape(C, CA)
        up_matrix = jnp.transpose(proj_low[task_index, 1], (1, 0, 2)).reshape(CA, C)
        down_pre = low_back(jnp.einsum('bhwc,ca->bhwa', shared_low, down_matrix, precision=highest))
        down_start = off_down + task_index * CA
        hidden = low(jax.nn.silu(batch_norm(down_pre, gains[down_start:down_start + CA], biases[down_start:down_start + CA])))
        mask_pre = low_back(jnp.einsum('bhwa,ac->bhwc', hidden, up_matrix, precision=highest))
        up_start = off_up + task_index * C
        attention = jax.nn.sigmoid(batch_norm(mask_pre, gains[up_start:up_start + C], biases[up_start:up_start + C]))
        attended = low(attention * shared_field + probe[task_index])
        start_mat = 18 + 9 * task_index
        task_map = low_back(conv_three(attended, matrices[start_mat:start_mat + 9]))
        pooled.append(pool_mean(task_map))
        masks.append(attention)
    return ((pool_mean(shared_field), jnp.concatenate(pooled, axis=-1)), jnp.stack(masks))

def shampoo(grad_block, left, right, left_root, right_root, weight, rate):
    left_new = stat_decay * left + (1.0 - stat_decay) * jnp.einsum('...ab,...cb->...ac', grad_block, grad_block, precision=highest)
    right_new = stat_decay * right + (1.0 - stat_decay) * jnp.einsum('...ba,...bc->...ac', grad_block, grad_block, precision=highest)
    partial_step = jnp.einsum('...ab,...bc->...ac', left_root, grad_block, precision=highest)
    step_value = jnp.einsum('...ab,...bc->...ac', partial_step, right_root, precision=highest)
    return (left_new, right_new, weight - rate * step_value)

def reference(images, cot_shared, cot_tasks, depth_mask, nash_weights, conv_weight, conv_left, conv_right, conv_left_root, conv_right_root, proj_weight, proj_left, proj_right, proj_left_root, proj_right_root, norm_params, norm_moment):
    images32 = images.astype(jnp.float32)
    probe = jnp.zeros((TASKS,) + images.shape, jnp.float32)
    outputs, pullback, attention = jax.vjp(forward, images32, conv_weight, proj_weight, norm_params, probe, has_aux=True)
    shared_field, task_field = outputs
    depth_pick = jnp.arange(TASKS) == 1
    task_scale = jnp.where(depth_pick, depth_mask.astype(jnp.float32)[..., None], 1.0) * nash_weights
    half_h = images.shape[1] // 2
    half_w = images.shape[2] // 2
    task_cot = cot_tasks.astype(jnp.float32).reshape(images.shape[0], half_h, half_w, TASKS, C) * task_scale[..., None]
    task_cot = task_cot.reshape(images.shape[0], half_h, half_w, TASKS * C)
    image_grad, conv_grad, proj_grad, norm_grad, probe_grad = pullback((cot_shared.astype(jnp.float32), task_cot))
    branch = attention * probe_grad
    gram = jnp.einsum('tbhwc,sbhwc->ts', branch, branch, precision=highest)
    conv_left_new, conv_right_new, conv_weight_new = shampoo(conv_grad, conv_left, conv_right, conv_left_root, conv_right_root, conv_weight, conv_rate)
    proj_left_new, proj_right_new, proj_weight_new = shampoo(proj_grad, proj_left, proj_right, proj_left_root, proj_right_root, proj_weight, proj_rate)
    moment_new = moment_decay * norm_moment + (1.0 - moment_decay) * norm_grad * norm_grad
    norm_new = norm_params - norm_rate * norm_grad / (jnp.sqrt(moment_new) + 1e-08)
    return (shared_field.astype(jnp.bfloat16), task_field.astype(jnp.bfloat16), image_grad.astype(jnp.bfloat16), gram, conv_grad, conv_left_new, conv_right_new, conv_weight_new, proj_grad, proj_left_new, proj_right_new, proj_weight_new, norm_grad, moment_new, norm_new)
```

```python
import functools

import jax
import jax.numpy as jnp
from jax import lax
from jax.experimental import pallas as pl
from jax.experimental.pallas import tpu as pltpu
from jax.sharding import PartitionSpec as P

C = 512
CA = 128
TASKS = 3
BLK = 128
HB = 64
NB = C // BLK
PROJ_ROWS = TASKS * 2 * NB * BLK // (2 * NB * NB)

eps_norm = 1e-05
conv_rate = 0.08
proj_rate = 0.2
norm_rate = 0.1
stat_decay = 0.9
moment_decay = 0.95

BF = jnp.bfloat16
F32 = jnp.float32
VM = pl.BlockSpec(memory_space=pltpu.VMEM)
SM = pl.BlockSpec(memory_space=pltpu.SMEM)
ANY = pl.BlockSpec(memory_space=pl.ANY)
VMEM_LIMIT = 56 * 1024 * 1024
NT = (((1,), (1,)), ((), ()))
TN = (((0,), (0,)), ((), ()))


def sds(shape, dtype):
    return jax.ShapeDtypeStruct(shape, dtype)


def params(**kw):
    return pltpu.CompilerParams(vmem_limit_bytes=VMEM_LIMIT, **kw)


def cost(flops, nbytes, trans=0):
    return pl.CostEstimate(
        flops=int(flops / 16), bytes_accessed=int(nbytes / 16), transcendentals=int(trans / 16)
    )


def pairs(axis, step):
    return [(i, i ^ step) for i in range(lax.axis_size(axis))]


def swap(value, axis, step):
    return lax.ppermute(value, axis, pairs(axis, step))


def sum_all(value, fillers=(), axes=("wa", "ha", "img")):
    fillers = list(fillers)
    for axis in axes:
        step = 1
        while step < lax.axis_size(axis):
            total = value + swap(value, axis, step)
            if fillers:
                total = after(total, *fillers.pop(0)(value))
            value = total
            step *= 2
    return value


def row_halo(first, last):
    count = lax.axis_size("ha")
    up = [(i, (i + 1) % count) for i in range(count)]
    down = [((i + 1) % count, i) for i in range(count)]
    return lax.ppermute(last, "ha", up), lax.ppermute(first, "ha", down)


def col_halo(left_edge, right_edge):
    count = lax.axis_size("wa")
    if count == 2:
        mine = jnp.where(lax.axis_index("wa") == 0, right_edge, left_edge)
        got = swap(mine, "wa", 1)
        none = jnp.zeros_like(got)
        first = lax.axis_index("wa") == 0
        return jnp.where(first, none, got), jnp.where(first, got, none)
    up = [(i, i + 1) for i in range(count - 1)]
    down = [(i + 1, i) for i in range(count - 1)]
    return lax.ppermute(right_edge, "wa", up), lax.ppermute(left_edge, "wa", down)


def halo(field, batch):
    top, bottom = row_halo(field[0].astype(BF), field[-1].astype(BF))
    rows = jnp.stack([top, bottom])
    return rows, halo_cols(field, rows, batch)


def after(value, *deps):
    return lax.optimization_barrier((value,) + deps)[0]


class Gather:
    def __init__(self, own):
        self.own = own

    def near(self, *deps):
        self.near_got = swap(after(self.own, *deps), "ha", 2)
        return self.near_got

    def join(self, *deps):
        self.line_low = after(jnp.concatenate([self.own, self.near_got], axis=0), *deps)
        return self.line_low

    def far(self, *deps):
        self.line_high = swap(after(self.line_low, *deps), "ha", 1)
        return self.line_high

    def low(self, *deps):
        low = after(self.line_low, *deps)
        self.low_x, self.low_y = swap(low, "img", 1), swap(low, "img", 2)
        return self.low_x, self.low_y

    def high(self, *deps):
        high = after(self.line_high, *deps)
        self.high_x, self.high_y = swap(high, "img", 1), swap(high, "img", 2)
        return self.high_x, self.high_y

    def corner_a(self, *deps):
        self.corner_low = swap(after(self.low_x, *deps), "img", 2)
        return self.corner_low

    def corner_b(self, *deps):
        self.corner_high = swap(after(self.high_y, *deps), "img", 1)
        return self.corner_high

    def pieces(self, *deps):
        mine = (
            self.line_low, self.line_high, self.low_x, self.high_x,
            self.low_y, self.high_y, self.corner_low, self.corner_high,
        )
        return mine + tuple(swap(after(part, *deps), "wa", 1) for part in mine)


def edge_row(field, h):
    return to_rows(field[:, h : h + 1])[0]


def halo_cols(field, rows, batch):
    height, tall, chans = field.shape
    across = tall // (2 * batch)
    split = field.reshape(height, 2, batch, across, chans)
    around = rows.reshape(2, 2, batch, across, chans)

    def edge(parity, place):
        inner = split[:, parity, :, place].astype(BF)
        outer = around[:, parity, :, place]
        return jnp.concatenate([outer[0:1], inner, outer[1:2]], axis=0)

    left, right = col_halo(edge(0, 0), edge(1, across - 1))
    return jnp.stack([left, right], axis=2).reshape(height + 2, 2 * batch, chans).astype(F32)


def gather_proj(own):
    got = swap(own, "wa", 1)
    even = lax.axis_index("wa") % 2 == 0
    value = jnp.stack([jnp.where(even, own, got), jnp.where(even, got, own)])
    for axis in ("ha", "img"):
        place = lax.axis_index(axis)
        for step in (1, 2):
            came = swap(value, axis, step)
            first = (place // step) % 2 == 0
            value = jnp.stack([jnp.where(first, value, came), jnp.where(first, came, value)])
    return value.reshape(TASKS, 2, NB, BLK, BLK).astype(F32)


def add_low(*parts):
    total = parts[0].astype(F32)
    for part in parts[1:]:
        total = total + part.astype(F32)
    return total.astype(BF)


class Scatter:
    def __init__(self, mine, other):
        self.mine, self.other = mine, other

    def wa(self, *deps):
        self.came = swap(after(self.other, *deps), "wa", 1)
        return self.came

    def corner_sum(self, *deps):
        self.corner = add_low(self.mine[3], after(self.came, *deps)[3])
        return self.corner

    def corner_send(self, *deps):
        corner = after(self.corner, *deps)
        self.to_x = swap(corner[0:2], "img", 1)
        self.to_y = swap(corner[2:4], "img", 2)
        return self.to_x, self.to_y

    def high_sum(self, *deps):
        came = after(self.came, *deps)
        self.high = (
            add_low(self.mine[1][2:4], came[1][2:4], self.to_y),
            add_low(self.mine[2][2:4], came[2][2:4]),
        )
        return self.high

    def high_send(self, *deps):
        self.high_x = swap(after(self.high[0], *deps), "img", 1)
        self.high_y = swap(after(self.high[1], *deps), "img", 2)
        return self.high_x, self.high_y

    def low_sum(self, *deps):
        came = after(self.came, *deps)
        self.low = (
            add_low(self.mine[1][0:2], came[1][0:2]),
            add_low(self.mine[2][0:2], came[2][0:2], self.to_x),
        )
        return self.low

    def low_send(self, *deps):
        self.low_x = swap(after(self.low[0], *deps), "img", 1)
        self.low_y = swap(after(self.low[1], *deps), "img", 2)
        return self.low_x, self.low_y

    def far_sum(self, *deps):
        came = after(self.came, *deps)
        self.far = add_low(self.mine[0][2:4], came[0][2:4], self.high_x, self.high_y)
        return self.far

    def far_send(self, *deps):
        self.from_far = swap(after(self.far, *deps), "ha", 1)
        return self.from_far

    def near_sum(self, *deps):
        came = after(self.came, *deps)
        self.near = add_low(
            self.mine[0][1], came[0][1], self.low_x[1], self.low_y[1], self.from_far[1]
        )
        return self.near

    def near_send(self, *deps):
        self.from_near = swap(after(self.near, *deps), "ha", 2)
        return self.from_near

    def finish(self, *deps):
        total = add_low(
            after(self.mine[0][0], *deps), self.came[0][0], self.low_x[0], self.low_y[0], self.from_far[0], self.from_near
        )
        step = 2
        while step < lax.axis_size("wa"):
            total = add_low(total, swap(total, "wa", step))
            step *= 2
        return total, swap(total, "wa", 1)


def coef(sums, gb, count_all):
    mean = sums[0:1] / count_all
    var = sums[1:2] / count_all - mean * mean
    rs = lax.rsqrt(var + eps_norm)
    sc = gb[0:1] * rs
    return mean, rs, sc, gb[1:2] - mean * sc


def sigm(v):
    return 1.0 / (1.0 + jnp.exp(-v))


def side_mask(idx, rows, lanes, count):
    side = lax.broadcasted_iota(jnp.int32, (rows, lanes), 0) % 2
    return jnp.where(side == 0, idx[5], idx[6]).astype(F32)


def col_block(cols, r, side, batch, across):
    lanes = cols.shape[-1]
    parts = [
        jnp.broadcast_to(cols[r, pl.ds(2 * b + side, 1), :], (across, lanes)) for b in range(batch)
    ]
    return jnp.concatenate(parts, axis=0)


def shifted(even, odd, hl, hr, batch, across):
    lanes = even.shape[-1]
    shape = (batch, across, lanes)
    j = lax.broadcasted_iota(jnp.int32, shape, 1)
    lo = jnp.where(j == 0, hl.reshape(shape), pltpu.roll(odd.reshape(shape), 1, 1))
    hi = jnp.where(j == across - 1, hr.reshape(shape), pltpu.roll(even.reshape(shape), across - 1, 1))
    return lo.reshape(even.shape), hi.reshape(even.shape)


def put_row(x3, r, row, cols, batch, across):
    q = batch * across
    even, odd = row[0:q], row[q : 2 * q]
    hl = col_block(cols, r, 0, batch, across)
    hr = col_block(cols, r, 1, batch, across)
    lo, hi = shifted(even, odd, hl, hr, batch, across)
    x3[0, r] = jnp.concatenate([lo, even], axis=0).astype(BF)
    x3[1, r] = row.astype(BF)
    x3[2, r] = jnp.concatenate([odd, hi], axis=0).astype(BF)


def flip(s):
    return s // 2 + 2 * (s % 2)


def weight_copies_rel(idx, pieces, first, wv, sems):
    copies = []
    count = len(pieces) // 2
    for half in range(2):
        parts = pieces[half * count : (half + 1) * count]
        h = lax.bitwise_xor(idx[2], half)
        for e in range(4):
            i = lax.bitwise_xor(idx[0], e)
            row0 = pl.multiple_of(i * BLK + h * HB, HB)
            for s in range(4):
                j = lax.bitwise_xor(idx[1], flip(s))
                col0 = pl.multiple_of(j * BLK, BLK)
                copies.append(
                    pltpu.make_async_copy(
                        parts[2 * e + s // 2].at[s % 2, pl.ds(first, 9)],
                        wv.at[:, pl.ds(row0, HB), pl.ds(col0, BLK)],
                        sems.at[len(copies)],
                    )
                )
    return copies


def weight_copies_task(idx, pieces, first, wv, sems):
    copies = []
    for half in range(2):
        h = lax.bitwise_xor(idx[2], half)
        for i in range(NB):
            row0 = pl.multiple_of(i * BLK + h * HB, HB)
            for j in range(NB):
                copies.append(
                    pltpu.make_async_copy(
                        pieces[half].at[i * NB + j, pl.ds(first, 9)],
                        wv.at[:, pl.ds(row0, HB), j * BLK : (j + 1) * BLK],
                        sems.at[len(copies)],
                    )
                )
    return copies


def shift_kernel(batch, idx, x_ref, rows_ref, cols_ref, x3_ref, work):
    height, tall = x_ref.shape[0], x_ref.shape[1]
    across = tall // (2 * batch)
    top, bottom = idx[3].astype(F32), idx[4].astype(F32)
    work[...] = cols_ref[...]
    work[0] = work[0] * top
    work[height + 1] = work[height + 1] * bottom
    cols_ref = work
    put_row(x3_ref, 0, rows_ref[0].astype(F32) * top, cols_ref, batch, across)
    put_row(x3_ref, height + 1, rows_ref[1].astype(F32) * bottom, cols_ref, batch, across)

    @pl.loop(0, height)
    def _(h):
        put_row(x3_ref, h + 1, x_ref[h].astype(F32), cols_ref, batch, across)


def shift_copies(idx, field, rows, cols, batch):
    height, tall, chans = field.shape
    lanes = BLK
    return pl.pallas_call(
        functools.partial(shift_kernel, batch),
        grid=(chans // lanes,),
        in_specs=[
            SM,
            pl.BlockSpec((height, tall, lanes), lambda c: (0, 0, c)),
            pl.BlockSpec((2, tall, lanes), lambda c: (0, 0, c)),
            pl.BlockSpec((height + 2, 2 * batch, lanes), lambda c: (0, 0, c)),
        ],
        out_specs=pl.BlockSpec((3, height + 2, tall, lanes), lambda c: (0, 0, 0, c)),
        out_shape=sds((3, height + 2, tall, chans), BF),
        scratch_shapes=[pltpu.VMEM((height + 2, 2 * batch, lanes), F32)],
        compiler_params=params(),
        cost_estimate=cost(0, 8e6),
        name="shift_copies",
    )(idx, field, rows, cols)


def conv_kernel(n_pieces, transposed, want_sums, idx_ref, x_ref, *refs):
    pieces = refs[:n_pieces]
    o_ref = refs[n_pieces]
    s_ref = refs[n_pieces + 1] if want_sums else None
    wv, sems = refs[-2:]
    copies = weight_copies_rel(idx_ref, pieces, 0, wv, sems)
    for copy in copies:
        copy.start()
    for copy in copies:
        copy.wait()
    height, tall = x_ref.shape[1] - 2, x_ref.shape[2]
    step = height // 2
    rows = step * tall
    if want_sums:
        s_ref[...] = jnp.zeros(s_ref.shape, F32)

    @pl.loop(0, 2)
    def _(part):
        acc = None
        for dy in range(3):
            for dx in range(3):
                if transposed:
                    view = x_ref[2 - dx, pl.ds(part * step + 2 - dy, step)]
                    dims = NT
                else:
                    view = x_ref[dx, pl.ds(part * step + dy, step)]
                    dims = (((1,), (0,)), ((), ()))
                piece = lax.dot_general(
                    view.reshape(rows, C), wv[3 * dy + dx], dims, preferred_element_type=F32
                )
                acc = piece if acc is None else acc + piece
        o_ref[pl.ds(part * step, step)] = acc.reshape(step, tall, C).astype(o_ref.dtype)
        if want_sums:
            s_ref[0:1] += jnp.sum(acc, axis=0, keepdims=True)
            s_ref[1:2] += jnp.sum(acc * acc, axis=0, keepdims=True)


def conv(idx, x3, pieces, transposed, want_sums, dtype, name):
    height, tall = x3.shape[1] - 2, x3.shape[2]
    out_shape = [sds((height, tall, C), dtype)]
    if want_sums:
        out_shape.append(sds((2, C), F32))
    out = pl.pallas_call(
        functools.partial(conv_kernel, len(pieces), transposed, want_sums),
        in_specs=[SM, VM] + [ANY] * len(pieces),
        out_specs=[VM] * len(out_shape),
        out_shape=out_shape,
        scratch_shapes=[pltpu.VMEM((9, C, C), BF), pltpu.SemaphoreType.DMA((32,))],
        compiler_params=params(),
        cost_estimate=cost(2 * 9 * C * C * height * tall, 10e6),
        name=name,
    )(idx, x3, *pieces)
    return out if want_sums else out[0]


def mid_kernel(batch, count_all, idx, st, gb, z_ref, rows_ref, cols_ref, d_ref, u3, hp, hc, hs, uc):
    height, tall, lanes = z_ref.shape
    across = tall // (2 * batch)
    step = pl.program_id(0)
    mean, rs, sc, sh = coef(st[...], gb[...], count_all)

    def act(v):
        y = v * sc + sh
        return y * sigm(y)

    mask = side_mask(idx, 2 * batch, lanes, 0)
    flat = act(cols_ref[...].reshape(-1, lanes)).reshape(height + 2, 2 * batch, lanes)
    uc[...] = flat * mask[None]
    uc[0] = uc[0] * idx[3].astype(F32)
    uc[height + 1] = uc[height + 1] * idx[4].astype(F32)
    put_row(u3, 0, act(rows_ref[0].astype(F32)) * idx[3].astype(F32), uc, batch, across)
    put_row(u3, height + 1, act(rows_ref[1].astype(F32)) * idx[4].astype(F32), uc, batch, across)

    @pl.loop(0, height)
    def _(h):
        put_row(u3, h + 1, act(z_ref[h]), uc, batch, across)

    @pl.when(step == 0)
    def _():
        hp[...] = jnp.zeros(hp.shape, F32)
        hc[...] = jnp.zeros(hc.shape, F32)

    hc[...] += jnp.dot(
        uc[...].reshape(-1, lanes).astype(BF), d_ref[...], preferred_element_type=F32
    )
    part = (height + 2) // 2
    size = part * tall

    @pl.loop(0, 2)
    def _(k):
        hp[pl.ds(pl.multiple_of(k * size, size), size)] += jnp.dot(
            u3[1, pl.ds(k * part, part)].reshape(size, lanes),
            d_ref[...],
            preferred_element_type=F32,
        )

    @pl.when(step == pl.num_programs(0) - 1)
    def _():
        inner = hp[tall : (height + 1) * tall]
        hs[0:1] = jnp.sum(inner, axis=0, keepdims=True)
        hs[1:2] = jnp.sum(inner * inner, axis=0, keepdims=True)


def mid(idx, st, gb, z, rows, cols, down, batch, count_all):
    height, tall, chans = z.shape
    lanes = BLK
    r = height + 2
    wide = TASKS * CA
    return pl.pallas_call(
        functools.partial(mid_kernel, batch, count_all),
        grid=(chans // lanes,),
        in_specs=[
            SM,
            pl.BlockSpec((2, lanes), lambda c: (0, c)),
            pl.BlockSpec((2, lanes), lambda c: (0, c)),
            pl.BlockSpec((height, tall, lanes), lambda c: (0, 0, c)),
            pl.BlockSpec((2, tall, lanes), lambda c: (0, 0, c)),
            pl.BlockSpec((r, 2 * batch, lanes), lambda c: (0, 0, c)),
            pl.BlockSpec((lanes, wide), lambda c: (c, 0)),
        ],
        out_specs=[
            pl.BlockSpec((3, r, tall, lanes), lambda c: (0, 0, 0, c)),
            pl.BlockSpec((r * tall, wide), lambda c: (0, 0)),
            pl.BlockSpec((r * 2 * batch, wide), lambda c: (0, 0)),
            pl.BlockSpec((2, wide), lambda c: (0, 0)),
        ],
        out_shape=[
            sds((3, r, tall, chans), BF),
            sds((r * tall, wide), F32),
            sds((r * 2 * batch, wide), F32),
            sds((2, wide), F32),
        ],
        scratch_shapes=[pltpu.VMEM((r, 2 * batch, lanes), F32)],
        compiler_params=params(),
        cost_estimate=cost(2 * r * tall * chans * wide, 10e6, 2e6),
        name="mid",
    )(idx, st, gb, z, rows, cols, down)


def hidden_kernel(tall, count_all, st, gb, hp, hc, up, h_ref, hcb, ms):
    mean, rs, sc, sh = coef(st[...], gb[...], count_all)
    yc = hc[...] * sc + sh
    hcb[...] = (yc * sigm(yc)).astype(BF)
    n_rows = hp.shape[0] // tall
    ms[...] = jnp.zeros(ms.shape, F32)

    def row(r):
        at = pl.ds(pl.multiple_of(r * tall, tall), tall)
        y = hp[at] * sc + sh
        h_ref[at] = (y * sigm(y)).astype(BF)

    @pl.loop(0, n_rows)
    def _(r):
        row(r)

    chunk = 4 * tall
    for t in range(TASKS):

        @pl.loop(0, (n_rows - 2) // 4)
        def _(k):
            at = pl.ds(pl.multiple_of(tall + k * chunk, tall), chunk)
            pre = jnp.dot(h_ref[at, t * CA : (t + 1) * CA], up[t], preferred_element_type=F32)
            ms[2 * t : 2 * t + 1] += jnp.sum(pre, axis=0, keepdims=True)
            ms[2 * t + 1 : 2 * t + 2] += jnp.sum(pre * pre, axis=0, keepdims=True)


def hidden(st, gb, hp, hc, up, tall, count_all):
    return pl.pallas_call(
        functools.partial(hidden_kernel, tall, count_all),
        in_specs=[VM] * 5,
        out_specs=[VM] * 3,
        out_shape=[sds(hp.shape, BF), sds(hc.shape, BF), sds((2 * TASKS, C), F32)],
        compiler_params=params(),
        cost_estimate=cost(2 * hp.shape[0] * CA * C * TASKS, 5e6, 2e6),
        name="hidden",
    )(st, gb, hp, hc, up)


def da_kernel(task, n_pieces, n_prev, idx, go, *refs):
    pieces = refs[:n_pieces]
    da, wv, ws, sems = refs[n_pieces + n_prev :]
    q = go.shape[3]
    half_h = go.shape[2] - 2
    copies = weight_copies_task(idx, pieces, task * 9, wv, sems)
    for copy in copies:
        copy.start()
    for copy in copies:
        copy.wait()

    def add(a, b):
        return (a.astype(F32) + b.astype(F32)).astype(BF)

    for a in range(2):
        for k in range(2):
            taps = []
            for dx in range(3):
                if k == 0:
                    taps.append(add(wv[3 * a + dx], wv[3 * (a + 1) + dx]))
                else:
                    taps.append(wv[3 * (2 if a == 0 else 0) + dx])
            ws[a, k, 0, 0] = add(taps[0], taps[1])
            ws[a, k, 0, 1] = taps[2]
            ws[a, k, 1, 0] = add(taps[1], taps[2])
            ws[a, k, 1, 1] = taps[0]
    for a in range(2):
        for bb in range(2):
            acc = None
            for k in range(2):
                for m in range(2):
                    ro = 0 if k == 0 else (-1 if a == 0 else 1)
                    co = 0 if m == 0 else (-1 if bb == 0 else 1)
                    view = go[0, co + 1, 1 + ro : 1 + ro + half_h].reshape(half_h * q, C)
                    piece = lax.dot_general(
                        view, ws[a, k, bb, m], NT, preferred_element_type=F32
                    )
                    acc = piece if acc is None else acc + piece
            da[0, :, a, bb] = acc.reshape(half_h, q, C).astype(BF)


def task_back(idx, go, pieces, task, prev):
    half_h, q = go.shape[2] - 2, go.shape[3]
    return pl.pallas_call(
        functools.partial(da_kernel, task, len(pieces), len(prev)),
        grid=(1,),
        in_specs=[SM, pl.BlockSpec((1,) + go.shape[1:], lambda k: (task, 0, 0, 0, 0))]
        + [ANY] * (len(pieces) + len(prev)),
        out_specs=pl.BlockSpec((1, half_h, 2, 2, q, C), lambda k: (task, 0, 0, 0, 0, 0)),
        out_shape=sds((TASKS, half_h, 2, 2, q, C), BF),
        scratch_shapes=[
            pltpu.VMEM((9, C, C), BF),
            pltpu.VMEM((2, 2, 2, 2, C, C), BF),
            pltpu.SemaphoreType.DMA((32,)),
        ],
        input_output_aliases={2 + len(pieces) + k: k for k in range(len(prev))},
        compiler_params=params(),
        cost_estimate=cost(2 * 16 * C * C * half_h * q, 8e6),
        name="task_back",
    )(idx, go, *pieces, *prev)


def attend_kernel(
    batch, count_all, idx, st, gb, mst, mgb, z_ref, rows_ref, cols_ref, h_ref, hc_ref, up, da, cot,
    se, so, dym, dy2, pooled, sums,
    ac, pre, prev,
):
    height, tall, lanes = z_ref.shape
    across = tall // (2 * batch)
    q = tall // 2
    mean, rs, sc, sh = coef(st[...], gb[...], count_all)
    mcoef = [
        coef(mst[2 * t : 2 * t + 2], mgb[2 * t : 2 * t + 2], count_all) for t in range(TASKS)
    ]
    mask = side_mask(idx, 2 * batch, lanes, 0)
    top, bottom = idx[3].astype(F32), idx[4].astype(F32)

    y = cols_ref[...].reshape(-1, lanes) * sc + sh
    pc = (y * sigm(y)).reshape(height + 2, 2 * batch, lanes) * mask[None]
    for t in range(TASKS):
        mc = jnp.dot(hc_ref[:, t * CA : (t + 1) * CA], up[t], preferred_element_type=F32)
        _, _, msc, msh = mcoef[t]
        mc = sigm(mc * msc + msh).reshape(height + 2, 2 * batch, lanes)
        ac[t] = (mc * pc).astype(BF).astype(F32)
        ac[t, 0] = ac[t, 0] * top
        ac[t, height + 1] = ac[t, height + 1] * bottom
        pre[t] = jnp.dot(
            h_ref[:, t * CA : (t + 1) * CA], up[t], preferred_element_type=F32
        ).reshape(height + 2, tall, lanes)
    sums[...] = jnp.zeros(sums.shape, F32)

    def col_sums(t, r, a):
        even, odd = a[0:q], a[q : 2 * q]
        lo, hi = shifted(
            even,
            odd,
            col_block(ac.at[t], r, 0, batch, across),
            col_block(ac.at[t], r, 1, batch, across),
            batch,
            across,
        )
        return lo + even, even + odd, odd + hi

    def halo_row(r, place, scale):
        yy = rows_ref[place].astype(F32) * sc + sh
        p = yy * sigm(yy) * scale
        out = []
        for t in range(TASKS):
            _, _, msc, msh = mcoef[t]
            a = (sigm(pre[t, r] * msc + msh) * p).astype(BF).astype(F32)
            out.append(col_sums(t, r, a))
        return out

    first = halo_row(0, 0, top)
    for t in range(TASKS):
        for dx in range(3):
            prev[t, dx] = first[t][dx]

    def inner(i, par):
        h = 2 * i + par
        r = h + 1
        z = z_ref[h]
        yy = z * sc + sh
        s = sigm(yy)
        p = yy * s
        slope = s * (1.0 + yy * (1.0 - s))
        shared = cot[i]
        shared = jnp.concatenate([shared, shared], axis=0)
        cs = []
        branches = []
        for t in range(TASKS):
            mmean, mrs, msc, msh = mcoef[t]
            mp = pre[t, r]
            m = sigm(mp * msc + msh)
            a = (m * p).astype(BF).astype(F32)
            cs.append(col_sums(t, r, a))
            d = da[t, h].astype(F32)
            br = m * d
            branches.append(br)
            shared = shared + br
            dm = br * p * (1.0 - m)
            dym[t, h] = dm.astype(BF)
            sums[2 * t : 2 * t + 1] += jnp.sum(dm, axis=0, keepdims=True)
            sums[2 * t + 1 : 2 * t + 2] += jnp.sum(dm * (mp - mmean), axis=0, keepdims=True)
        g2 = shared * slope
        dy2[h] = g2
        sums[6:7] += jnp.sum(g2, axis=0, keepdims=True)
        sums[7:8] += jnp.sum(g2 * (z - mean), axis=0, keepdims=True)
        k = 8
        for t in range(TASKS):
            for s2 in range(t, TASKS):
                sums[k : k + 1] += jnp.sum(branches[t] * branches[s2], axis=0, keepdims=True)
                k += 1
        return cs, p[0:q] + p[q : 2 * q]

    @pl.loop(0, height // 2)
    def _(i):
        cs, pool_a = inner(i, 0)
        for t in range(TASKS):
            for dx in range(3):
                se[t, dx, i] = (prev[t, dx] + cs[t][dx]).astype(BF)
                prev[t, dx] = cs[t][dx]
        cs, pool_b = inner(i, 1)
        for t in range(TASKS):
            for dx in range(3):
                so[t, dx, i] = (prev[t, dx] + cs[t][dx]).astype(BF)
                prev[t, dx] = cs[t][dx]
        pooled[i] = (pool_a + pool_b) * 0.25

    last = halo_row(height + 1, 1, bottom)
    for t in range(TASKS):
        for dx in range(3):
            se[t, dx, height // 2] = (prev[t, dx] + last[t][dx]).astype(BF)
        sums[2 * t + 1 : 2 * t + 2] = sums[2 * t + 1 : 2 * t + 2] * mcoef[t][1]
    sums[7:8] = sums[7:8] * rs


def attend(idx, st, gb, mst, mgb, z, rows, cols, h, hc, up, da, cot, batch, count_all):
    height, tall, chans = z.shape
    lanes = BLK
    r, q, half = height + 2, tall // 2, height // 2

    def two(n):
        return pl.BlockSpec((n, lanes), lambda c: (0, c))

    def three(a, b):
        return pl.BlockSpec((a, b, lanes), lambda c: (0, 0, c))

    def four(a, b, d):
        return pl.BlockSpec((a, b, d, lanes), lambda c: (0, 0, 0, c))

    def five(a, b, d, e):
        return pl.BlockSpec((a, b, d, e, lanes), lambda c: (0, 0, 0, 0, c))

    def whole(a):
        return pl.BlockSpec(a.shape, lambda c: (0,) * a.ndim)

    return pl.pallas_call(
        functools.partial(attend_kernel, batch, count_all),
        grid=(chans // lanes,),
        in_specs=[
            SM,
            two(2),
            two(2),
            two(2 * TASKS),
            two(2 * TASKS),
            three(height, tall),
            three(2, tall),
            three(r, 2 * batch),
            whole(h),
            whole(hc),
            three(TASKS, CA),
            four(TASKS, height, tall),
            three(half, q),
        ],
        out_specs=[
            five(TASKS, 3, half + 1, q),
            five(TASKS, 3, half, q),
            four(TASKS, height, tall),
            three(height, tall),
            three(half, q),
            two(14),
        ],
        out_shape=[
            sds((TASKS, 3, half + 1, q, chans), BF),
            sds((TASKS, 3, half, q, chans), BF),
            sds((TASKS, height, tall, chans), BF),
            sds((height, tall, chans), F32),
            sds((half, q, chans), F32),
            sds((14, chans), F32),
        ],
        scratch_shapes=[
            pltpu.VMEM((TASKS, r, 2 * batch, lanes), F32),
            pltpu.VMEM((TASKS, r, tall, lanes), F32),
            pltpu.VMEM((TASKS, 3, q, lanes), F32),
        ],
        compiler_params=params(),
        cost_estimate=cost(2 * r * tall * CA * chans * TASKS, 25e6, 6e6),
        name="attend",
    )(idx, st, gb, mst, mgb, z, rows, cols, h, hc, up, da, cot)


def mask_back_kernel(
    tall, count_all, mst, mgb, msum, hst, hgb, dym, h_ref, hp, up, du, dh, hs, acc
):
    step = pl.program_id(0)
    n_rows = h_ref.shape[0]

    @pl.when(step == 0)
    def _():
        acc[...] = jnp.zeros(acc.shape, F32)

    inner = pl.ds(tall, n_rows - 2 * tall)
    for t in range(TASKS):
        mean, rs, sc, _ = coef(mst[2 * t : 2 * t + 2], mgb[2 * t : 2 * t + 2], count_all)
        tot = msum[2 * t : 2 * t + 1] / count_all
        cross = msum[2 * t + 1 : 2 * t + 2] * rs / count_all
        ht = h_ref[inner, t * CA : (t + 1) * CA]
        pre = jnp.dot(ht, up[t], preferred_element_type=F32)
        dm = dym[t].reshape(pre.shape).astype(F32)
        dz = (sc * (dm - tot - (pre - mean) * cross)).astype(BF)
        du[t] = lax.dot_general(ht, dz, TN, preferred_element_type=F32)
        acc[:, t * CA : (t + 1) * CA] += lax.dot_general(dz, up[t], NT, preferred_element_type=F32)

    @pl.when(step == pl.num_programs(0) - 1)
    def _():
        mean, rs, sc, sh = coef(hst[...], hgb[...], count_all)
        hs[...] = jnp.zeros(hs.shape, F32)
        chunk = 2 * tall

        @pl.loop(0, (n_rows - 2 * tall) // chunk)
        def _(k):
            at = pl.ds(pl.multiple_of(k * chunk, chunk), chunk)
            v = hp[pl.ds(pl.multiple_of(tall + k * chunk, tall), chunk)]
            y = v * sc + sh
            s = sigm(y)
            g = acc[at] * (s * (1.0 + y * (1.0 - s)))
            dh[at] = g
            hs[0:1] += jnp.sum(g, axis=0, keepdims=True)
            hs[1:2] += jnp.sum(g * (v - mean) * rs, axis=0, keepdims=True)


def mask_back(mst, mgb, msum, hst, hgb, dym, h, hp, up, tall, count_all):
    lanes = BLK
    wide = TASKS * CA
    pixels = h.shape[0] - 2 * tall

    def two(n):
        return pl.BlockSpec((n, lanes), lambda c: (0, c))

    def whole(a):
        return pl.BlockSpec(a.shape, lambda c: (0,) * a.ndim)

    return pl.pallas_call(
        functools.partial(mask_back_kernel, tall, count_all),
        grid=(C // lanes,),
        in_specs=[
            two(2 * TASKS),
            two(2 * TASKS),
            two(2 * TASKS),
            whole(hst),
            whole(hgb),
            pl.BlockSpec(dym.shape[:3] + (lanes,), lambda c: (0, 0, 0, c)),
            whole(h),
            whole(hp),
            pl.BlockSpec((TASKS, CA, lanes), lambda c: (0, 0, c)),
        ],
        out_specs=[
            pl.BlockSpec((TASKS, CA, lanes), lambda c: (0, 0, c)),
            pl.BlockSpec((pixels, wide), lambda c: (0, 0)),
            pl.BlockSpec((2, wide), lambda c: (0, 0)),
        ],
        out_shape=[sds((TASKS, CA, C), F32), sds((pixels, wide), F32), sds((2, wide), F32)],
        scratch_shapes=[pltpu.VMEM((pixels, wide), F32)],
        compiler_params=params(),
        cost_estimate=cost(6 * pixels * C * wide, 8e6, 1e6),
        name="mask_back",
    )(mst, mgb, msum, hst, hgb, dym, h, hp, up)


def norm_back_kernel(
    batch, count_all, idx, st, gb, gs, dy, drows, dcols, z, zrows, zcols, x3, work
):
    height, tall, lanes = z.shape
    across = tall // (2 * batch)
    mean, rs, sc, _ = coef(st[...], gb[...], count_all)
    tot = gs[0:1] / count_all
    cross = gs[1:2] * rs / count_all

    def back(d, v):
        return sc * (d - tot - (v - mean) * cross)

    mask = side_mask(idx, 2 * batch, lanes, 0)
    flat = back(dcols[...].reshape(-1, lanes), zcols[...].reshape(-1, lanes))
    work[...] = flat.reshape(height + 2, 2 * batch, lanes) * mask[None]
    top, bottom = idx[3].astype(F32), idx[4].astype(F32)
    work[0] = work[0] * top
    work[height + 1] = work[height + 1] * bottom
    put_row(x3, 0, back(drows[0].astype(F32), zrows[0].astype(F32)) * top, work, batch, across)
    put_row(
        x3, height + 1, back(drows[1].astype(F32), zrows[1].astype(F32)) * bottom, work, batch, across
    )

    @pl.loop(0, height)
    def _(h):
        put_row(x3, h + 1, back(dy[h], z[h]), work, batch, across)


def norm_back(idx, st, gb, gs, dy, dhalo, z, zhalo, batch, count_all, name):
    height, tall, chans = z.shape
    lanes = BLK
    r = height + 2

    def two(n):
        return pl.BlockSpec((n, lanes), lambda c: (0, c))

    def three(a, b):
        return pl.BlockSpec((a, b, lanes), lambda c: (0, 0, c))

    field = [three(height, tall), three(2, tall), three(r, 2 * batch)]
    return pl.pallas_call(
        functools.partial(norm_back_kernel, batch, count_all),
        grid=(chans // lanes,),
        in_specs=[SM, two(2), two(2), two(2)] + field + field,
        out_specs=pl.BlockSpec((3, r, tall, lanes), lambda c: (0, 0, 0, c)),
        out_shape=sds((3, r, tall, chans), BF),
        scratch_shapes=[pltpu.VMEM((r, 2 * batch, lanes), F32)],
        compiler_params=params(),
        cost_estimate=cost(0, 10e6),
        name=name,
    )(idx, st, gb, gs, dy, *dhalo, z, *zhalo)


def first_back_kernel(
    count_all, hst, hgb, hsum, st, gb, dh, hp, u3, part, z, down, dd, dy, gs, low
):
    height, tall, lanes = z.shape

    @pl.when(pl.program_id(0) == 0)
    def _():
        mean, rs, sc, _ = coef(hst[...], hgb[...], count_all)
        tot = hsum[0:1] / count_all
        cross = hsum[1:2] * rs / count_all
        chunk = 2 * tall

        @pl.loop(0, height // 2)
        def _(k):
            at = pl.ds(pl.multiple_of(k * chunk, chunk), chunk)
            v = hp[pl.ds(pl.multiple_of(tall + k * chunk, tall), chunk)]
            low[at] = (sc * (dh[at] - tot - (v - mean) * cross)).astype(BF)

    u = u3[0, 1 : height + 1].reshape(height * tall, lanes)
    dd[...] = lax.dot_general(u, low[...], TN, preferred_element_type=F32)
    mean, rs, sc, sh = coef(st[...], gb[...], count_all)
    gs[...] = jnp.zeros(gs.shape, F32)
    rows = 4

    @pl.loop(0, height // rows)
    def _(k):
        at = pl.ds(pl.multiple_of(k * rows * tall, rows * tall), rows * tall)
        back = lax.dot_general(low[at], down[...], NT, preferred_element_type=F32)
        v = z[pl.ds(k * rows, rows)].reshape(rows * tall, lanes)
        y = v * sc + sh
        s = sigm(y)
        total = part[pl.ds(k * rows, rows)].reshape(rows * tall, lanes) + back
        g = total * (s * (1.0 + y * (1.0 - s)))
        dy[pl.ds(k * rows, rows)] = g.reshape(rows, tall, lanes)
        gs[0:1] += jnp.sum(g, axis=0, keepdims=True)
        gs[1:2] += jnp.sum(g * (v - mean) * rs, axis=0, keepdims=True)


def first_back(hst, hgb, hsum, st, gb, dh, hp, u3, part, z, down, count_all):
    height, tall, chans = z.shape
    lanes = BLK
    wide = TASKS * CA

    def two(n):
        return pl.BlockSpec((n, lanes), lambda c: (0, c))

    def whole(a):
        return pl.BlockSpec(a.shape, lambda c: (0,) * a.ndim)

    field = pl.BlockSpec((height, tall, lanes), lambda c: (0, 0, c))
    return pl.pallas_call(
        functools.partial(first_back_kernel, count_all),
        grid=(chans // lanes,),
        in_specs=[
            whole(hst),
            whole(hgb),
            whole(hsum),
            two(2),
            two(2),
            whole(dh),
            whole(hp),
            pl.BlockSpec((1, height + 2, tall, lanes), lambda c: (1, 0, 0, c)),
            field,
            field,
            pl.BlockSpec((lanes, wide), lambda c: (c, 0)),
        ],
        out_specs=[pl.BlockSpec((lanes, wide), lambda c: (c, 0)), field, two(2)],
        out_shape=[sds((chans, wide), F32), sds((height, tall, chans), F32), sds((2, chans), F32)],
        scratch_shapes=[pltpu.VMEM((height * tall, wide), BF)],
        compiler_params=params(),
        cost_estimate=cost(4 * height * tall * chans * wide, 12e6, 1e6),
        name="first_back",
    )(hst, hgb, hsum, st, gb, dh, hp, u3, part, z, down)


def flip_place(place, j):
    s = lax.bitwise_xor(place, j)
    return lax.shift_right_logical(s, 1) + 2 * lax.bitwise_and(s, 1)


def put_blocks(idx, grad, mine, other, m):
    low = grad.astype(BF)
    even = idx[2] == 0
    for i in range(NB):
        e = lax.bitwise_xor(idx[0], i)
        for j in range(NB):
            s = flip_place(idx[1], j)
            block = low[i * BLK : (i + 1) * BLK, j * BLK : (j + 1) * BLK]
            a, b = block[0:HB], block[HB:BLK]
            at = pl.ds(pl.multiple_of(m * HB, HB), HB)
            mine[e, s, at] = jnp.where(even, a, b)
            other[e, s, at] = jnp.where(even, b, a)


def put_in_order(idx, grad, mine, other, m):
    low = grad.astype(BF)
    even = idx[2] == 0
    at = slice(m * HB, (m + 1) * HB)
    for i in range(NB):
        for j in range(NB):
            block = low[i * BLK : (i + 1) * BLK, j * BLK : (j + 1) * BLK]
            a, b = block[0:HB], block[HB:BLK]
            mine[i * NB + j, at] = jnp.where(even, a, b)
            other[i * NB + j, at] = jnp.where(even, b, a)


def wgrad_kernel(n_extra, idx, x3, g3, *refs):
    mine, other = refs[n_extra:]
    height, tall = x3.shape[1] - 2, x3.shape[2]
    g = g3[0, 1 : height + 1].reshape(height * tall, C)

    @pl.loop(0, 3)
    def _(dy):
        for dx in range(3):
            view = x3[dx, pl.ds(dy, height)].reshape(height * tall, C)
            grad = lax.dot_general(view, g, TN, preferred_element_type=F32)
            put_blocks(idx, grad, mine, other, 3 * dy + dx)

    if n_extra:
        ddown, dup = refs[:2]
        even = idx[2] == 0
        unit = BLK // 4

        def chunk(c):
            block, r = divmod(c, 4)
            t, block = divmod(block, 2 * NB)
            kind, n = divmod(block, NB)
            if kind == 0:
                return ddown[n * BLK + r * unit : n * BLK + (r + 1) * unit, t * CA : (t + 1) * CA]
            return dup[t, r * unit : (r + 1) * unit, n * BLK : (n + 1) * BLK]

        at = pl.ds(9 * HB, PROJ_ROWS)
        for n in range(NB * NB):
            e = lax.bitwise_xor(idx[0], n // NB)
            s = flip_place(idx[1], n % NB)
            a, b = [
                jnp.concatenate([chunk(6 * n + 3 * k + c) for c in range(3)], axis=0).astype(BF)
                for k in range(2)
            ]
            mine[e, s, at] = jnp.where(even, a, b)
            other[e, s, at] = jnp.where(even, b, a)


def wgrad(idx, x3, g3, name, extra=()):
    r, tall = x3.shape[1], x3.shape[2]
    rows = 9 * HB + (PROJ_ROWS if extra else 0)
    return pl.pallas_call(
        functools.partial(wgrad_kernel, len(extra)),
        grid=(1,),
        in_specs=[
            SM,
            pl.BlockSpec(x3.shape, lambda c: (0, 0, 0, 0)),
            pl.BlockSpec((1,) + g3.shape[1:], lambda c: (1, 0, 0, 0)),
        ]
        + [VM] * len(extra),
        out_specs=[pl.BlockSpec((4, 4, rows, BLK), lambda c: (0, 0, 0, 0))] * 2,
        out_shape=[sds((4, 4, rows, BLK), BF)] * 2,
        compiler_params=params(),
        cost_estimate=cost(2 * 9 * C * C * (r - 2) * tall, 10e6),
        name=name,
    )(idx, x3, g3, *extra)


def task_wgrad_kernel(n_prev, idx, se, so, go, *refs):
    mine, other = refs[n_prev:]
    half, q = so.shape[2], so.shape[3]
    g = go[0, 0, 1 : half + 1].reshape(half * q, C)
    for dy in range(3):
        for dx in range(3):
            if dy == 1:
                view = so[0, dx]
            else:
                view = se[0, dx, dy // 2 : dy // 2 + half]
            grad = lax.dot_general(view.reshape(half * q, C), g, TN, preferred_element_type=F32)
            put_in_order(idx, grad, mine, other, 3 * dy + dx)


def task_wgrad(idx, se, so, go, task, prev):
    half, q = so.shape[2], so.shape[3]
    return pl.pallas_call(
        functools.partial(task_wgrad_kernel, len(prev)),
        grid=(1,),
        in_specs=[
            SM,
            pl.BlockSpec((1,) + se.shape[1:], lambda k: (task, 0, 0, 0, 0)),
            pl.BlockSpec((1,) + so.shape[1:], lambda k: (task, 0, 0, 0, 0)),
            pl.BlockSpec((1, 1) + go.shape[2:], lambda k: (task, 1, 0, 0, 0)),
        ]
        + [ANY] * len(prev),
        out_specs=[pl.BlockSpec((NB * NB, 9 * HB, BLK), lambda k: (0, task, 0))] * 2,
        out_shape=[sds((NB * NB, 9 * TASKS * HB, BLK), BF)] * 2,
        input_output_aliases={4 + k: k for k in range(len(prev))},
        compiler_params=params(),
        cost_estimate=cost(2 * 9 * C * C * half * q, 8e6),
        name="task_wgrad",
    )(idx, se, so, go, *prev)


def task_fwd_kernel(task, n_pieces, n_prev, idx, se, so, *refs):
    pieces = refs[:n_pieces]
    out, wv, sems = refs[n_pieces + n_prev :]
    half, q = so.shape[2], so.shape[3]
    copies = weight_copies_task(idx, pieces, task * 9, wv, sems)
    for copy in copies:
        copy.start()
    for copy in copies:
        copy.wait()
    acc = None
    for dy in range(3):
        for dx in range(3):
            if dy == 1:
                view = so[0, dx]
            else:
                view = se[0, dx, dy // 2 : dy // 2 + half]
            piece = jnp.dot(
                view.reshape(half * q, C), wv[3 * dy + dx], preferred_element_type=F32
            )
            acc = piece if acc is None else acc + piece
    out[0] = (acc * 0.25).reshape(half, q, C).astype(BF)


def task_fwd(idx, se, so, pieces, task, prev):
    half, q = so.shape[2], so.shape[3]
    return pl.pallas_call(
        functools.partial(task_fwd_kernel, task, len(pieces), len(prev)),
        grid=(1,),
        in_specs=[
            SM,
            pl.BlockSpec((1,) + se.shape[1:], lambda k: (task, 0, 0, 0, 0)),
            pl.BlockSpec((1,) + so.shape[1:], lambda k: (task, 0, 0, 0, 0)),
        ]
        + [ANY] * (len(pieces) + len(prev)),
        out_specs=pl.BlockSpec((1, half, q, C), lambda k: (task, 0, 0, 0)),
        out_shape=sds((TASKS, half, q, C), BF),
        scratch_shapes=[pltpu.VMEM((9, C, C), BF), pltpu.SemaphoreType.DMA((32,))],
        input_output_aliases={3 + len(pieces) + k: k for k in range(len(prev))},
        compiler_params=params(),
        cost_estimate=cost(2 * 9 * C * C * half * q, 8e6),
        name="task_fwd",
    )(idx, se, so, *pieces, *prev)


def shampoo_step(g, left, right, lroot, rroot, weight, rate):
    low = g.astype(BF)
    ln = stat_decay * left + (1.0 - stat_decay) * lax.dot_general(
        low, low, NT, preferred_element_type=F32
    )
    rn = stat_decay * right + (1.0 - stat_decay) * lax.dot_general(
        low, low, TN, preferred_element_type=F32
    )
    step = jnp.dot(lroot.astype(BF), low, preferred_element_type=F32)
    step = jnp.dot(step.astype(BF), rroot.astype(BF), preferred_element_type=F32)
    return ln, rn, weight - rate * step


def shampoo_kernel(n_prev, idx, mine, other, left, right, lroot, rroot, weight, *refs):
    gr, ln, rn, wn = refs[n_prev:]
    even = idx[2] == 0
    for k in range(mine.shape[0] // HB):
        a, b = mine[k * HB : (k + 1) * HB], other[k * HB : (k + 1) * HB]
        g = jnp.concatenate([jnp.where(even, a, b), jnp.where(even, b, a)], axis=0).astype(F32)
        gr[0, k] = g
        ln[0, k], rn[0, k], wn[0, k] = shampoo_step(
            g, left[0, k], right[0, k], lroot[0, k], rroot[0, k], weight[0, k], conv_rate
        )


def shampoo_conv(idx, mine, other, state, first, prev):
    n = mine.shape[0] // HB
    each = 3
    block = pl.BlockSpec((1, each, BLK, BLK), lambda k: (0, first // each + k, 0, 0))
    half = pl.BlockSpec((each * HB, BLK), lambda k: (k, 0))
    full = state[0].shape
    return pl.pallas_call(
        functools.partial(shampoo_kernel, len(prev)),
        grid=(n // each,),
        in_specs=[SM, half, half] + [block] * 5 + [ANY] * len(prev),
        out_specs=[block] * 4,
        out_shape=[sds(full, F32)] * 4,
        input_output_aliases={8 + k: k for k in range(len(prev))},
        compiler_params=params(),
        cost_estimate=cost(n * 8 * BLK**3, n * 9 * BLK * BLK * 4),
        name="shampoo_conv",
    )(idx, mine, other, *state, *prev)


def shampoo_proj_kernel(g, left, right, lroot, rroot, weight, ln, rn, wn):
    for k in range(g.shape[2]):
        ln[0, 0, k], rn[0, 0, k], wn[0, 0, k] = shampoo_step(
            g[0, 0, k], left[0, 0, k], right[0, 0, k], lroot[0, 0, k], rroot[0, 0, k],
            weight[0, 0, k], proj_rate,
        )


def shampoo_proj(g, left, right, lroot, rroot, weight):
    block = pl.BlockSpec((1, 1) + g.shape[2:], lambda t, k: (t, k, 0, 0, 0))
    return pl.pallas_call(
        shampoo_proj_kernel,
        grid=g.shape[:2],
        in_specs=[block] * 6,
        out_specs=[block] * 3,
        out_shape=[sds(g.shape, F32)] * 3,
        compiler_params=params(),
        cost_estimate=cost(24 * 8 * BLK**3, 24 * 9 * BLK * BLK * 4),
        name="shampoo_proj",
    )(g, left, right, lroot, rroot, weight)


def to_rows(field):
    b, h, w, c = field.shape
    split = field.reshape(b, h, w // 2, 2, c)
    return jnp.transpose(split, (1, 3, 0, 2, 4)).reshape(h, w * b, c)


def from_rows(field, b):
    h, tall, c = field.shape
    split = field.reshape(h, 2, b, tall // (2 * b), c)
    return jnp.transpose(split, (2, 0, 3, 1, 4)).reshape(b, h, tall // b, c)


def pooled_rows(field):
    b, h, w, c = field.shape
    return jnp.transpose(field, (1, 0, 2, 3)).reshape(h, b * w, c)


def shards(
    images,
    cot_shared,
    cot_tasks,
    depth_mask,
    nash_weights,
    conv_weight,
    conv_left,
    conv_right,
    conv_left_root,
    conv_right_root,
    proj_weight,
    proj_left,
    proj_right,
    proj_left_root,
    proj_right_root,
    norm_params,
    norm_moment,
):
    batch, tile_h, tile_w, _ = images.shape
    half_h, half_w = tile_h // 2, tile_w // 2
    tall = batch * tile_w
    q = batch * half_w
    ha, wa = lax.axis_index("ha"), lax.axis_index("wa")
    count_all = float(
        batch * tile_h * tile_w * lax.axis_size("img") * lax.axis_size("ha") * lax.axis_size("wa")
    )
    idx = jnp.stack(
        [
            lax.axis_index("img"),
            ha,
            wa % 2,
            ha > 0,
            ha < lax.axis_size("ha") - 1,
            wa > 0,
            wa < lax.axis_size("wa") - 1,
        ]
    ).astype(jnp.int32)

    halves = conv_weight[0].reshape(conv_weight.shape[1], 2, HB, BLK)
    own = lax.dynamic_index_in_dim(halves, wa % 2, axis=1, keepdims=False).astype(BF)
    g0, g1 = Gather(own[None, 0:9]), Gather(own[None, 9:18])
    g0.near()
    edges = after(images, own)
    rows0 = jnp.stack(row_halo(edge_row(edges, 0), edge_row(edges, tile_h - 1)))
    g0.join(rows0)
    g0.far()
    g0.low()
    images = after(images, g0.line_low)
    off_down = 2 * C
    off_up = off_down + TASKS * CA
    gb1 = norm_params[:, 0:C]
    gb2 = norm_params[:, C : 2 * C]
    gbd = norm_params[:, off_down:off_up]
    gbu = jnp.transpose(norm_params[:, off_up:].reshape(2, TASKS, C), (1, 0, 2)).reshape(-1, C)
    proj_low = proj_weight.astype(BF)
    down = jnp.transpose(proj_low[:, 0].reshape(TASKS, C, CA), (1, 0, 2)).reshape(C, TASKS * CA)
    up = jnp.transpose(proj_low[:, 1], (0, 2, 1, 3)).reshape(TASKS, CA, C)

    image_rows = to_rows(images)
    x3 = shift_copies(idx, image_rows, rows0, halo_cols(image_rows, rows0, batch), batch)
    g0.high(g0.low_x, g0.low_y)
    g0.corner_a(x3)
    g0.corner_b()
    g1.near(g0.line_high)
    cot_tasks = after(cot_tasks, g0.line_high)

    depth_pick = jnp.arange(TASKS) == 1
    scale = jnp.where(depth_pick, depth_mask.astype(F32)[..., None], 1.0) * nash_weights
    weighted = cot_tasks.astype(F32).reshape(batch, half_h, half_w, TASKS, C)
    weighted = (weighted * (scale * 0.25)[..., None]).astype(BF)
    grid = jnp.transpose(weighted, (3, 1, 0, 2, 4))
    top, bottom = row_halo(grid[:, 0:1], grid[:, half_h - 1 :])
    top = jnp.where(ha > 0, top, jnp.zeros_like(top))
    bottom = jnp.where(ha < lax.axis_size("ha") - 1, bottom, jnp.zeros_like(bottom))
    grid = jnp.concatenate([top, grid, bottom], axis=1)
    left, right = col_halo(grid[:, :, :, 0:1], grid[:, :, :, half_w - 1 :])
    grid = jnp.concatenate([left, grid, right], axis=3)
    go3 = jnp.stack([grid[:, :, :, k : k + half_w] for k in range(3)], axis=1)
    go3 = go3.reshape(TASKS, 3, half_h + 2, q, C)
    cot = pooled_rows(cot_shared.astype(F32) * 0.25)

    g1.join(g0.corner_high)
    g1.far()
    g1.low()
    w0 = g0.pieces()
    z1, s1 = conv(after(idx, g1.line_low, go3), x3, w0, False, True, F32, "conv_first")

    def none(dep):
        return ()

    halo1 = halo(z1, batch)
    s1 = after(s1, g1.line_high)
    wt_mine = lax.all_gather(after(own[18:], s1), ("img", "ha"), axis=0, tiled=False)
    g1.high(s1)

    def s1_img1(dep):
        return g1.high_x, g1.high_y

    def s1_img2(dep):
        g1.corner_a(dep)
        g1.corner_b(dep)
        return ()

    s1 = sum_all(s1, [none, none, none, s1_img1, s1_img2])
    u3, hp, hc, hs = mid(idx, s1, gb1, z1, *halo1, down, batch, count_all)
    w1 = g1.pieces(hs)
    kept = {}

    def s2_ha1(dep):
        kept["z2"], kept["s2"] = conv(idx, after(u3, dep), w1, False, True, F32, "conv_second")
        return (kept["s2"],)

    hs = sum_all(hs, [none, none, none, s2_ha1, none], ("wa", "img", "ha"))
    z2, s2 = kept["z2"], kept["s2"]
    halo2 = halo(z2, batch)
    h, hcb, ms = hidden(hs, gbd, hp, hc, up, tall, count_all)
    s2m = sum_all(jnp.concatenate([s2, ms], axis=0), (), ("wa", "img", "ha"))
    wt_mine = after(wt_mine, s2m)
    wt = (wt_mine, swap(wt_mine, "wa", 1))
    kept["da"] = ()
    for task in range(TASKS):
        kept["da"] = (task_back(idx, go3, wt, task, kept["da"]),)
    s2, ms = s2m[0:2], s2m[2:]
    da = kept["da"][0].reshape(TASKS, tile_h, tall, C)
    se, so, dym, dy2, pooled, gsum = attend(
        idx, s2, gb2, ms, gbu, z2, *halo2, h, hcb, up, da, cot, batch, count_all
    )

    dhalo2 = halo(dy2, batch)
    kept["wt"] = ()

    def run_wgrad(task):
        def run(dep):
            kept["wt"] = task_wgrad(after(idx, dep), se, so, go3, task, kept["wt"])
            return tuple(kept["wt"])

        return run

    gsum = sum_all(gsum, [none, run_wgrad(0), run_wgrad(1), run_wgrad(2)])
    mine_t, other_t = kept["wt"]
    other_t = swap(other_t, "wa", 1)
    dup, dh, dhs = mask_back(ms, gbu, gsum[0:6], hs, gbd, dym, h, hp, up, tall, count_all)

    def run_second_back(dep):
        gs = after(gsum[6:8], dep)
        kept["z3"] = norm_back(
            idx, s2, gb2, gs, dy2, dhalo2, z2, halo2, batch, count_all, "second_back"
        )
        part_t = add_low(mine_t, after(other_t, dep))
        kept["gt"] = lax.psum_scatter(part_t, ("img", "ha"), scatter_dimension=0, tiled=True)
        return kept["z3"], part_t

    def run_conv_back(dep):
        kept["part"] = conv(idx, after(kept["z3"], dep), w1, True, False, F32, "conv_second_back")
        return (kept["part"],)

    dhs = sum_all(dhs, [run_second_back, none, run_conv_back, none, none])
    z3, part = kept["z3"], kept["part"]
    ddown, dy1, gs1 = first_back(hs, gbd, dhs, s1, gb1, dh, hp, u3, part, z1, down, count_all)
    dhalo1 = halo(dy1, batch)

    def run_wgrad_second(dep):
        kept["r1"] = Scatter(*wgrad(after(idx, dep), u3, z3, "wgrad_second", (ddown, dup)))
        return (kept["r1"].other,)

    def run_wa(dep):
        kept["r1"].wa(dep)
        return ()

    gs1 = sum_all(gs1, [none, run_wgrad_second, none, none, run_wa])
    r1 = kept["r1"]
    y3 = norm_back(idx, s1, gb1, gs1, dy1, dhalo1, z1, halo1, batch, count_all, "first_norm_back")
    y3 = after(y3, r1.corner_sum(y3))
    r1.corner_send()
    r0 = Scatter(*wgrad(idx, x3, y3, "wgrad_first"))
    state = (conv_left, conv_right, conv_left_root, conv_right_root, conv_weight)
    r0.wa()
    r1.high_sum(r0.mine)
    r1.high_send()
    r1.low_sum(*r1.high)
    r0.corner_sum(*r1.low)
    r0.corner_send()
    r1.low_send(r0.corner)
    outs = (task_fwd(after(idx, r0.corner, *r1.low), se, so, wt, 0, ()),)
    r0.high_sum(*outs)
    r0.high_send()
    r0.low_sum(*r0.high)
    r0.low_send()
    r1.far_sum(*r0.low)
    r1.far_send()
    outs = (task_fwd(after(idx, r1.far), se, so, wt, 1, outs),)
    r0.far_sum(*outs)
    r0.far_send()
    r1.near_sum(r0.far)
    r1.near_send()
    outs = (task_fwd(after(idx, r1.near), se, so, wt, 2, outs),)
    r0.near_sum(*outs)
    r0.near_send()
    grad1, grad1_other = r1.finish(r0.near)
    proj_total = gather_proj(grad1[9 * HB :])
    image_grad = conv(idx, after(y3, grad1), w0, True, False, BF, "conv_first_back")
    new = shampoo_conv(
        after(idx, image_grad), grad1[: 9 * HB], grad1_other[: 9 * HB], state, 9, ()
    )
    grad0, grad0_other = r0.finish(image_grad)
    new = shampoo_conv(idx, grad0, grad0_other, state, 0, new)
    gradt = after(kept["gt"][0], new[0])
    new = shampoo_conv(idx, gradt, swap(gradt, "wa", 1), state, 18, new)
    conv_total, conv_left_new, conv_right_new, conv_weight_new = new
    task_out = outs[0]

    image_grad = from_rows(image_grad, batch)
    task_out = jnp.transpose(
        task_out.reshape(TASKS, half_h, batch, half_w, C), (2, 1, 3, 0, 4)
    ).reshape(batch, half_h, half_w, TASKS * C)
    shared_out = jnp.transpose(
        pooled.astype(BF).reshape(half_h, batch, half_w, C), (1, 0, 2, 3)
    )

    proj_left_new, proj_right_new, proj_weight_new = shampoo_proj(
        proj_total, proj_left, proj_right, proj_left_root, proj_right_root, proj_weight
    )

    corner = jnp.sum(gsum[8:14], axis=1)
    gram = jnp.stack(
        [corner[0], corner[1], corner[2], corner[1], corner[3], corner[4], corner[2], corner[4], corner[5]]
    ).reshape(TASKS, TASKS)
    gain_grads = jnp.concatenate([gs1[1], gsum[7], dhs[1], gsum[1], gsum[3], gsum[5]])
    bias_grads = jnp.concatenate([gs1[0], gsum[6], dhs[0], gsum[0], gsum[2], gsum[4]])
    norm_grad = jnp.stack([gain_grads, bias_grads])
    moment_new = moment_decay * norm_moment + (1.0 - moment_decay) * norm_grad * norm_grad
    norm_new = norm_params - norm_rate * norm_grad / (jnp.sqrt(moment_new) + 1e-08)
    return (
        shared_out,
        task_out,
        image_grad,
        gram,
        conv_total,
        conv_left_new,
        conv_right_new,
        conv_weight_new,
        proj_total,
        proj_left_new,
        proj_right_new,
        proj_weight_new,
        norm_grad,
        moment_new,
        norm_new,
    )


def solution(mesh):
    tile = P("img", "ha", "wa", None)
    owned = P(("img", "ha"), None, None, None)
    return jax.shard_map(
        shards,
        mesh=mesh,
        in_specs=(tile, tile, tile, P("img", "ha", "wa"), P()) + (owned,) * 5 + (P(),) * 7,
        out_specs=(tile, tile, tile, P()) + (owned,) * 4 + (P(),) * 7,
        check_vma=False,
    )
```

```python
import functools

import jax
import jax.numpy as jnp
from jax import lax
from jax.experimental import pallas as pl
from jax.experimental.pallas import tpu as pltpu
from jax.sharding import PartitionSpec as P

C = 512
CA = 128
TASKS = 3
BLK = 128
HB = 64
NB = C // BLK
PROJ_ROWS = TASKS * 2 * NB * BLK // (2 * NB * NB)

eps_norm = 1e-05
conv_rate = 0.08
proj_rate = 0.2
norm_rate = 0.1
stat_decay = 0.9
moment_decay = 0.95

BF = jnp.bfloat16
F32 = jnp.float32
VM = pl.BlockSpec(memory_space=pltpu.VMEM)
SM = pl.BlockSpec(memory_space=pltpu.SMEM)
ANY = pl.BlockSpec(memory_space=pl.ANY)
VMEM_LIMIT = 56 * 1024 * 1024
NT = (((1,), (1,)), ((), ()))
TN = (((0,), (0,)), ((), ()))


def sds(shape, dtype):
    return jax.ShapeDtypeStruct(shape, dtype)


def params(**kw):
    return pltpu.CompilerParams(vmem_limit_bytes=VMEM_LIMIT, **kw)


def cost(flops, nbytes, trans=0):
    return pl.CostEstimate(
        flops=int(flops / 16), bytes_accessed=int(nbytes / 16), transcendentals=int(trans / 16)
    )


def pairs(axis, step):
    return [(i, i ^ step) for i in range(lax.axis_size(axis))]


def swap(value, axis, step):
    return lax.ppermute(value, axis, pairs(axis, step))


def sum_all(value, axes=("wa", "ha", "img"), **fillers):
    for axis in axes:
        count = lax.axis_size(axis)
        total = value
        if count <= 4:
            for step in range(1, count):
                total = total + swap(value, axis, step)
        else:
            step = 1
            while step < count:
                total = total + swap(total, axis, step)
                step *= 2
        if axis in fillers:
            total = after(total, *fillers[axis](value))
        value = total
    return value


def row_halo(first, last):
    count = lax.axis_size("ha")
    odd = lax.axis_index("ha") % 2 == 1
    got = []
    for shift in (0, 1):
        upper = [i for i in range(count) if i % 2 == shift and i + 1 < count]
        pairing = {i: i + 1 for i in upper} | {i + 1: i for i in upper}
        send = jnp.where(odd == (shift == 1), last, first)
        got.append(lax.ppermute(send, "ha", [(i, pairing.get(i, i)) for i in range(count)]))
    return jnp.where(odd, got[0], got[1]), jnp.where(odd, got[1], got[0])


def col_halo(left_edge, right_edge):
    count = lax.axis_size("wa")
    if count == 2:
        mine = jnp.where(lax.axis_index("wa") == 0, right_edge, left_edge)
        got = swap(mine, "wa", 1)
        none = jnp.zeros_like(got)
        first = lax.axis_index("wa") == 0
        return jnp.where(first, none, got), jnp.where(first, got, none)
    up = [(i, i + 1) for i in range(count - 1)]
    down = [(i + 1, i) for i in range(count - 1)]
    return lax.ppermute(right_edge, "wa", up), lax.ppermute(left_edge, "wa", down)


def halo(edges, batch):
    edge_rows, edge_cols = edges
    top, bottom = row_halo(edge_rows[0], edge_rows[1])
    rows = jnp.stack([top, bottom])
    return rows, halo_cols(edge_cols.astype(BF), rows, batch)


def after(value, *deps):
    return lax.optimization_barrier((value,) + deps)[0]


class Gather:
    def __init__(self, own):
        self.own = own

    def near(self, *deps):
        self.near_got = swap(after(self.own, *deps), "ha", 2)
        return self.near_got

    def join(self, *deps):
        self.line_low = after(jnp.concatenate([self.own, self.near_got], axis=0), *deps)
        return self.line_low

    def far(self, *deps):
        self.line_high = swap(after(self.line_low, *deps), "ha", 1)
        return self.line_high

    def low(self, *deps):
        low = after(self.line_low, *deps)
        self.low_x, self.low_y = swap(low, "img", 1), swap(low, "img", 2)
        return self.low_x, self.low_y

    def high(self, *deps):
        high = after(self.line_high, *deps)
        self.high_x, self.high_y = swap(high, "img", 1), swap(high, "img", 2)
        return self.high_x, self.high_y

    def corner_a(self, *deps):
        self.corner_low = swap(after(self.low_x, *deps), "img", 2)
        return self.corner_low

    def corner_b(self, *deps):
        self.corner_high = swap(after(self.high_y, *deps), "img", 1)
        return self.corner_high

    def pieces(self, *deps):
        mine = (
            self.line_low, self.line_high, self.low_x, self.high_x,
            self.low_y, self.high_y, self.corner_low, self.corner_high,
        )
        return mine + tuple(swap(after(part, *deps), "wa", 1) for part in mine)


def edge_row(field, h):
    return to_rows(field[:, h : h + 1])[0]


def halo_cols(edge_cols, rows, batch):
    tall, chans = rows.shape[1:]
    across = tall // (2 * batch)
    around = rows.reshape(2, 2, batch, across, chans)

    def edge(side):
        inner = edge_cols[:, side * batch : (side + 1) * batch]
        outer = around[:, side, :, (across - 1) * side]
        return jnp.concatenate([outer[0:1], inner, outer[1:2]], axis=0)

    return jnp.concatenate(col_halo(edge(0), edge(1)), axis=1).astype(F32)


def ring_gather(value, axis):
    count = lax.axis_size(axis)
    parts = [value] + [
        lax.ppermute(value, axis, [(i, (i + step) % count) for i in range(count)])
        for step in range(1, count)
    ]
    ring = jnp.stack(parts[::-1] + parts[:0:-1])
    start = count - 1 - lax.axis_index(axis)
    return lax.dynamic_slice_in_dim(ring, start, count, axis=0)


def gather_proj_line(own):
    got = swap(own, "wa", 1)
    even = lax.axis_index("wa") % 2 == 0
    value = jnp.stack([jnp.where(even, own, got), jnp.where(even, got, own)])
    return ring_gather(value, "ha")


def gather_proj(line):
    return ring_gather(line, "img").reshape(TASKS, 2, NB, BLK, BLK).astype(F32)


def add_low(*parts):
    total = parts[0].astype(F32)
    for part in parts[1:]:
        total = total + part.astype(F32)
    return total.astype(BF)


class Scatter:
    def __init__(self, mine, other):
        self.mine, self.other = mine, other

    def wa(self, *deps):
        self.came = swap(after(self.other, *deps), "wa", 1)
        return self.came

    def corner_sum(self, *deps):
        self.corner = add_low(self.mine[3], after(self.came, *deps)[3])
        return self.corner

    def corner_send(self, *deps):
        corner = after(self.corner, *deps)
        self.to_x = swap(corner[0:2], "img", 1)
        self.to_y = swap(corner[2:4], "img", 2)
        return self.to_x, self.to_y

    def high_sum(self, *deps):
        came = after(self.came, *deps)
        self.high = (
            add_low(self.mine[1][2:4], came[1][2:4], self.to_y),
            add_low(self.mine[2][2:4], came[2][2:4]),
        )
        return self.high

    def high_send(self, *deps):
        self.high_x = swap(after(self.high[0], *deps), "img", 1)
        self.high_y = swap(after(self.high[1], *deps), "img", 2)
        return self.high_x, self.high_y

    def low_sum(self, *deps):
        came = after(self.came, *deps)
        self.low = (
            add_low(self.mine[1][0:2], came[1][0:2]),
            add_low(self.mine[2][0:2], came[2][0:2], self.to_x),
        )
        return self.low

    def low_send(self, *deps):
        self.low_x = swap(after(self.low[0], *deps), "img", 1)
        self.low_y = swap(after(self.low[1], *deps), "img", 2)
        return self.low_x, self.low_y

    def far_sum(self, *deps):
        came = after(self.came, *deps)
        self.far = add_low(self.mine[0][2:4], came[0][2:4], self.high_x, self.high_y)
        return self.far

    def far_send(self, *deps):
        self.from_far = swap(after(self.far, *deps), "ha", 1)
        return self.from_far

    def near_sum(self, *deps):
        came = after(self.came, *deps)
        self.near = add_low(
            self.mine[0][1], came[0][1], self.low_x[1], self.low_y[1], self.from_far[1]
        )
        return self.near

    def near_send(self, *deps):
        self.from_near = swap(after(self.near, *deps), "ha", 2)
        return self.from_near

    def finish(self, *deps):
        total = add_low(
            after(self.mine[0][0], *deps), self.came[0][0], self.low_x[0], self.low_y[0], self.from_far[0], self.from_near
        )
        step = 2
        while step < lax.axis_size("wa"):
            total = add_low(total, swap(total, "wa", step))
            step *= 2
        return total, swap(total, "wa", 1)


def coef(sums, gb, count_all):
    mean = sums[0:1] / count_all
    var = sums[1:2] / count_all - mean * mean
    rs = lax.rsqrt(var + eps_norm)
    sc = gb[0:1] * rs
    return mean, rs, sc, gb[1:2] - mean * sc


def sigm(v):
    return pl.reciprocal(1.0 + jnp.exp(-v), approx=True)


def side_mask(idx, rows, lanes, count):
    row = lax.broadcasted_iota(jnp.int32, (rows, lanes), 0)
    return jnp.where(row < rows // 2, idx[5], idx[6]).astype(F32)


def col_block(cols, r, side, batch, across):
    lanes = cols.shape[-1]
    parts = [
        jnp.broadcast_to(cols[r, pl.ds(side * batch + b, 1), :], (across, lanes))
        for b in range(batch)
    ]
    return jnp.concatenate(parts, axis=0)


def shifted(even, odd, hl, hr, batch, across):
    lanes = even.shape[-1]
    shape = (batch, across, lanes)
    j = lax.broadcasted_iota(jnp.int32, shape, 1)
    lo = jnp.where(j == 0, hl.reshape(shape), pltpu.roll(odd.reshape(shape), 1, 1))
    hi = jnp.where(j == across - 1, hr.reshape(shape), pltpu.roll(even.reshape(shape), across - 1, 1))
    return lo.reshape(even.shape), hi.reshape(even.shape)


def put_row(x3, r, row, cols, batch, across):
    q = batch * across
    even, odd = row[0:q], row[q : 2 * q]
    hl = col_block(cols, r, 0, batch, across)
    hr = col_block(cols, r, 1, batch, across)
    lo, hi = shifted(even, odd, hl, hr, batch, across)
    x3[0, r] = jnp.concatenate([lo, even], axis=0).astype(BF)
    x3[1, r] = row.astype(BF)
    x3[2, r] = jnp.concatenate([odd, hi], axis=0).astype(BF)


def flip(s):
    return s // 2 + 2 * (s % 2)


def weight_copies_rel(idx, pieces, first, wv, sems):
    copies = []
    count = len(pieces) // 2
    for half in range(2):
        parts = pieces[half * count : (half + 1) * count]
        h = lax.bitwise_xor(idx[2], half)
        for e in range(4):
            i = lax.bitwise_xor(idx[0], e)
            row0 = pl.multiple_of(i * BLK + h * HB, HB)
            for s in range(4):
                j = lax.bitwise_xor(idx[1], flip(s))
                col0 = pl.multiple_of(j * BLK, BLK)
                copies.append(
                    pltpu.make_async_copy(
                        parts[2 * e + s // 2].at[s % 2, pl.ds(first, 9)],
                        wv.at[:, pl.ds(row0, HB), pl.ds(col0, BLK)],
                        sems.at[len(copies)],
                    )
                )
    return copies


def weight_copies_task(idx, pieces, first, wv, sems):
    copies = []
    for half in range(2):
        h = lax.bitwise_xor(idx[2], half)
        for i in range(NB):
            row0 = pl.multiple_of(i * BLK + h * HB, HB)
            for j in range(NB):
                copies.append(
                    pltpu.make_async_copy(
                        pieces[half].at[i * NB + j, pl.ds(first, 9)],
                        wv.at[:, pl.ds(row0, HB), j * BLK : (j + 1) * BLK],
                        sems.at[len(copies)],
                    )
                )
    return copies


def put_edges(field, edge_rows, edge_cols, batch):
    height, tall = field.shape[0], field.shape[1]
    across = tall // (2 * batch)
    edge_rows[0] = field[0].astype(BF)
    edge_rows[1] = field[height - 1].astype(BF)

    @pl.loop(0, height)
    def _(h):
        for side in range(2):
            for b in range(batch):
                place = side * (tall // 2 + across - 1) + b * across
                edge_cols[h, side * batch + b : side * batch + b + 1] = field[h, place : place + 1]


def shift_kernel(batch, idx, x_ref, rows_ref, cols_ref, x3_ref, work):
    height, tall = x_ref.shape[0], x_ref.shape[1]
    across = tall // (2 * batch)
    top, bottom = idx[3].astype(F32), idx[4].astype(F32)
    work[...] = cols_ref[...]
    work[0] = work[0] * top
    work[height + 1] = work[height + 1] * bottom
    cols_ref = work
    put_row(x3_ref, 0, rows_ref[0].astype(F32) * top, cols_ref, batch, across)
    put_row(x3_ref, height + 1, rows_ref[1].astype(F32) * bottom, cols_ref, batch, across)

    @pl.loop(0, height)
    def _(h):
        put_row(x3_ref, h + 1, x_ref[h].astype(F32), cols_ref, batch, across)


def shift_copies(idx, field, rows, cols, batch):
    height, tall, chans = field.shape
    lanes = BLK
    return pl.pallas_call(
        functools.partial(shift_kernel, batch),
        grid=(chans // lanes,),
        in_specs=[
            SM,
            pl.BlockSpec((height, tall, lanes), lambda c: (0, 0, c)),
            pl.BlockSpec((2, tall, lanes), lambda c: (0, 0, c)),
            pl.BlockSpec((height + 2, 2 * batch, lanes), lambda c: (0, 0, c)),
        ],
        out_specs=pl.BlockSpec((3, height + 2, tall, lanes), lambda c: (0, 0, 0, c)),
        out_shape=sds((3, height + 2, tall, chans), BF),
        scratch_shapes=[pltpu.VMEM((height + 2, 2 * batch, lanes), F32)],
        compiler_params=params(),
        cost_estimate=cost(0, 8e6),
        name="shift_copies",
    )(idx, field, rows, cols)


def conv_kernel(n_pieces, batch, transposed, want_sums, idx_ref, x_ref, *refs):
    pieces = refs[:n_pieces]
    o_ref = refs[n_pieces]
    s_ref, er_ref, ec_ref = refs[n_pieces + 1 : n_pieces + 4] if want_sums else (None,) * 3
    wv, sems = refs[-2:]
    copies = weight_copies_rel(idx_ref, pieces, 0, wv, sems)
    for copy in copies:
        copy.start()
    for copy in copies:
        copy.wait()
    height, tall = x_ref.shape[1] - 2, x_ref.shape[2]
    step = height // 2
    rows = step * tall
    if want_sums:
        s_ref[...] = jnp.zeros(s_ref.shape, F32)

    @pl.loop(0, 2)
    def _(part):
        acc = None
        for dy in range(3):
            for dx in range(3):
                if transposed:
                    view = x_ref[2 - dx, pl.ds(part * step + 2 - dy, step)]
                    dims = NT
                else:
                    view = x_ref[dx, pl.ds(part * step + dy, step)]
                    dims = (((1,), (0,)), ((), ()))
                piece = lax.dot_general(
                    view.reshape(rows, C), wv[3 * dy + dx], dims, preferred_element_type=F32
                )
                acc = piece if acc is None else acc + piece
        o_ref[pl.ds(part * step, step)] = acc.reshape(step, tall, C).astype(o_ref.dtype)
        if want_sums:
            s_ref[0:1] += jnp.sum(acc, axis=0, keepdims=True)
            s_ref[1:2] += jnp.sum(acc * acc, axis=0, keepdims=True)

    if want_sums:
        put_edges(o_ref, er_ref, ec_ref, batch)


def conv(idx, x3, pieces, transposed, dtype, name, batch=0):
    want_sums = batch > 0
    height, tall = x3.shape[1] - 2, x3.shape[2]
    out_shape = [sds((height, tall, C), dtype)]
    if want_sums:
        out_shape += [sds((2, C), F32), sds((2, tall, C), BF), sds((height, 2 * batch, C), F32)]
    out = pl.pallas_call(
        functools.partial(conv_kernel, len(pieces), batch, transposed, want_sums),
        in_specs=[SM, VM] + [ANY] * len(pieces),
        out_specs=[VM] * len(out_shape),
        out_shape=out_shape,
        scratch_shapes=[pltpu.VMEM((9, C, C), BF), pltpu.SemaphoreType.DMA((32,))],
        compiler_params=params(),
        cost_estimate=cost(2 * 9 * C * C * height * tall, 10e6),
        name=name,
    )(idx, x3, *pieces)
    return (out[0], out[1], out[2:]) if want_sums else out[0]


def mid_kernel(batch, count_all, idx, st, gb, z_ref, rows_ref, cols_ref, d_ref, u3, hp, hc, hs, uc):
    height, tall, lanes = z_ref.shape
    across = tall // (2 * batch)
    step = pl.program_id(0)
    mean, rs, sc, sh = coef(st[...], gb[...], count_all)

    def act(v):
        y = v * sc + sh
        return y * sigm(y)

    mask = side_mask(idx, 2 * batch, lanes, 0)
    flat = act(cols_ref[...].reshape(-1, lanes)).reshape(height + 2, 2 * batch, lanes)
    uc[...] = flat * mask[None]
    uc[0] = uc[0] * idx[3].astype(F32)
    uc[height + 1] = uc[height + 1] * idx[4].astype(F32)
    put_row(u3, 0, act(rows_ref[0].astype(F32)) * idx[3].astype(F32), uc, batch, across)
    put_row(u3, height + 1, act(rows_ref[1].astype(F32)) * idx[4].astype(F32), uc, batch, across)

    @pl.loop(0, height)
    def _(h):
        put_row(u3, h + 1, act(z_ref[h]), uc, batch, across)

    @pl.when(step == 0)
    def _():
        hp[...] = jnp.zeros(hp.shape, F32)
        hc[...] = jnp.zeros(hc.shape, F32)

    hc[...] += jnp.dot(
        uc[...].reshape(-1, lanes).astype(BF), d_ref[...], preferred_element_type=F32
    )
    part = (height + 2) // 2
    size = part * tall

    @pl.loop(0, 2)
    def _(k):
        hp[pl.ds(pl.multiple_of(k * size, size), size)] += jnp.dot(
            u3[1, pl.ds(k * part, part)].reshape(size, lanes),
            d_ref[...],
            preferred_element_type=F32,
        )

    @pl.when(step == pl.num_programs(0) - 1)
    def _():
        inner = hp[tall : (height + 1) * tall]
        hs[0:1] = jnp.sum(inner, axis=0, keepdims=True)
        hs[1:2] = jnp.sum(inner * inner, axis=0, keepdims=True)


def mid(idx, st, gb, z, rows, cols, down, batch, count_all):
    height, tall, chans = z.shape
    lanes = BLK
    r = height + 2
    wide = TASKS * CA
    return pl.pallas_call(
        functools.partial(mid_kernel, batch, count_all),
        grid=(chans // lanes,),
        in_specs=[
            SM,
            pl.BlockSpec((2, lanes), lambda c: (0, c)),
            pl.BlockSpec((2, lanes), lambda c: (0, c)),
            pl.BlockSpec((height, tall, lanes), lambda c: (0, 0, c)),
            pl.BlockSpec((2, tall, lanes), lambda c: (0, 0, c)),
            pl.BlockSpec((r, 2 * batch, lanes), lambda c: (0, 0, c)),
            pl.BlockSpec((lanes, wide), lambda c: (c, 0)),
        ],
        out_specs=[
            pl.BlockSpec((3, r, tall, lanes), lambda c: (0, 0, 0, c)),
            pl.BlockSpec((r * tall, wide), lambda c: (0, 0)),
            pl.BlockSpec((r * 2 * batch, wide), lambda c: (0, 0)),
            pl.BlockSpec((2, wide), lambda c: (0, 0)),
        ],
        out_shape=[
            sds((3, r, tall, chans), BF),
            sds((r * tall, wide), F32),
            sds((r * 2 * batch, wide), F32),
            sds((2, wide), F32),
        ],
        scratch_shapes=[pltpu.VMEM((r, 2 * batch, lanes), F32)],
        compiler_params=params(),
        cost_estimate=cost(2 * r * tall * chans * wide, 10e6, 2e6),
        name="mid",
    )(idx, st, gb, z, rows, cols, down)


def hidden_kernel(tall, count_all, st, gb, hp, hc, up, h_ref, hcb, ms):
    mean, rs, sc, sh = coef(st[...], gb[...], count_all)
    yc = hc[...] * sc + sh
    hcb[...] = (yc * sigm(yc)).astype(BF)
    n_rows = hp.shape[0] // tall
    ms[...] = jnp.zeros(ms.shape, F32)

    def row(r):
        at = pl.ds(pl.multiple_of(r * tall, tall), tall)
        y = hp[at] * sc + sh
        h_ref[at] = (y * sigm(y)).astype(BF)

    @pl.loop(0, n_rows)
    def _(r):
        row(r)

    chunk = 4 * tall
    for t in range(TASKS):

        @pl.loop(0, (n_rows - 2) // 4)
        def _(k):
            at = pl.ds(pl.multiple_of(tall + k * chunk, tall), chunk)
            pre = jnp.dot(h_ref[at, t * CA : (t + 1) * CA], up[t], preferred_element_type=F32)
            ms[2 * t : 2 * t + 1] += jnp.sum(pre, axis=0, keepdims=True)
            ms[2 * t + 1 : 2 * t + 2] += jnp.sum(pre * pre, axis=0, keepdims=True)


def hidden(st, gb, hp, hc, up, tall, count_all):
    return pl.pallas_call(
        functools.partial(hidden_kernel, tall, count_all),
        in_specs=[VM] * 5,
        out_specs=[VM] * 3,
        out_shape=[sds(hp.shape, BF), sds(hc.shape, BF), sds((2 * TASKS, C), F32)],
        compiler_params=params(),
        cost_estimate=cost(2 * hp.shape[0] * CA * C * TASKS, 5e6, 2e6),
        name="hidden",
    )(st, gb, hp, hc, up)


def task_weights(idx, pieces, wv, sems):
    t = pl.program_id(0)
    slot = lax.rem(t, 2)

    def copies(task, place):
        return weight_copies_task(idx, pieces, task * 9, wv.at[place], sems.at[place])

    @pl.when(t == 0)
    def _():
        for copy in copies(0, 0):
            copy.start()

    for copy in copies(t, slot):
        copy.wait()

    @pl.when(t + 1 < pl.num_programs(0))
    def _():
        for copy in copies(t + 1, 1 - slot):
            copy.start()

    return slot


def da_kernel(idx, go, mine, other, da, wv, ws, sems):
    q = go.shape[3]
    half_h = go.shape[2] - 2
    slot = task_weights(idx, (mine, other), wv, sems)

    def add(a, b):
        return (a.astype(F32) + b.astype(F32)).astype(BF)

    for a in range(2):
        for k in range(2):
            taps = []
            for dx in range(3):
                if k == 0:
                    taps.append(add(wv[slot, 3 * a + dx], wv[slot, 3 * (a + 1) + dx]))
                else:
                    taps.append(wv[slot, 3 * (2 if a == 0 else 0) + dx])
            ws[a, k, 0, 0] = add(taps[0], taps[1])
            ws[a, k, 0, 1] = taps[2]
            ws[a, k, 1, 0] = add(taps[1], taps[2])
            ws[a, k, 1, 1] = taps[0]
    for a in range(2):
        for bb in range(2):
            acc = None
            for k in range(2):
                for m in range(2):
                    ro = 0 if k == 0 else (-1 if a == 0 else 1)
                    co = 0 if m == 0 else (-1 if bb == 0 else 1)
                    view = go[0, co + 1, 1 + ro : 1 + ro + half_h].reshape(half_h * q, C)
                    piece = lax.dot_general(
                        view, ws[a, k, bb, m], NT, preferred_element_type=F32
                    )
                    acc = piece if acc is None else acc + piece
            da[0, :, a, bb] = acc.reshape(half_h, q, C).astype(BF)


def task_back(idx, go, pieces):
    half_h, q = go.shape[2] - 2, go.shape[3]
    out = pl.pallas_call(
        da_kernel,
        grid=(TASKS,),
        in_specs=[SM, pl.BlockSpec((1,) + go.shape[1:], lambda t: (t, 0, 0, 0, 0)), ANY, ANY],
        out_specs=pl.BlockSpec((1, half_h, 2, 2, q, C), lambda t: (t, 0, 0, 0, 0, 0)),
        out_shape=sds((TASKS, half_h, 2, 2, q, C), BF),
        scratch_shapes=[
            pltpu.VMEM((2, 9, C, C), BF),
            pltpu.VMEM((2, 2, 2, 2, C, C), BF),
            pltpu.SemaphoreType.DMA((2, 32)),
        ],
        compiler_params=params(),
        cost_estimate=cost(TASKS * 2 * 16 * C * C * half_h * q, 24e6),
        name="task_back",
    )(idx, go, *pieces)
    return out.reshape(TASKS, 2 * half_h, 2 * q, C)


def attend_kernel(
    batch, count_all, idx, st, gb, mst, mgb, z_ref, rows_ref, cols_ref, h_ref, hc_ref, up,
    se, so, pooled,
    ac, pre, prev,
):
    height, tall, lanes = z_ref.shape
    across = tall // (2 * batch)
    q = tall // 2
    _, _, sc, sh = coef(st[...], gb[...], count_all)
    mcoef = [
        coef(mst[2 * t : 2 * t + 2], mgb[2 * t : 2 * t + 2], count_all) for t in range(TASKS)
    ]
    mask = side_mask(idx, 2 * batch, lanes, 0)
    top, bottom = idx[3].astype(F32), idx[4].astype(F32)

    y = cols_ref[...].reshape(-1, lanes) * sc + sh
    pc = (y * sigm(y)).reshape(height + 2, 2 * batch, lanes) * mask[None]
    for t in range(TASKS):
        mc = jnp.dot(hc_ref[:, t * CA : (t + 1) * CA], up[t], preferred_element_type=F32)
        _, _, msc, msh = mcoef[t]
        mc = sigm(mc * msc + msh).reshape(height + 2, 2 * batch, lanes)
        ac[t] = (mc * pc).astype(BF).astype(F32)
        ac[t, 0] = ac[t, 0] * top
        ac[t, height + 1] = ac[t, height + 1] * bottom
        pre[t] = jnp.dot(
            h_ref[:, t * CA : (t + 1) * CA], up[t], preferred_element_type=F32
        ).reshape(height + 2, tall, lanes)

    def sums_of(r, p):
        out = []
        for t in range(TASKS):
            _, _, msc, msh = mcoef[t]
            a = (sigm(pre[t, r] * msc + msh) * p).astype(BF).astype(F32)
            even, odd = a[0:q], a[q : 2 * q]
            lo, hi = shifted(
                even,
                odd,
                col_block(ac.at[t], r, 0, batch, across),
                col_block(ac.at[t], r, 1, batch, across),
                batch,
                across,
            )
            out.append((lo + even, even + odd, odd + hi))
        return out

    def halo_row(r, place, scale):
        yy = rows_ref[place].astype(F32) * sc + sh
        return sums_of(r, yy * sigm(yy) * scale)

    def inner(h):
        yy = z_ref[h] * sc + sh
        p = yy * sigm(yy)
        return sums_of(h + 1, p), p[0:q] + p[q : 2 * q]

    first = halo_row(0, 0, top)
    for t in range(TASKS):
        for dx in range(3):
            prev[t, dx] = first[t][dx]

    @pl.loop(0, height // 2)
    def _(i):
        cs, pool_a = inner(2 * i)
        for t in range(TASKS):
            for dx in range(3):
                se[t, dx, i] = (prev[t, dx] + cs[t][dx]).astype(BF)
                prev[t, dx] = cs[t][dx]
        cs, pool_b = inner(2 * i + 1)
        for t in range(TASKS):
            for dx in range(3):
                so[t, dx, i] = (prev[t, dx] + cs[t][dx]).astype(BF)
                prev[t, dx] = cs[t][dx]
        pooled[i] = ((pool_a + pool_b) * 0.25).astype(BF)

    last = halo_row(height + 1, 1, bottom)
    for t in range(TASKS):
        for dx in range(3):
            se[t, dx, height // 2] = (prev[t, dx] + last[t][dx]).astype(BF)


def lane_blocks(lanes):
    def block(*lead):
        return pl.BlockSpec(lead + (lanes,), lambda c: (0,) * len(lead) + (c,))

    return block


def whole(a):
    return pl.BlockSpec(a.shape, lambda c: (0,) * a.ndim)


def attend(idx, st, gb, mst, mgb, z, rows, cols, h, hc, up, batch, count_all):
    height, tall, chans = z.shape
    lanes = BLK
    r, q, half = height + 2, tall // 2, height // 2
    block = lane_blocks(lanes)
    return pl.pallas_call(
        functools.partial(attend_kernel, batch, count_all),
        grid=(chans // lanes,),
        in_specs=[
            SM, block(2), block(2), block(2 * TASKS), block(2 * TASKS), block(height, tall), block(2, tall),
            block(r, 2 * batch), whole(h), whole(hc), block(TASKS, CA),
        ],
        out_specs=[block(TASKS, 3, half + 1, q), block(TASKS, 3, half, q), block(half, q)],
        out_shape=[
            sds((TASKS, 3, half + 1, q, chans), BF),
            sds((TASKS, 3, half, q, chans), BF),
            sds((half, q, chans), BF),
        ],
        scratch_shapes=[
            pltpu.VMEM((TASKS, r, 2 * batch, lanes), F32),
            pltpu.VMEM((TASKS, r, tall, lanes), F32),
            pltpu.VMEM((TASKS, 3, q, lanes), F32),
        ],
        compiler_params=params(),
        cost_estimate=cost(2 * r * tall * CA * chans * TASKS, 15e6, 6e6),
        name="attend",
    )(idx, st, gb, mst, mgb, z, rows, cols, h, hc, up)


def attend_back_kernel(
    batch, count_all, st, gb, mst, mgb, z_ref, h_ref, up, da, cot, dym, dy2, sums, er, ec, pre
):
    height, tall, lanes = z_ref.shape
    mean, rs, sc, sh = coef(st[...], gb[...], count_all)
    mcoef = [
        coef(mst[2 * t : 2 * t + 2], mgb[2 * t : 2 * t + 2], count_all) for t in range(TASKS)
    ]
    for t in range(TASKS):
        pre[t] = jnp.dot(
            h_ref[tall : (height + 1) * tall, t * CA : (t + 1) * CA],
            up[t],
            preferred_element_type=F32,
        ).reshape(height, tall, lanes)
    sums[...] = jnp.zeros(sums.shape, F32)

    @pl.loop(0, height)
    def _(h):
        z = z_ref[h]
        yy = z * sc + sh
        s = sigm(yy)
        p = yy * s
        shared = cot[h // 2]
        shared = jnp.concatenate([shared, shared], axis=0)
        branches = []
        for t in range(TASKS):
            mmean, _, msc, msh = mcoef[t]
            mp = pre[t, h]
            m = sigm(mp * msc + msh)
            br = m * da[t, h].astype(F32)
            branches.append(br)
            shared = shared + br
            dm = br * p * (1.0 - m)
            dym[t, h] = dm.astype(BF)
            sums[2 * t : 2 * t + 1] += jnp.sum(dm, axis=0, keepdims=True)
            sums[2 * t + 1 : 2 * t + 2] += jnp.sum(dm * (mp - mmean), axis=0, keepdims=True)
        g2 = shared * (s * (1.0 + yy * (1.0 - s)))
        dy2[h] = g2
        sums[6:7] += jnp.sum(g2, axis=0, keepdims=True)
        sums[7:8] += jnp.sum(g2 * (z - mean), axis=0, keepdims=True)
        k = 8
        for t in range(TASKS):
            for s2 in range(t, TASKS):
                sums[k : k + 1] += jnp.sum(branches[t] * branches[s2], axis=0, keepdims=True)
                k += 1

    for t in range(TASKS):
        sums[2 * t + 1 : 2 * t + 2] = sums[2 * t + 1 : 2 * t + 2] * mcoef[t][1]
    sums[7:8] = sums[7:8] * rs
    put_edges(dy2, er, ec, batch)


def attend_back(st, gb, mst, mgb, z, h, up, da, cot, batch, count_all):
    height, tall, chans = z.shape
    lanes = BLK
    block = lane_blocks(lanes)
    return pl.pallas_call(
        functools.partial(attend_back_kernel, batch, count_all),
        grid=(chans // lanes,),
        in_specs=[
            block(2), block(2), block(2 * TASKS), block(2 * TASKS), block(height, tall), whole(h),
            block(TASKS, CA), block(TASKS, height, tall), block(height // 2, tall // 2),
        ],
        out_specs=[
            block(TASKS, height, tall), block(height, tall), block(14), block(2, tall),
            block(height, 2 * batch),
        ],
        out_shape=[
            sds((TASKS, height, tall, chans), BF),
            sds((height, tall, chans), F32),
            sds((14, chans), F32),
            sds((2, tall, chans), BF),
            sds((height, 2 * batch, chans), F32),
        ],
        scratch_shapes=[pltpu.VMEM((TASKS, height, tall, lanes), F32)],
        compiler_params=params(),
        cost_estimate=cost(2 * height * tall * CA * chans * TASKS, 15e6, 4e6),
        name="attend_back",
    )(st, gb, mst, mgb, z, h, up, da, cot)


def mask_back_kernel(
    tall, count_all, mst, mgb, msum, hst, hgb, dym, h_ref, hp, up, du, dh, hs, acc
):
    step = pl.program_id(0)
    n_rows = h_ref.shape[0]

    @pl.when(step == 0)
    def _():
        acc[...] = jnp.zeros(acc.shape, F32)

    inner = pl.ds(tall, n_rows - 2 * tall)
    for t in range(TASKS):
        mean, rs, sc, _ = coef(mst[2 * t : 2 * t + 2], mgb[2 * t : 2 * t + 2], count_all)
        tot = msum[2 * t : 2 * t + 1] / count_all
        cross = msum[2 * t + 1 : 2 * t + 2] * rs / count_all
        ht = h_ref[inner, t * CA : (t + 1) * CA]
        pre = jnp.dot(ht, up[t], preferred_element_type=F32)
        dm = dym[t].reshape(pre.shape).astype(F32)
        dz = (sc * (dm - tot - (pre - mean) * cross)).astype(BF)
        du[t] = lax.dot_general(ht, dz, TN, preferred_element_type=F32)
        acc[:, t * CA : (t + 1) * CA] += lax.dot_general(dz, up[t], NT, preferred_element_type=F32)

    @pl.when(step == pl.num_programs(0) - 1)
    def _():
        mean, rs, sc, sh = coef(hst[...], hgb[...], count_all)
        hs[...] = jnp.zeros(hs.shape, F32)
        chunk = 2 * tall

        @pl.loop(0, (n_rows - 2 * tall) // chunk)
        def _(k):
            at = pl.ds(pl.multiple_of(k * chunk, chunk), chunk)
            v = hp[pl.ds(pl.multiple_of(tall + k * chunk, tall), chunk)]
            y = v * sc + sh
            s = sigm(y)
            g = acc[at] * (s * (1.0 + y * (1.0 - s)))
            dh[at] = g
            hs[0:1] += jnp.sum(g, axis=0, keepdims=True)
            hs[1:2] += jnp.sum(g * (v - mean) * rs, axis=0, keepdims=True)


def mask_back(mst, mgb, msum, hst, hgb, dym, h, hp, up, tall, count_all):
    lanes = BLK
    wide = TASKS * CA
    pixels = h.shape[0] - 2 * tall

    def two(n):
        return pl.BlockSpec((n, lanes), lambda c: (0, c))

    def whole(a):
        return pl.BlockSpec(a.shape, lambda c: (0,) * a.ndim)

    return pl.pallas_call(
        functools.partial(mask_back_kernel, tall, count_all),
        grid=(C // lanes,),
        in_specs=[
            two(2 * TASKS),
            two(2 * TASKS),
            two(2 * TASKS),
            whole(hst),
            whole(hgb),
            pl.BlockSpec(dym.shape[:3] + (lanes,), lambda c: (0, 0, 0, c)),
            whole(h),
            whole(hp),
            pl.BlockSpec((TASKS, CA, lanes), lambda c: (0, 0, c)),
        ],
        out_specs=[
            pl.BlockSpec((TASKS, CA, lanes), lambda c: (0, 0, c)),
            pl.BlockSpec((pixels, wide), lambda c: (0, 0)),
            pl.BlockSpec((2, wide), lambda c: (0, 0)),
        ],
        out_shape=[sds((TASKS, CA, C), F32), sds((pixels, wide), F32), sds((2, wide), F32)],
        scratch_shapes=[pltpu.VMEM((pixels, wide), F32)],
        compiler_params=params(),
        cost_estimate=cost(6 * pixels * C * wide, 8e6, 1e6),
        name="mask_back",
    )(mst, mgb, msum, hst, hgb, dym, h, hp, up)


def norm_back_kernel(
    batch, count_all, idx, st, gb, gs, dy, drows, dcols, z, zrows, zcols, x3, work
):
    height, tall, lanes = z.shape
    across = tall // (2 * batch)
    mean, rs, sc, _ = coef(st[...], gb[...], count_all)
    tot = gs[0:1] / count_all
    cross = gs[1:2] * rs / count_all

    def back(d, v):
        return sc * (d - tot - (v - mean) * cross)

    mask = side_mask(idx, 2 * batch, lanes, 0)
    flat = back(dcols[...].reshape(-1, lanes), zcols[...].reshape(-1, lanes))
    work[...] = flat.reshape(height + 2, 2 * batch, lanes) * mask[None]
    top, bottom = idx[3].astype(F32), idx[4].astype(F32)
    work[0] = work[0] * top
    work[height + 1] = work[height + 1] * bottom
    put_row(x3, 0, back(drows[0].astype(F32), zrows[0].astype(F32)) * top, work, batch, across)
    put_row(
        x3, height + 1, back(drows[1].astype(F32), zrows[1].astype(F32)) * bottom, work, batch, across
    )

    @pl.loop(0, height)
    def _(h):
        put_row(x3, h + 1, back(dy[h], z[h]), work, batch, across)


def norm_back(idx, st, gb, gs, dy, dhalo, z, zhalo, batch, count_all, name):
    height, tall, chans = z.shape
    lanes = BLK
    r = height + 2

    def two(n):
        return pl.BlockSpec((n, lanes), lambda c: (0, c))

    def three(a, b):
        return pl.BlockSpec((a, b, lanes), lambda c: (0, 0, c))

    field = [three(height, tall), three(2, tall), three(r, 2 * batch)]
    return pl.pallas_call(
        functools.partial(norm_back_kernel, batch, count_all),
        grid=(chans // lanes,),
        in_specs=[SM, two(2), two(2), two(2)] + field + field,
        out_specs=pl.BlockSpec((3, r, tall, lanes), lambda c: (0, 0, 0, c)),
        out_shape=sds((3, r, tall, chans), BF),
        scratch_shapes=[pltpu.VMEM((r, 2 * batch, lanes), F32)],
        compiler_params=params(),
        cost_estimate=cost(0, 10e6),
        name=name,
    )(idx, st, gb, gs, dy, *dhalo, z, *zhalo)


def first_back_kernel(
    batch, count_all, hst, hgb, hsum, st, gb, dh, hp, u3, part, z, down, dd, dy, gs, er, ec, low
):
    height, tall, lanes = z.shape

    @pl.when(pl.program_id(0) == 0)
    def _():
        mean, rs, sc, _ = coef(hst[...], hgb[...], count_all)
        tot = hsum[0:1] / count_all
        cross = hsum[1:2] * rs / count_all
        chunk = 2 * tall

        @pl.loop(0, height // 2)
        def _(k):
            at = pl.ds(pl.multiple_of(k * chunk, chunk), chunk)
            v = hp[pl.ds(pl.multiple_of(tall + k * chunk, tall), chunk)]
            low[at] = (sc * (dh[at] - tot - (v - mean) * cross)).astype(BF)

    u = u3[0, 1 : height + 1].reshape(height * tall, lanes)
    dd[...] = lax.dot_general(u, low[...], TN, preferred_element_type=F32)
    mean, rs, sc, sh = coef(st[...], gb[...], count_all)
    gs[...] = jnp.zeros(gs.shape, F32)
    rows = 4

    @pl.loop(0, height // rows)
    def _(k):
        at = pl.ds(pl.multiple_of(k * rows * tall, rows * tall), rows * tall)
        back = lax.dot_general(low[at], down[...], NT, preferred_element_type=F32)
        v = z[pl.ds(k * rows, rows)].reshape(rows * tall, lanes)
        y = v * sc + sh
        s = sigm(y)
        total = part[pl.ds(k * rows, rows)].reshape(rows * tall, lanes) + back
        g = total * (s * (1.0 + y * (1.0 - s)))
        dy[pl.ds(k * rows, rows)] = g.reshape(rows, tall, lanes)
        gs[0:1] += jnp.sum(g, axis=0, keepdims=True)
        gs[1:2] += jnp.sum(g * (v - mean) * rs, axis=0, keepdims=True)

    put_edges(dy, er, ec, batch)


def first_back(hst, hgb, hsum, st, gb, dh, hp, u3, part, z, down, batch, count_all):
    height, tall, chans = z.shape
    lanes = BLK
    wide = TASKS * CA

    def two(n):
        return pl.BlockSpec((n, lanes), lambda c: (0, c))

    def whole(a):
        return pl.BlockSpec(a.shape, lambda c: (0,) * a.ndim)

    field = pl.BlockSpec((height, tall, lanes), lambda c: (0, 0, c))
    return pl.pallas_call(
        functools.partial(first_back_kernel, batch, count_all),
        grid=(chans // lanes,),
        in_specs=[
            whole(hst),
            whole(hgb),
            whole(hsum),
            two(2),
            two(2),
            whole(dh),
            whole(hp),
            pl.BlockSpec((1, height + 2, tall, lanes), lambda c: (1, 0, 0, c)),
            field,
            field,
            pl.BlockSpec((lanes, wide), lambda c: (c, 0)),
        ],
        out_specs=[
            pl.BlockSpec((lanes, wide), lambda c: (c, 0)),
            field,
            two(2),
            pl.BlockSpec((2, tall, lanes), lambda c: (0, 0, c)),
            pl.BlockSpec((height, 2 * batch, lanes), lambda c: (0, 0, c)),
        ],
        out_shape=[
            sds((chans, wide), F32),
            sds((height, tall, chans), F32),
            sds((2, chans), F32),
            sds((2, tall, chans), BF),
            sds((height, 2 * batch, chans), F32),
        ],
        scratch_shapes=[pltpu.VMEM((height * tall, wide), BF)],
        compiler_params=params(),
        cost_estimate=cost(4 * height * tall * chans * wide, 12e6, 1e6),
        name="first_back",
    )(hst, hgb, hsum, st, gb, dh, hp, u3, part, z, down)


def flip_place(place, j):
    s = lax.bitwise_xor(place, j)
    return lax.shift_right_logical(s, 1) + 2 * lax.bitwise_and(s, 1)


def put_blocks(idx, grad, mine, other, m):
    low = grad.astype(BF)
    even = idx[2] == 0
    for i in range(NB):
        e = lax.bitwise_xor(idx[0], i)
        for j in range(NB):
            s = flip_place(idx[1], j)
            block = low[i * BLK : (i + 1) * BLK, j * BLK : (j + 1) * BLK]
            a, b = block[0:HB], block[HB:BLK]
            at = pl.ds(pl.multiple_of(m * HB, HB), HB)
            mine[e, s, at] = jnp.where(even, a, b)
            other[e, s, at] = jnp.where(even, b, a)


def put_in_order(grad, halves, m):
    low = grad.astype(BF)
    at = slice(m * HB, (m + 1) * HB)
    for i in range(NB):
        for j in range(NB):
            for h in range(2):
                row = i * BLK + h * HB
                halves[h, i * NB + j, at] = low[row : row + HB, j * BLK : (j + 1) * BLK]


def wgrad_kernel(n_extra, idx, x3, g3, *refs):
    mine, other = refs[n_extra:]
    height, tall = x3.shape[1] - 2, x3.shape[2]
    g = g3[0, 1 : height + 1].reshape(height * tall, C)

    @pl.loop(0, 3)
    def _(dy):
        for dx in range(3):
            view = x3[dx, pl.ds(dy, height)].reshape(height * tall, C)
            grad = lax.dot_general(view, g, TN, preferred_element_type=F32)
            put_blocks(idx, grad, mine, other, 3 * dy + dx)

    if n_extra:
        ddown, dup = refs[:2]
        even = idx[2] == 0
        unit = BLK // 4

        def chunk(c):
            block, r = divmod(c, 4)
            t, block = divmod(block, 2 * NB)
            kind, n = divmod(block, NB)
            if kind == 0:
                return ddown[n * BLK + r * unit : n * BLK + (r + 1) * unit, t * CA : (t + 1) * CA]
            return dup[t, r * unit : (r + 1) * unit, n * BLK : (n + 1) * BLK]

        at = pl.ds(9 * HB, PROJ_ROWS)
        for n in range(NB * NB):
            e = lax.bitwise_xor(idx[0], n // NB)
            s = flip_place(idx[1], n % NB)
            a, b = [
                jnp.concatenate([chunk(6 * n + 3 * k + c) for c in range(3)], axis=0).astype(BF)
                for k in range(2)
            ]
            mine[e, s, at] = jnp.where(even, a, b)
            other[e, s, at] = jnp.where(even, b, a)


def wgrad(idx, x3, g3, name, extra=()):
    r, tall = x3.shape[1], x3.shape[2]
    rows = 9 * HB + (PROJ_ROWS if extra else 0)
    return pl.pallas_call(
        functools.partial(wgrad_kernel, len(extra)),
        grid=(1,),
        in_specs=[
            SM,
            pl.BlockSpec(x3.shape, lambda c: (0, 0, 0, 0)),
            pl.BlockSpec((1,) + g3.shape[1:], lambda c: (1, 0, 0, 0)),
        ]
        + [VM] * len(extra),
        out_specs=[pl.BlockSpec((4, 4, rows, BLK), lambda c: (0, 0, 0, 0))] * 2,
        out_shape=[sds((4, 4, rows, BLK), BF)] * 2,
        compiler_params=params(),
        cost_estimate=cost(2 * 9 * C * C * (r - 2) * tall, 10e6),
        name=name,
    )(idx, x3, g3, *extra)


def task_wgrad_kernel(idx, se, so, go, halves):
    half, q = so.shape[2], so.shape[3]
    g = go[0, 0, 1 : half + 1].reshape(half * q, C)
    for dy in range(3):
        for dx in range(3):
            if dy == 1:
                view = so[0, dx]
            else:
                view = se[0, dx, dy // 2 : dy // 2 + half]
            grad = lax.dot_general(view.reshape(half * q, C), g, TN, preferred_element_type=F32)
            put_in_order(grad, halves, 3 * dy + dx)


def task_wgrad(idx, se, so, go):
    half, q = so.shape[2], so.shape[3]
    return pl.pallas_call(
        task_wgrad_kernel,
        grid=(TASKS,),
        in_specs=[
            SM,
            pl.BlockSpec((1,) + se.shape[1:], lambda t: (t, 0, 0, 0, 0)),
            pl.BlockSpec((1,) + so.shape[1:], lambda t: (t, 0, 0, 0, 0)),
            pl.BlockSpec((1, 1) + go.shape[2:], lambda t: (t, 1, 0, 0, 0)),
        ],
        out_specs=pl.BlockSpec((2, NB * NB, 9 * HB, BLK), lambda t: (0, 0, t, 0)),
        out_shape=sds((2, NB * NB, 9 * TASKS * HB, BLK), BF),
        compiler_params=params(),
        cost_estimate=cost(TASKS * 2 * 9 * C * C * half * q, 24e6),
        name="task_wgrad",
    )(idx, se, so, go)


def task_fwd_kernel(idx, se, so, mine, other, out, wv, sems):
    half, q = so.shape[2], so.shape[3]
    slot = task_weights(idx, (mine, other), wv, sems)
    acc = None
    for dy in range(3):
        for dx in range(3):
            if dy == 1:
                view = so[0, dx]
            else:
                view = se[0, dx, dy // 2 : dy // 2 + half]
            piece = jnp.dot(
                view.reshape(half * q, C), wv[slot, 3 * dy + dx], preferred_element_type=F32
            )
            acc = piece if acc is None else acc + piece
    out[0] = (acc * 0.25).reshape(half, q, C).astype(BF)


def task_fwd(idx, se, so, pieces):
    half, q = so.shape[2], so.shape[3]
    return pl.pallas_call(
        task_fwd_kernel,
        grid=(TASKS,),
        in_specs=[
            SM,
            pl.BlockSpec((1,) + se.shape[1:], lambda t: (t, 0, 0, 0, 0)),
            pl.BlockSpec((1,) + so.shape[1:], lambda t: (t, 0, 0, 0, 0)),
            ANY,
            ANY,
        ],
        out_specs=pl.BlockSpec((1, half, q, C), lambda t: (t, 0, 0, 0)),
        out_shape=sds((TASKS, half, q, C), BF),
        scratch_shapes=[pltpu.VMEM((2, 9, C, C), BF), pltpu.SemaphoreType.DMA((2, 32))],
        compiler_params=params(),
        cost_estimate=cost(TASKS * 2 * 9 * C * C * half * q, 20e6),
        name="task_fwd",
    )(idx, se, so, *pieces)


def shampoo_steps(grads, left, right, lroot, rroot, weight, rate):
    count = len(grads)
    low = [g.astype(BF) for g in grads]
    step = [jnp.dot(lroot(k).astype(BF), low[k], preferred_element_type=F32) for k in range(count)]
    ll = [lax.dot_general(g, g, NT, preferred_element_type=F32) for g in low]
    rr = [lax.dot_general(g, g, TN, preferred_element_type=F32) for g in low]
    step = [
        jnp.dot(step[k].astype(BF), rroot(k).astype(BF), preferred_element_type=F32)
        for k in range(count)
    ]
    keep, add = stat_decay, 1.0 - stat_decay
    return [
        (keep * left(k) + add * ll[k], keep * right(k) + add * rr[k], weight(k) - rate * step[k])
        for k in range(count)
    ]


def shampoo_kernel(n_prev, idx, mine, other, left, right, lroot, rroot, weight, *refs):
    gr, ln, rn, wn = refs[n_prev:]
    even = idx[2] == 0
    together = 3
    for first in range(0, mine.shape[0] // HB, together):
        places = range(first, first + together)
        grads = []
        for k in places:
            a, b = mine[k * HB : (k + 1) * HB], other[k * HB : (k + 1) * HB]
            grads.append(jnp.concatenate([jnp.where(even, a, b), jnp.where(even, b, a)], axis=0))
        state = [
            functools.partial(lambda ref, k: ref[0, first + k], ref)
            for ref in (left, right, lroot, rroot, weight)
        ]
        done = shampoo_steps(grads, *state, conv_rate)
        for k, g, (new_l, new_r, new_w) in zip(places, grads, done):
            gr[0, k] = g.astype(F32)
            ln[0, k], rn[0, k], wn[0, k] = new_l, new_r, new_w


def shampoo_conv(idx, mine, other, state, first, prev):
    n = mine.shape[0] // HB
    each = 9
    block = pl.BlockSpec((1, each, BLK, BLK), lambda k: (0, first // each + k, 0, 0))
    half = pl.BlockSpec((each * HB, BLK), lambda k: (k, 0))
    full = state[0].shape
    return pl.pallas_call(
        functools.partial(shampoo_kernel, len(prev)),
        grid=(n // each,),
        in_specs=[SM, half, half] + [block] * 5 + [ANY] * len(prev),
        out_specs=[block] * 4,
        out_shape=[sds(full, F32)] * 4,
        input_output_aliases={8 + k: k for k in range(len(prev))},
        compiler_params=params(),
        cost_estimate=cost(n * 8 * BLK**3, n * 9 * BLK * BLK * 4),
        name="shampoo_conv",
    )(idx, mine, other, *state, *prev)


def shampoo_proj_kernel(g, left, right, lroot, rroot, weight, ln, rn, wn):
    kinds, count = g.shape[1], g.shape[2]
    for kind in range(kinds):
        grads = [g[0, kind, k] for k in range(count)]
        state = [
            functools.partial(lambda ref, k: ref[0, kind, k], ref)
            for ref in (left, right, lroot, rroot, weight)
        ]
        done = shampoo_steps(grads, *state, proj_rate)
        for k, (new_l, new_r, new_w) in enumerate(done):
            ln[0, kind, k], rn[0, kind, k], wn[0, kind, k] = new_l, new_r, new_w


def shampoo_proj(g, left, right, lroot, rroot, weight):
    block = pl.BlockSpec((1,) + g.shape[1:], lambda t: (t, 0, 0, 0, 0))
    return pl.pallas_call(
        shampoo_proj_kernel,
        grid=g.shape[:1],
        in_specs=[block] * 6,
        out_specs=[block] * 3,
        out_shape=[sds(g.shape, F32)] * 3,
        compiler_params=params(),
        cost_estimate=cost(24 * 8 * BLK**3, 24 * 9 * BLK * BLK * 4),
        name="shampoo_proj",
    )(g, left, right, lroot, rroot, weight)


def norm_step_kernel(gs1, gsum, dhs, norm, moment, gram, grad, moment_new, norm_new):
    off_down = 2 * C
    off_up = off_down + TASKS * CA
    for row in range(2):
        k = 1 - row
        at = slice(row, row + 1)
        grad[at, 0:C] = gs1[k : k + 1]
        grad[at, C : 2 * C] = gsum[6 + k : 7 + k]
        grad[at, off_down:off_up] = dhs[k : k + 1]
        for t in range(TASKS):
            grad[at, off_up + t * C : off_up + (t + 1) * C] = gsum[2 * t + k : 2 * t + k + 1]
    g = grad[...]
    new = moment_decay * moment[...] + (1.0 - moment_decay) * g * g
    moment_new[...] = new
    norm_new[...] = norm[...] - norm_rate * g / (jnp.sqrt(new) + 1e-08)
    row = lax.broadcasted_iota(jnp.int32, (TASKS, TASKS), 0)
    col = lax.broadcasted_iota(jnp.int32, (TASKS, TASKS), 1)
    value = jnp.zeros((TASKS, TASKS), F32)
    k = 8
    for t in range(TASKS):
        for s in range(t, TASKS):
            total = jnp.sum(gsum[k : k + 1], axis=1, keepdims=True)
            hit = ((row == t) & (col == s)) | ((row == s) & (col == t))
            value = jnp.where(hit, total, value)
            k += 1
    gram[...] = value


def norm_step(gs1, gsum, dhs, norm, moment):
    like = sds(norm.shape, F32)
    return pl.pallas_call(
        norm_step_kernel,
        in_specs=[VM] * 5,
        out_specs=[VM] * 4,
        out_shape=[sds((TASKS, TASKS), F32), like, like, like],
        compiler_params=params(),
        cost_estimate=cost(0, 1e5),
        name="norm_step",
    )(gs1, gsum, dhs, norm, moment)


def to_rows(field):
    b, h, w, c = field.shape
    split = field.reshape(b, h, w // 2, 2, c)
    return jnp.transpose(split, (1, 3, 0, 2, 4)).reshape(h, w * b, c)


def from_rows(field, b):
    h, tall, c = field.shape
    split = field.reshape(h, 2, b, tall // (2 * b), c)
    return jnp.transpose(split, (2, 0, 3, 1, 4)).reshape(b, h, tall // b, c)


def pooled_rows(field):
    b, h, w, c = field.shape
    return jnp.transpose(field, (1, 0, 2, 3)).reshape(h, b * w, c)


def shards(
    images,
    cot_shared,
    cot_tasks,
    depth_mask,
    nash_weights,
    conv_weight,
    conv_left,
    conv_right,
    conv_left_root,
    conv_right_root,
    proj_weight,
    proj_left,
    proj_right,
    proj_left_root,
    proj_right_root,
    norm_params,
    norm_moment,
):
    batch, tile_h, tile_w, _ = images.shape
    half_h, half_w = tile_h // 2, tile_w // 2
    tall = batch * tile_w
    q = batch * half_w
    ha, wa = lax.axis_index("ha"), lax.axis_index("wa")
    count_all = float(
        batch * tile_h * tile_w * lax.axis_size("img") * lax.axis_size("ha") * lax.axis_size("wa")
    )
    idx = jnp.stack(
        [
            lax.axis_index("img"),
            ha,
            wa % 2,
            ha > 0,
            ha < lax.axis_size("ha") - 1,
            wa > 0,
            wa < lax.axis_size("wa") - 1,
        ]
    ).astype(jnp.int32)

    halves = conv_weight[0].reshape(conv_weight.shape[1], 2, HB, BLK)
    own = lax.dynamic_index_in_dim(halves, wa % 2, axis=1, keepdims=False).astype(BF)
    g0, g1 = Gather(own[None, 0:9]), Gather(own[None, 9:18])
    g0.near()
    g0.join()
    g0.far()
    g0.low()
    images = after(images, g0.line_low)
    rows0 = jnp.stack(row_halo(edge_row(images, 0), edge_row(images, tile_h - 1)))
    off_down = 2 * C
    off_up = off_down + TASKS * CA
    for row in range(2):
        k = 1 - row
        at = slice(row, row + 1)
        grad[at, 0:C] = gs1[k : k + 1]
        grad[at, C : 2 * C] = gsum[6 + k : 7 + k]
        grad[at, off_down:off_up] = dhs[k : k + 1]
        for t in range(TASKS):
            grad[at, off_up + t * C : off_up + (t + 1) * C] = gsum[2 * t + k : 2 * t + k + 1]
    g = grad[...]
    new = moment_decay * moment[...] + (1.0 - moment_decay) * g * g
    moment_new[...] = new
    norm_new[...] = norm[...] - norm_rate * g / (jnp.sqrt(new) + 1e-08)
    row = lax.broadcasted_iota(jnp.int32, (TASKS, TASKS), 0)
    col = lax.broadcasted_iota(jnp.int32, (TASKS, TASKS), 1)
    value = jnp.zeros((TASKS, TASKS), F32)
    k = 8
    for t in range(TASKS):
        for s in range(t, TASKS):
            total = jnp.sum(gsum[k : k + 1], axis=1, keepdims=True)
            hit = ((row == t) & (col == s)) | ((row == s) & (col == t))
            value = jnp.where(hit, total, value)
            k += 1
    gram[...] = value


def norm_step(gs1, gsum, dhs, norm, moment):
    like = sds(norm.shape, F32)
    return pl.pallas_call(
        norm_step_kernel,
        in_specs=[VM] * 5,
        out_specs=[VM] * 4,
        out_shape=[sds((TASKS, TASKS), F32), like, like, like],
        compiler_params=params(),
        cost_estimate=cost(0, 1e5),
        name="norm_step",
    )(gs1, gsum, dhs, norm, moment)


def to_rows(field):
    b, h, w, c = field.shape
    split = field.reshape(b, h, w // 2, 2, c)
    return jnp.transpose(split, (1, 3, 0, 2, 4)).reshape(h, w * b, c)


def from_rows(field, b):
    h, tall, c = field.shape
    split = field.reshape(h, 2, b, tall // (2 * b), c)
    return jnp.transpose(split, (2, 0, 3, 1, 4)).reshape(b, h, tall // b, c)


def pooled_rows(field):
    b, h, w, c = field.shape
    return jnp.transpose(field, (1, 0, 2, 3)).reshape(h, b * w, c)


def shards(
    images,
    cot_shared,
    cot_tasks,
    depth_mask,
    nash_weights,
    conv_weight,
    conv_left,
    conv_right,
    conv_left_root,
    conv_right_root,
    proj_weight,
    proj_left,
    proj_right,
    proj_left_root,
    proj_right_root,
    norm_params,
    norm_moment,
):
    batch, tile_h, tile_w, _ = images.shape
    half_h, half_w = tile_h // 2, tile_w // 2
    tall = batch * tile_w
    q = batch * half_w
    ha, wa = lax.axis_index("ha"), lax.axis_index("wa")
    count_all = float(
        batch * tile_h * tile_w * lax.axis_size("img") * lax.axis_size("ha") * lax.axis_size("wa")
    )
    idx = jnp.stack(
        [
            lax.axis_index("img"),
            ha,
            wa % 2,
            ha > 0,
            ha < lax.axis_size("ha") - 1,
            wa > 0,
            wa < lax.axis_size("wa") - 1,
        ]
    ).astype(jnp.int32)

    halves = conv_weight[0].reshape(conv_weight.shape[1], 2, HB, BLK)
    own = lax.dynamic_index_in_dim(halves, wa % 2, axis=1, keepdims=False).astype(BF)
    g0, g1 = Gather(own[None, 0:9]), Gather(own[None, 9:18])
    g0.near()
    edges = after(images, own)
    rows0 = jnp.stack(row_halo(edge_row(edges, 0), edge_row(edges, tile_h - 1)))
    g0.join(rows0)
    g0.far()
    g0.low()
    images = after(images, g0.line_low)
    off_down = 2 * C
    off_up = off_down + TASKS * CA
    gb1 = norm_params[:, 0:C]
    gb2 = norm_params[:, C : 2 * C]
    gbd = norm_params[:, off_down:off_up]
    gbu = jnp.transpose(norm_params[:, off_up:].reshape(2, TASKS, C), (1, 0, 2)).reshape(-1, C)
    proj_low = proj_weight.astype(BF)
    down = jnp.transpose(proj_low[:, 0].reshape(TASKS, C, CA), (1, 0, 2)).reshape(C, TASKS * CA)
    up = jnp.transpose(proj_low[:, 1], (0, 2, 1, 3)).reshape(TASKS, CA, C)

    image_rows = to_rows(images)
    edges = jnp.concatenate([images[:, :, 0], images[:, :, tile_w - 1]], axis=0)
    edges = jnp.transpose(edges, (1, 0, 2))
    x3 = shift_copies(idx, image_rows, rows0, halo_cols(edges, rows0, batch), batch)
    g0.high(g0.low_x, g0.low_y)
    g0.corner_a(x3)
    g1.near(g0.line_high)
    g0.corner_b(g0.high_x, g1.near_got)

    cot = pooled_rows(cot_shared.astype(F32) * 0.25)

    g1.join(g0.corner_high)
    g1.far()
    g1.low()
    w0 = g0.pieces()
    z1, s1, edges1 = conv(after(idx, g1.line_low), x3, w0, False, F32, "conv_first", batch)

    halo1 = halo(edges1, batch)
    s1 = after(s1, g1.line_high, g1.low_x, g1.low_y)
    wt_mine = lax.all_gather(after(own[18:], s1), ("img", "ha"), axis=0, tiled=False)

    cot_tasks = after(cot_tasks, z1)
    depth_pick = jnp.arange(TASKS) == 1
    scale = jnp.where(depth_pick, depth_mask.astype(F32)[..., None], 1.0) * nash_weights
    weighted = cot_tasks.astype(F32).reshape(batch, half_h, half_w, TASKS, C)
    weighted = (weighted * (scale * 0.25)[..., None]).astype(BF)
    grid = jnp.transpose(weighted, (3, 1, 0, 2, 4))
    top, bottom = row_halo(grid[:, 0:1], grid[:, half_h - 1 :])
    top = jnp.where(ha > 0, top, jnp.zeros_like(top))
    bottom = jnp.where(ha < lax.axis_size("ha") - 1, bottom, jnp.zeros_like(bottom))
    grid = jnp.concatenate([top, grid, bottom], axis=1)
    left, right = col_halo(grid[:, :, :, 0:1], grid[:, :, :, half_w - 1 :])
    grid = jnp.concatenate([left, grid, right], axis=3)
    go3 = jnp.stack([grid[:, :, :, k : k + half_w] for k in range(3)], axis=1)
    go3 = go3.reshape(TASKS, 3, half_h + 2, q, C)
    def s1_img(dep):
        g1.high(dep)
        return halo1

    s1 = after(sum_all(s1, img=s1_img), g1.high_x, g1.high_y)
    g1.corner_a(s1)
    g1.corner_b(s1)
    u3, hp, hc, hs = mid(idx, s1, gb1, z1, *halo1, down, batch, count_all)
    hs = after(hs, g1.corner_low, g1.corner_high)
    w1 = g1.pieces(hs)
    kept = {}

    def s2_ha1(dep):
        kept["z2"], kept["s2"], kept["edges2"] = conv(
            idx, after(u3, dep), w1, False, F32, "conv_second", batch
        )
        return (kept["s2"],)

    hs = sum_all(hs, ("wa", "img", "ha"), ha=s2_ha1)
    z2, s2 = kept["z2"], kept["s2"]
    halo2 = halo(kept["edges2"], batch)
    h, hcb, ms = hidden(hs, gbd, hp, hc, up, tall, count_all)

    def s3_img(dep):
        return halo2 + (go3,)

    s2m = sum_all(jnp.concatenate([s2, ms], axis=0), ("wa", "img", "ha"), img=s3_img)
    s2, ms = s2m[0:2], s2m[2:]
    se, so, pooled = attend(
        idx, s2, gb2, ms, gbu, z2, *halo2, h, hcb, up, batch, count_all
    )
    halves_t = task_wgrad(idx, se, so, go3)
    if lax.axis_size("wa") == 2:
        part_t = lax.psum_scatter(halves_t, "wa", scatter_dimension=0, tiled=True)[0]
    else:
        mine_t = lax.dynamic_index_in_dim(halves_t, wa % 2, keepdims=False)
        other_t = lax.dynamic_index_in_dim(halves_t, 1 - wa % 2, keepdims=False)
        part_t = add_low(mine_t, swap(other_t, "wa", 1))
    wt_mine = after(wt_mine, s2m)
    wt = (wt_mine, swap(wt_mine, "wa", 1))
    da = task_back(after(idx, halves_t), go3, wt)
    dym, dy2, gsum, *edges2 = attend_back(
        s2, gb2, ms, gbu, z2, h, up, da, cot, batch, count_all
    )

    grad_t = lax.psum_scatter(
        after(part_t, gsum), ("img", "ha"), scatter_dimension=0, tiled=True
    )

    dhalo2 = halo(edges2, batch)

    def run_task_fwd(dep):
        kept["task_out"] = task_fwd(after(idx, dep), se, so, wt)
        return (kept["task_out"],) + tuple(dhalo2)

    gsum = sum_all(gsum, ha=run_task_fwd)
    dup, dh, dhs = mask_back(ms, gbu, gsum[0:6], hs, gbd, dym, h, hp, up, tall, count_all)

    def run_second_back(dep):
        gs = after(gsum[6:8], dep)
        kept["z3"] = norm_back(
            idx, s2, gb2, gs, dy2, dhalo2, z2, halo2, batch, count_all, "second_back"
        )
        return (kept["z3"],)

    def run_conv_back(dep):
        kept["part"] = conv(idx, after(kept["z3"], dep), w1, True, F32, "conv_second_back")
        return (kept["part"],)

    dhs = sum_all(dhs, ha=run_second_back, img=run_conv_back)
    z3, part = kept["z3"], kept["part"]
    ddown, dy1, gs1, *edges1 = first_back(
        hs, gbd, dhs, s1, gb1, dh, hp, u3, part, z1, down, batch, count_all
    )
    dhalo1 = halo(edges1, batch)

    def run_wgrad_second(dep):
        kept["r1"] = Scatter(*wgrad(after(idx, dep), u3, z3, "wgrad_second", (ddown, dup)))
        return (kept["r1"].other,) + tuple(dhalo1)

    def run_wa(dep):
        kept["r1"].wa(dep)
        return ()

    gs1 = sum_all(gs1, ha=run_wgrad_second, img=run_wa)
    r1 = kept["r1"]
    r1.corner_sum(gs1)
    r1.corner_send()
    y3 = norm_back(
        after(idx, r1.corner), s1, gb1, gs1, dy1, dhalo1, z1, halo1, batch, count_all, "first_norm_back"
    )
    r1.high_sum(y3)
    r1.low_sum(y3)
    r1.high_send()
    r1.low_send(*r1.high)
    r0 = Scatter(*wgrad(after(idx, *r1.high, *r1.low), x3, y3, "wgrad_first"))
    state = (conv_left, conv_right, conv_left_root, conv_right_root, conv_weight)
    r0.wa(r1.high_x, r1.high_y, r1.low_x, r1.low_y)
    r0.corner_sum()
    r0.corner_send()
    r1.far_sum(r0.corner)
    r1.far_send()
    image_grad = conv(after(idx, r0.corner, r1.far), y3, w0, True, BF, "conv_first_back")
    image_grad = after(image_grad, r0.to_x, r0.to_y, r1.from_far)
    gradt = after(grad_t[0], image_grad)
    step = 2
    while step < lax.axis_size("wa"):
        gradt = add_low(gradt, swap(gradt, "wa", step))
        step *= 2
    gradt_other = swap(gradt, "wa", 1)
    r0.high_sum(image_grad)
    r0.high_send()
    r0.low_sum(*r0.high)
    r0.low_send()
    r1.near_sum(*r0.low)
    r1.near_send()
    new = shampoo_conv(after(idx, *r0.low, r1.near), gradt, gradt_other, state, 18, ())
    r0.far_sum(new[0], r0.low_x, r0.low_y, r1.from_near)
    r0.far_send()
    grad1, grad1_other = r1.finish(r0.far)
    new = shampoo_conv(
        after(idx, grad1), grad1[: 9 * HB], grad1_other[: 9 * HB], state, 9, new
    )
    r0.near_sum(new[0])
    r0.near_send()
    proj = gather_proj_line(after(grad1[9 * HB :], r0.near))
    grad0, grad0_other = r0.finish(proj)
    proj_total = gather_proj(after(proj, grad0))
    new = shampoo_conv(idx, grad0, grad0_other, state, 0, new)
    proj_left_new, proj_right_new, proj_weight_new = shampoo_proj(
        after(proj_total, new[0]), proj_left, proj_right, proj_left_root, proj_right_root, proj_weight
    )
    conv_total, conv_left_new, conv_right_new, conv_weight_new = new

    image_grad = from_rows(image_grad, batch)
    task_out = jnp.transpose(
        kept["task_out"].reshape(TASKS, half_h, batch, half_w, C), (2, 1, 3, 0, 4)
    ).reshape(batch, half_h, half_w, TASKS * C)
    shared_out = jnp.transpose(
        pooled.reshape(half_h, batch, half_w, C), (1, 0, 2, 3)
    )

    gram, norm_grad, moment_new, norm_new = norm_step(gs1, gsum, dhs, norm_params, norm_moment)
    return (
        shared_out,
        task_out,
        image_grad,
        gram,
        conv_total,
        conv_left_new,
        conv_right_new,
        conv_weight_new,
        proj_total,
        proj_left_new,
        proj_right_new,
        proj_weight_new,
        norm_grad,
        moment_new,
        norm_new,
    )


def solution(mesh):
    tile = P("img", "ha", "wa", None)
    owned = P(("img", "ha"), None, None, None)
    return jax.shard_map(
        shards,
        mesh=mesh,
        in_specs=(tile, tile, tile, P("img", "ha", "wa"), P()) + (owned,) * 5 + (P(),) * 7,
        out_specs=(tile, tile, tile, P()) + (owned,) * 4 + (P(),) * 7,
        check_vma=False,
    )
```

```python
import functools

import jax
import jax.numpy as jnp
from jax import lax
from jax.experimental import pallas as pl
from jax.experimental.pallas import tpu as pltpu
from jax.sharding import PartitionSpec as P

C = 512
CA = 128
TASKS = 3
BLK = 128
HB = 64
NB = C // BLK
PROJ_ROWS = TASKS * 2 * NB * BLK // (2 * NB * NB)

eps_norm = 1e-05
conv_rate = 0.08
proj_rate = 0.2
norm_rate = 0.1
stat_decay = 0.9
moment_decay = 0.95

BF = jnp.bfloat16
F32 = jnp.float32
VM = pl.BlockSpec(memory_space=pltpu.VMEM)
SM = pl.BlockSpec(memory_space=pltpu.SMEM)
ANY = pl.BlockSpec(memory_space=pl.ANY)
VMEM_LIMIT = 56 * 1024 * 1024
NT = (((1,), (1,)), ((), ()))
TN = (((0,), (0,)), ((), ()))


def sds(shape, dtype):
    return jax.ShapeDtypeStruct(shape, dtype)


def params(**kw):
    return pltpu.CompilerParams(vmem_limit_bytes=VMEM_LIMIT, **kw)


def cost(flops, nbytes, trans=0):
    return pl.CostEstimate(
        flops=int(flops / 16), bytes_accessed=int(nbytes / 16), transcendentals=int(trans / 16)
    )


def pairs(axis, step):
    return [(i, i ^ step) for i in range(lax.axis_size(axis))]


def swap(value, axis, step):
    return lax.ppermute(value, axis, pairs(axis, step))


def sum_all(value, axes=("wa", "ha", "img"), **fillers):
    for axis in axes:
        count = lax.axis_size(axis)
        total = value
        if count <= 4:
            for step in range(1, count):
                total = total + swap(value, axis, step)
        else:
            step = 1
            while step < count:
                total = total + swap(total, axis, step)
                step *= 2
        if axis in fillers:
            total = after(total, *fillers[axis](value))
        value = total
    return value


def row_halo(first, last):
    count = lax.axis_size("ha")
    odd = lax.axis_index("ha") % 2 == 1
    got = []
    for shift in (0, 1):
        upper = [i for i in range(count) if i % 2 == shift and i + 1 < count]
        pairing = {i: i + 1 for i in upper} | {i + 1: i for i in upper}
        send = jnp.where(odd == (shift == 1), last, first)
        got.append(lax.ppermute(send, "ha", [(i, pairing.get(i, i)) for i in range(count)]))
    return jnp.where(odd, got[0], got[1]), jnp.where(odd, got[1], got[0])


def col_halo(left_edge, right_edge):
    count = lax.axis_size("wa")
    if count == 2:
        mine = jnp.where(lax.axis_index("wa") == 0, right_edge, left_edge)
        got = swap(mine, "wa", 1)
        none = jnp.zeros_like(got)
        first = lax.axis_index("wa") == 0
        return jnp.where(first, none, got), jnp.where(first, got, none)
    up = [(i, i + 1) for i in range(count - 1)]
    down = [(i + 1, i) for i in range(count - 1)]
    return lax.ppermute(right_edge, "wa", up), lax.ppermute(left_edge, "wa", down)


def halo(edges, batch):
    edge_rows, edge_cols = edges
    top, bottom = row_halo(edge_rows[0], edge_rows[1])
    rows = jnp.stack([top, bottom])
    return rows, halo_cols(edge_cols.astype(BF), rows, batch)


def after(value, *deps):
    return lax.optimization_barrier((value,) + deps)[0]


class Gather:
    def __init__(self, own):
        self.own = own

    def near(self, *deps):
        self.near_got = swap(after(self.own, *deps), "ha", 2)
        return self.near_got

    def join(self, *deps):
        self.line_low = after(jnp.concatenate([self.own, self.near_got], axis=0), *deps)
        return self.line_low

    def far(self, *deps):
        self.line_high = swap(after(self.line_low, *deps), "ha", 1)
        return self.line_high

    def low(self, *deps):
        low = after(self.line_low, *deps)
        self.low_x, self.low_y = swap(low, "img", 1), swap(low, "img", 2)
        return self.low_x, self.low_y

    def high(self, *deps):
        high = after(self.line_high, *deps)
        self.high_x, self.high_y = swap(high, "img", 1), swap(high, "img", 2)
        return self.high_x, self.high_y

    def corner_a(self, *deps):
        self.corner_low = swap(after(self.low_x, *deps), "img", 2)
        return self.corner_low

    def corner_b(self, *deps):
        self.corner_high = swap(after(self.high_y, *deps), "img", 1)
        return self.corner_high

    def pieces(self, *deps):
        mine = (
            self.line_low, self.line_high, self.low_x, self.high_x,
            self.low_y, self.high_y, self.corner_low, self.corner_high,
        )
        return mine + tuple(swap(after(part, *deps), "wa", 1) for part in mine)


def edge_row(field, h):
    return to_rows(field[:, h : h + 1])[0]


def halo_cols(edge_cols, rows, batch):
    tall, chans = rows.shape[1:]
    across = tall // (2 * batch)
    around = rows.reshape(2, 2, batch, across, chans)

    def edge(side):
        inner = edge_cols[:, side * batch : (side + 1) * batch]
        outer = around[:, side, :, (across - 1) * side]
        return jnp.concatenate([outer[0:1], inner, outer[1:2]], axis=0)

    return jnp.concatenate(col_halo(edge(0), edge(1)), axis=1).astype(F32)


def ring_gather(value, axis):
    count = lax.axis_size(axis)
    place = lax.axis_index(axis)
    value = value[None]
    if count == 4:
        value = jnp.concatenate([value] + [swap(value, axis, step) for step in (1, 2, 3)], axis=0)
        for step in (1, 2):
            parts = value.reshape((2, 2) + value.shape[1:])
            along = 1 if step == 1 else 0
            turned = jnp.flip(parts, along)
            value = jnp.where((place // step) % 2 == 0, parts, turned).reshape(value.shape)
        return value
    step = 1
    while step < count:
        came = swap(value, axis, step)
        first = (place // step) % 2 == 0
        value = jnp.concatenate(
            [jnp.where(first, value, came), jnp.where(first, came, value)], axis=0
        )
        step *= 2
    return value


def gather_proj_core(own):
    got = swap(own, "wa", 1)
    even = lax.axis_index("wa") % 2 == 0
    return jnp.stack([jnp.where(even, own, got), jnp.where(even, got, own)])


def add_low(*parts):
    total = parts[0].astype(F32)
    for part in parts[1:]:
        total = total + part.astype(F32)
    return total.astype(BF)


class Scatter:
    def __init__(self, mine, other):
        self.mine, self.other = mine, other

    def wa(self, *deps):
        self.came = swap(after(self.other, *deps), "wa", 1)
        return self.came

    def corner_sum(self, *deps):
        self.corner = add_low(self.mine[3], after(self.came, *deps)[3])
        return self.corner

    def corner_send(self, *deps):
        corner = after(self.corner, *deps)
        self.to_x = swap(corner[0:2], "img", 1)
        self.to_y = swap(corner[2:4], "img", 2)
        return self.to_x, self.to_y

    def high_sum(self, *deps):
        came = after(self.came, *deps)
        self.high = (
            add_low(self.mine[1][2:4], came[1][2:4], self.to_y),
            add_low(self.mine[2][2:4], came[2][2:4]),
        )
        return self.high

    def high_send(self, *deps):
        self.high_x = swap(after(self.high[0], *deps), "img", 1)
        self.high_y = swap(after(self.high[1], *deps), "img", 2)
        return self.high_x, self.high_y

    def low_sum(self, *deps):
        came = after(self.came, *deps)
        self.low = (
            add_low(self.mine[1][0:2], came[1][0:2]),
            add_low(self.mine[2][0:2], came[2][0:2], self.to_x),
        )
        return self.low

    def low_send(self, *deps):
        self.low_x = swap(after(self.low[0], *deps), "img", 1)
        self.low_y = swap(after(self.low[1], *deps), "img", 2)
        return self.low_x, self.low_y

    def far_sum(self, *deps):
        came = after(self.came, *deps)
        self.far = add_low(self.mine[0][2:4], came[0][2:4], self.high_x, self.high_y)
        return self.far

    def far_send(self, *deps):
        self.from_far = swap(after(self.far, *deps), "ha", 1)
        return self.from_far

    def near_sum(self, *deps):
        came = after(self.came, *deps)
        self.near = add_low(
            self.mine[0][1], came[0][1], self.low_x[1], self.low_y[1], self.from_far[1]
        )
        return self.near

    def near_send(self, *deps):
        self.from_near = swap(after(self.near, *deps), "ha", 2)
        return self.from_near

    def finish(self, *deps):
        total = add_low(
            after(self.mine[0][0], *deps), self.came[0][0], self.low_x[0], self.low_y[0], self.from_far[0], self.from_near
        )
        step = 2
        while step < lax.axis_size("wa"):
            total = add_low(total, swap(total, "wa", step))
            step *= 2
        return total, swap(total, "wa", 1)


def coef(sums, gb, count_all):
    mean = sums[0:1] / count_all
    var = sums[1:2] / count_all - mean * mean
    rs = lax.rsqrt(var + eps_norm)
    sc = gb[0:1] * rs
    return mean, rs, sc, gb[1:2] - mean * sc


def sigm(v):
    return pl.reciprocal(1.0 + jnp.exp(-v), approx=True)


def side_mask(idx, rows, lanes, count):
    row = lax.broadcasted_iota(jnp.int32, (rows, lanes), 0)
    return jnp.where(row < rows // 2, idx[5], idx[6]).astype(F32)


def col_block(cols, r, side, batch, across):
    lanes = cols.shape[-1]
    parts = [
        jnp.broadcast_to(cols[r, pl.ds(side * batch + b, 1), :], (across, lanes))
        for b in range(batch)
    ]
    return jnp.concatenate(parts, axis=0)


def shifted(even, odd, hl, hr, batch, across):
    lanes = even.shape[-1]
    shape = (batch, across, lanes)
    j = lax.broadcasted_iota(jnp.int32, shape, 1)
    lo = jnp.where(j == 0, hl.reshape(shape), pltpu.roll(odd.reshape(shape), 1, 1))
    hi = jnp.where(j == across - 1, hr.reshape(shape), pltpu.roll(even.reshape(shape), across - 1, 1))
    return lo.reshape(even.shape), hi.reshape(even.shape)


def put_row(x3, r, row, cols, batch, across):
    q = batch * across
    even, odd = row[0:q], row[q : 2 * q]
    hl = col_block(cols, r, 0, batch, across)
    hr = col_block(cols, r, 1, batch, across)
    lo, hi = shifted(even, odd, hl, hr, batch, across)
    x3[0, r] = jnp.concatenate([lo, even], axis=0).astype(BF)
    x3[1, r] = row.astype(BF)
    x3[2, r] = jnp.concatenate([odd, hi], axis=0).astype(BF)


def flip(s):
    return s // 2 + 2 * (s % 2)


WEIGHTS = (NB * NB, 9, 2, HB, BLK)


def weight_copies_rel(idx, pieces, wv, sems):
    rows = ([], [], [])
    count = len(pieces) // 2
    for half in range(2):
        parts = pieces[half * count : (half + 1) * count]
        h = lax.bitwise_xor(idx[2], half)
        for e in range(4):
            for k in range(2):
                src = parts[2 * e + k]
                for dy, copies in enumerate(rows):
                    taps = pl.ds(3 * dy, 3)
                    copies.append(
                        pltpu.make_async_copy(
                            src.at[:, taps],
                            wv.at[pl.ds(NB * e + 2 * k, 2), taps, h],
                            sems.at[dy, len(copies)],
                        )
                    )
    return rows


def weight_copies_task(idx, pieces, first, wv, sems):
    return [
        pltpu.make_async_copy(
            pieces[half].at[:, pl.ds(first, 9)],
            wv.at[:, :, lax.bitwise_xor(idx[2], half)],
            sems.at[half],
        )
        for half in range(2)
    ]


def tap(wv, m, idx=None):
    def block(i, j):
        if idx is not None:
            i, j = lax.bitwise_xor(idx[0], i), flip_place(idx[1], j)
        return wv[NB * i + j, m].reshape(BLK, BLK)

    rows = [jnp.concatenate([block(i, j) for j in range(NB)], axis=1) for i in range(NB)]
    return jnp.concatenate(rows, axis=0)


def put_edges(field, edge_rows, edge_cols, batch):
    height, tall = field.shape[0], field.shape[1]
    across = tall // (2 * batch)
    edge_rows[0] = field[0].astype(BF)
    edge_rows[1] = field[height - 1].astype(BF)

    @pl.loop(0, height)
    def _(h):
        for side in range(2):
            for b in range(batch):
                place = side * (tall // 2 + across - 1) + b * across
                edge_cols[h, side * batch + b : side * batch + b + 1] = field[h, place : place + 1]


def shift_kernel(batch, idx, x_ref, rows_ref, cols_ref, x3_ref, work):
    height, tall = x_ref.shape[0], x_ref.shape[1]
    across = tall // (2 * batch)
    top, bottom = idx[3].astype(F32), idx[4].astype(F32)
    work[...] = cols_ref[...]
    work[0] = work[0] * top
    work[height + 1] = work[height + 1] * bottom
    cols_ref = work
    put_row(x3_ref, 0, rows_ref[0].astype(F32) * top, cols_ref, batch, across)
    put_row(x3_ref, height + 1, rows_ref[1].astype(F32) * bottom, cols_ref, batch, across)

    @pl.loop(0, height)
    def _(h):
        put_row(x3_ref, h + 1, x_ref[h].astype(F32), cols_ref, batch, across)


def shift_copies(idx, field, rows, cols, batch):
    height, tall, chans = field.shape
    lanes = BLK
    return pl.pallas_call(
        functools.partial(shift_kernel, batch),
        grid=(chans // lanes,),
        in_specs=[
            SM,
            pl.BlockSpec((height, tall, lanes), lambda c: (0, 0, c)),
            pl.BlockSpec((2, tall, lanes), lambda c: (0, 0, c)),
            pl.BlockSpec((height + 2, 2 * batch, lanes), lambda c: (0, 0, c)),
        ],
        out_specs=pl.BlockSpec((3, height + 2, tall, lanes), lambda c: (0, 0, 0, c)),
        out_shape=sds((3, height + 2, tall, chans), BF),
        scratch_shapes=[pltpu.VMEM((height + 2, 2 * batch, lanes), F32)],
        compiler_params=params(),
        cost_estimate=cost(0, 8e6),
        name="shift_copies",
    )(idx, field, rows, cols)


def conv_kernel(n_pieces, batch, transposed, want_sums, idx_ref, x_hbm, *refs):
    pieces = refs[:n_pieces]
    o_hbm = refs[n_pieces]
    s_ref, er_ref, ec_ref = refs[n_pieces + 1 : n_pieces + 4] if want_sums else (None,) * 3
    wv, x_ref, acc_ref, o_ref, w_sems, x_sems, o_sems = refs[-7:]
    height, tall = x_ref.shape[1] - 2, x_ref.shape[2]
    step = height // 2
    rows = step * tall
    cut = ((0, step + 2), (step + 2, step))
    x_copies = [
        pltpu.make_async_copy(
            x_hbm.at[:, pl.ds(first, count)], x_ref.at[:, pl.ds(first, count)], x_sems.at[k]
        )
        for k, (first, count) in enumerate(cut)
    ]
    w_copies = weight_copies_rel(idx_ref, pieces, wv, w_sems)
    order = (2, 1, 0) if transposed else (0, 1, 2)
    x_copies[0].start()
    for dy in order:
        for copy in w_copies[dy]:
            copy.start()
    x_copies[1].start()

    def part_of(part, waits):
        for n, dy in enumerate(order):
            if waits:
                for copy in w_copies[dy]:
                    copy.wait()
                if n == 0:
                    x_copies[0].wait()
            acc = None
            for dx in range(3):
                if transposed:
                    view = x_ref[2 - dx, part * step + 2 - dy : (part + 1) * step + 2 - dy]
                    dims = NT
                else:
                    view = x_ref[dx, part * step + dy : (part + 1) * step + dy]
                    dims = (((1,), (0,)), ((), ()))
                piece = lax.dot_general(
                    view.reshape(rows, C), tap(wv, 3 * dy + dx, idx_ref), dims, preferred_element_type=F32
                )
                acc = piece if acc is None else acc + piece
            if n == 0:
                acc_ref[...] = acc
            elif n == 1:
                acc_ref[...] += acc
        total = acc_ref[...] + acc
        o_ref[part * step : (part + 1) * step] = total.reshape(step, tall, C).astype(o_ref.dtype)
        out = pltpu.make_async_copy(
            o_ref.at[pl.ds(part * step, step)], o_hbm.at[pl.ds(part * step, step)], o_sems.at[part]
        )
        out.start()
        if want_sums:
            first = jnp.sum(total, axis=0, keepdims=True)
            second = jnp.sum(total * total, axis=0, keepdims=True)
            if part == 0:
                s_ref[0:1], s_ref[1:2] = first, second
            else:
                s_ref[0:1] += first
                s_ref[1:2] += second
        return out

    first = part_of(0, True)
    x_copies[1].wait()
    second = part_of(1, False)
    if want_sums:
        put_edges(o_ref, er_ref, ec_ref, batch)
    first.wait()
    second.wait()


def conv(idx, x3, pieces, transposed, dtype, name, batch=0):
    want_sums = batch > 0
    height, tall = x3.shape[1] - 2, x3.shape[2]
    out_shape = [sds((height, tall, C), dtype)]
    if want_sums:
        out_shape += [sds((2, C), F32), sds((2, tall, C), BF), sds((height, 2 * batch, C), F32)]
    out = pl.pallas_call(
        functools.partial(conv_kernel, len(pieces), batch, transposed, want_sums),
        in_specs=[SM, ANY] + [ANY] * len(pieces),
        out_specs=[ANY] + [VM] * (len(out_shape) - 1),
        out_shape=out_shape,
        scratch_shapes=[
            pltpu.VMEM(WEIGHTS, BF),
            pltpu.VMEM(x3.shape, BF),
            pltpu.VMEM((height // 2 * tall, C), F32),
            pltpu.VMEM((height, tall, C), dtype),
            pltpu.SemaphoreType.DMA((3, 16)),
            pltpu.SemaphoreType.DMA((2,)),
            pltpu.SemaphoreType.DMA((2,)),
        ],
        compiler_params=params(),
        cost_estimate=cost(2 * 9 * C * C * height * tall, 10e6),
        name=name,
    )(idx, x3, *pieces)
    return (out[0], out[1], out[2:]) if want_sums else out[0]


def mid_kernel(batch, count_all, idx, st, gb, z_ref, rows_ref, cols_ref, d_ref, u3, hp, hc, hs, uc):
    height, tall, lanes = z_ref.shape
    across = tall // (2 * batch)
    step = pl.program_id(0)
    mean, rs, sc, sh = coef(st[...], gb[...], count_all)

    def act(v):
        y = v * sc + sh
        return y * sigm(y)

    mask = side_mask(idx, 2 * batch, lanes, 0)
    flat = act(cols_ref[...].reshape(-1, lanes)).reshape(height + 2, 2 * batch, lanes)
    uc[...] = flat * mask[None]
    uc[0] = uc[0] * idx[3].astype(F32)
    uc[height + 1] = uc[height + 1] * idx[4].astype(F32)
    put_row(u3, 0, act(rows_ref[0].astype(F32)) * idx[3].astype(F32), uc, batch, across)
    put_row(u3, height + 1, act(rows_ref[1].astype(F32)) * idx[4].astype(F32), uc, batch, across)

    @pl.loop(0, height)
    def _(h):
        put_row(u3, h + 1, act(z_ref[h]), uc, batch, across)

    @pl.when(step == 0)
    def _():
        hp[...] = jnp.zeros(hp.shape, F32)
        hc[...] = jnp.zeros(hc.shape, F32)

    hc[...] += jnp.dot(
        uc[...].reshape(-1, lanes).astype(BF), d_ref[...], preferred_element_type=F32
    )
    part = (height + 2) // 2
    size = part * tall

    @pl.loop(0, 2)
    def _(k):
        hp[pl.ds(pl.multiple_of(k * size, size), size)] += jnp.dot(
            u3[1, pl.ds(k * part, part)].reshape(size, lanes),
            d_ref[...],
            preferred_element_type=F32,
        )

    @pl.when(step == pl.num_programs(0) - 1)
    def _():
        inner = hp[tall : (height + 1) * tall]
        hs[0:1] = jnp.sum(inner, axis=0, keepdims=True)
        hs[1:2] = jnp.sum(inner * inner, axis=0, keepdims=True)


def mid(idx, st, gb, z, rows, cols, down, batch, count_all):
    height, tall, chans = z.shape
    lanes = 2 * BLK
    r = height + 2
    wide = TASKS * CA
    return pl.pallas_call(
        functools.partial(mid_kernel, batch, count_all),
        grid=(chans // lanes,),
        in_specs=[
            SM,
            pl.BlockSpec((2, lanes), lambda c: (0, c)),
            pl.BlockSpec((2, lanes), lambda c: (0, c)),
            pl.BlockSpec((height, tall, lanes), lambda c: (0, 0, c)),
            pl.BlockSpec((2, tall, lanes), lambda c: (0, 0, c)),
            pl.BlockSpec((r, 2 * batch, lanes), lambda c: (0, 0, c)),
            pl.BlockSpec((lanes, wide), lambda c: (c, 0)),
        ],
        out_specs=[
            pl.BlockSpec((3, r, tall, lanes), lambda c: (0, 0, 0, c)),
            pl.BlockSpec((r * tall, wide), lambda c: (0, 0)),
            pl.BlockSpec((r * 2 * batch, wide), lambda c: (0, 0)),
            pl.BlockSpec((2, wide), lambda c: (0, 0)),
        ],
        out_shape=[
            sds((3, r, tall, chans), BF),
            sds((r * tall, wide), F32),
            sds((r * 2 * batch, wide), F32),
            sds((2, wide), F32),
        ],
        scratch_shapes=[pltpu.VMEM((r, 2 * batch, lanes), F32)],
        compiler_params=params(),
        cost_estimate=cost(2 * r * tall * chans * wide, 10e6, 2e6),
        name="mid",
    )(idx, st, gb, z, rows, cols, down)


def hidden_kernel(tall, count_all, st, gb, hp, hc, up, h_ref, hcb, ms):
    mean, rs, sc, sh = coef(st[...], gb[...], count_all)
    yc = hc[...] * sc + sh
    hcb[...] = (yc * sigm(yc)).astype(BF)
    n_rows = hp.shape[0] // tall
    ms[...] = jnp.zeros(ms.shape, F32)

    def row(r):
        at = pl.ds(pl.multiple_of(r * tall, tall), tall)
        y = hp[at] * sc + sh
        h_ref[at] = (y * sigm(y)).astype(BF)

    @pl.loop(0, n_rows)
    def _(r):
        row(r)

    chunk = 4 * tall
    for t in range(TASKS):

        @pl.loop(0, (n_rows - 2) // 4)
        def _(k):
            at = pl.ds(pl.multiple_of(tall + k * chunk, tall), chunk)
            pre = jnp.dot(h_ref[at, t * CA : (t + 1) * CA], up[t], preferred_element_type=F32)
            ms[2 * t : 2 * t + 1] += jnp.sum(pre, axis=0, keepdims=True)
            ms[2 * t + 1 : 2 * t + 2] += jnp.sum(pre * pre, axis=0, keepdims=True)


def hidden(st, gb, hp, hc, up, tall, count_all):
    return pl.pallas_call(
        functools.partial(hidden_kernel, tall, count_all),
        in_specs=[VM] * 5,
        out_specs=[VM] * 3,
        out_shape=[sds(hp.shape, BF), sds(hc.shape, BF), sds((2 * TASKS, C), F32)],
        compiler_params=params(),
        cost_estimate=cost(2 * hp.shape[0] * CA * C * TASKS, 5e6, 2e6),
        name="hidden",
    )(st, gb, hp, hc, up)


def task_weights(idx, pieces, wv, sems):
    t = pl.program_id(0)
    slot = lax.rem(t, 2)

    def copies(task, place):
        return weight_copies_task(idx, pieces, task * 9, wv.at[place], sems.at[place])

    @pl.when(t == 0)
    def _():
        for copy in copies(0, 0):
            copy.start()

    for copy in copies(t, slot):
        copy.wait()

    @pl.when(t + 1 < pl.num_programs(0))
    def _():
        for copy in copies(t + 1, 1 - slot):
            copy.start()

    return slot


def da_kernel(idx, go, mine, other, da, wv, ws, sems):
    q = go.shape[3]
    half_h = go.shape[2] - 2
    slot = task_weights(idx, (mine, other), wv, sems)

    def add(a, b):
        return (a.astype(F32) + b.astype(F32)).astype(BF)

    for a in range(2):
        for k in range(2):
            taps = []
            for dx in range(3):
                if k == 0:
                    taps.append(add(tap(wv.at[slot], 3 * a + dx), tap(wv.at[slot], 3 * (a + 1) + dx)))
                else:
                    taps.append(tap(wv.at[slot], 3 * (2 if a == 0 else 0) + dx))
            ws[a, k, 0, 0] = add(taps[0], taps[1])
            ws[a, k, 0, 1] = taps[2]
            ws[a, k, 1, 0] = add(taps[1], taps[2])
            ws[a, k, 1, 1] = taps[0]
    for a in range(2):
        for bb in range(2):
            acc = None
            for k in range(2):
                for m in range(2):
                    ro = 0 if k == 0 else (-1 if a == 0 else 1)
                    co = 0 if m == 0 else (-1 if bb == 0 else 1)
                    view = go[0, co + 1, 1 + ro : 1 + ro + half_h].reshape(half_h * q, C)
                    piece = lax.dot_general(
                        view, ws[a, k, bb, m], NT, preferred_element_type=F32
                    )
                    acc = piece if acc is None else acc + piece
            da[0, :, a, bb] = acc.reshape(half_h, q, C).astype(BF)


def task_back(idx, go, pieces):
    half_h, q = go.shape[2] - 2, go.shape[3]
    out = pl.pallas_call(
        da_kernel,
        grid=(TASKS,),
        in_specs=[SM, pl.BlockSpec((1,) + go.shape[1:], lambda t: (t, 0, 0, 0, 0)), ANY, ANY],
        out_specs=pl.BlockSpec((1, half_h, 2, 2, q, C), lambda t: (t, 0, 0, 0, 0, 0)),
        out_shape=sds((TASKS, half_h, 2, 2, q, C), BF),
        scratch_shapes=[
            pltpu.VMEM((2,) + WEIGHTS, BF),
            pltpu.VMEM((2, 2, 2, 2, C, C), BF),
            pltpu.SemaphoreType.DMA((2, 2)),
        ],
        compiler_params=params(),
        cost_estimate=cost(TASKS * 2 * 16 * C * C * half_h * q, 24e6),
        name="task_back",
    )(idx, go, *pieces)
    return out.reshape(TASKS, 2 * half_h, 2 * q, C)


def attend_kernel(
    batch, count_all, idx, st, gb, mst, mgb, z_ref, rows_ref, cols_ref, h_ref, hc_ref, up,
    se, so, pooled,
    ac, pre, prev,
):
    height, tall, lanes = z_ref.shape
    across = tall // (2 * batch)
    q = tall // 2
    _, _, sc, sh = coef(st[...], gb[...], count_all)
    mcoef = [
        coef(mst[2 * t : 2 * t + 2], mgb[2 * t : 2 * t + 2], count_all) for t in range(TASKS)
    ]
    mask = side_mask(idx, 2 * batch, lanes, 0)
    top, bottom = idx[3].astype(F32), idx[4].astype(F32)

    y = cols_ref[...].reshape(-1, lanes) * sc + sh
    pc = (y * sigm(y)).reshape(height + 2, 2 * batch, lanes) * mask[None]
    for t in range(TASKS):
        mc = jnp.dot(hc_ref[:, t * CA : (t + 1) * CA], up[t], preferred_element_type=F32)
        _, _, msc, msh = mcoef[t]
        mc = sigm(mc * msc + msh).reshape(height + 2, 2 * batch, lanes)
        ac[t] = (mc * pc).astype(BF).astype(F32)
        ac[t, 0] = ac[t, 0] * top
        ac[t, height + 1] = ac[t, height + 1] * bottom
        pre[t] = jnp.dot(
            h_ref[:, t * CA : (t + 1) * CA], up[t], preferred_element_type=F32
        ).reshape(height + 2, tall, lanes)

    def sums_of(r, p):
        out = []
        for t in range(TASKS):
            _, _, msc, msh = mcoef[t]
            a = (sigm(pre[t, r] * msc + msh) * p).astype(BF).astype(F32)
            even, odd = a[0:q], a[q : 2 * q]
            lo, hi = shifted(
                even,
                odd,
                col_block(ac.at[t], r, 0, batch, across),
                col_block(ac.at[t], r, 1, batch, across),
                batch,
                across,
            )
            out.append((lo + even, even + odd, odd + hi))
        return out

    def halo_row(r, place, scale):
        yy = rows_ref[place].astype(F32) * sc + sh
        return sums_of(r, yy * sigm(yy) * scale)

    def inner(h):
        yy = z_ref[h] * sc + sh
        p = yy * sigm(yy)
        return sums_of(h + 1, p), p[0:q] + p[q : 2 * q]

    first = halo_row(0, 0, top)
    for t in range(TASKS):
        for dx in range(3):
            prev[t, dx] = first[t][dx]

    @pl.loop(0, height // 2)
    def _(i):
        cs, pool_a = inner(2 * i)
        for t in range(TASKS):
            for dx in range(3):
                se[t, dx, i] = (prev[t, dx] + cs[t][dx]).astype(BF)
                prev[t, dx] = cs[t][dx]
        cs, pool_b = inner(2 * i + 1)
        for t in range(TASKS):
            for dx in range(3):
                so[t, dx, i] = (prev[t, dx] + cs[t][dx]).astype(BF)
                prev[t, dx] = cs[t][dx]
        pooled[i] = ((pool_a + pool_b) * 0.25).astype(BF)

    last = halo_row(height + 1, 1, bottom)
    for t in range(TASKS):
        for dx in range(3):
            se[t, dx, height // 2] = (prev[t, dx] + last[t][dx]).astype(BF)


def lane_blocks(lanes):
    def block(*lead):
        return pl.BlockSpec(lead + (lanes,), lambda c: (0,) * len(lead) + (c,))

    return block


def whole(a):
    return pl.BlockSpec(a.shape, lambda c: (0,) * a.ndim)


def attend(idx, st, gb, mst, mgb, z, rows, cols, h, hc, up, batch, count_all):
    height, tall, chans = z.shape
    lanes = BLK
    r, q, half = height + 2, tall // 2, height // 2
    block = lane_blocks(lanes)
    return pl.pallas_call(
        functools.partial(attend_kernel, batch, count_all),
        grid=(chans // lanes,),
        in_specs=[
            SM, block(2), block(2), block(2 * TASKS), block(2 * TASKS), block(height, tall), block(2, tall),
            block(r, 2 * batch), whole(h), whole(hc), block(TASKS, CA),
        ],
        out_specs=[block(TASKS, 3, half + 1, q), block(TASKS, 3, half, q), block(half, q)],
        out_shape=[
            sds((TASKS, 3, half + 1, q, chans), BF),
            sds((TASKS, 3, half, q, chans), BF),
            sds((half, q, chans), BF),
        ],
        scratch_shapes=[
            pltpu.VMEM((TASKS, r, 2 * batch, lanes), F32),
            pltpu.VMEM((TASKS, r, tall, lanes), F32),
            pltpu.VMEM((TASKS, 3, q, lanes), F32),
        ],
        compiler_params=params(),
        cost_estimate=cost(2 * r * tall * CA * chans * TASKS, 15e6, 6e6),
        name="attend",
    )(idx, st, gb, mst, mgb, z, rows, cols, h, hc, up)


def attend_back_kernel(
    batch, count_all, st, gb, mst, mgb, z_ref, h_ref, up, da, cot, dym, dy2, sums, er, ec, pre, acc
):
    height, tall, lanes = z_ref.shape
    mean, rs, sc, sh = coef(st[...], gb[...], count_all)
    mcoef = [
        coef(mst[2 * t : 2 * t + 2], mgb[2 * t : 2 * t + 2], count_all) for t in range(TASKS)
    ]
    for t in range(TASKS):
        pre[t] = jnp.dot(
            h_ref[tall : (height + 1) * tall, t * CA : (t + 1) * CA],
            up[t],
            preferred_element_type=F32,
        ).reshape(height, tall, lanes)
    acc[...] = jnp.zeros(acc.shape, F32)

    def add(k, value):
        acc[k] += jnp.sum(value.reshape(-1, 8, lanes), axis=0)

    @pl.loop(0, height)
    def _(h):
        z = z_ref[h]
        yy = z * sc + sh
        s = sigm(yy)
        p = yy * s
        shared = cot[h // 2]
        shared = jnp.concatenate([shared, shared], axis=0)
        branches = []
        for t in range(TASKS):
            mmean, _, msc, msh = mcoef[t]
            mp = pre[t, h]
            m = sigm(mp * msc + msh)
            br = m * da[t, h].astype(F32)
            branches.append(br)
            shared = shared + br
            dm = br * p * (1.0 - m)
            dym[t, h] = dm.astype(BF)
            add(2 * t, dm)
            add(2 * t + 1, dm * (mp - mmean))
        g2 = shared * (s * (1.0 + yy * (1.0 - s)))
        dy2[h] = g2
        add(6, g2)
        add(7, g2 * (z - mean))
        k = 8
        for t in range(TASKS):
            for s2 in range(t, TASKS):
                add(k, branches[t] * branches[s2])
                k += 1

    sums[...] = jnp.sum(acc[...], axis=1)
    for t in range(TASKS):
        sums[2 * t + 1 : 2 * t + 2] = sums[2 * t + 1 : 2 * t + 2] * mcoef[t][1]
    sums[7:8] = sums[7:8] * rs
    put_edges(dy2, er, ec, batch)


def attend_back(st, gb, mst, mgb, z, h, up, da, cot, batch, count_all):
    height, tall, chans = z.shape
    lanes = BLK
    block = lane_blocks(lanes)
    return pl.pallas_call(
        functools.partial(attend_back_kernel, batch, count_all),
        grid=(chans // lanes,),
        in_specs=[
            block(2), block(2), block(2 * TASKS), block(2 * TASKS), block(height, tall), whole(h),
            block(TASKS, CA), block(TASKS, height, tall), block(height // 2, tall // 2),
        ],
        out_specs=[
            block(TASKS, height, tall), block(height, tall), block(14), block(2, tall),
            block(height, 2 * batch),
        ],
        out_shape=[
            sds((TASKS, height, tall, chans), BF),
            sds((height, tall, chans), F32),
            sds((14, chans), F32),
            sds((2, tall, chans), BF),
            sds((height, 2 * batch, chans), F32),
        ],
        scratch_shapes=[
            pltpu.VMEM((TASKS, height, tall, lanes), F32),
            pltpu.VMEM((14, 8, lanes), F32),
        ],
        compiler_params=params(),
        cost_estimate=cost(2 * height * tall * CA * chans * TASKS, 15e6, 4e6),
        name="attend_back",
    )(st, gb, mst, mgb, z, h, up, da, cot)


def mask_back_kernel(
    tall, count_all, mst, mgb, msum, hst, hgb, dym, h_ref, hp, up, du, dh, hs, acc
):
    step = pl.program_id(0)
    n_rows = h_ref.shape[0]

    @pl.when(step == 0)
    def _():
        acc[...] = jnp.zeros(acc.shape, F32)

    inner = pl.ds(tall, n_rows - 2 * tall)
    for t in range(TASKS):
        mean, rs, sc, _ = coef(mst[2 * t : 2 * t + 2], mgb[2 * t : 2 * t + 2], count_all)
        tot = msum[2 * t : 2 * t + 1] / count_all
        cross = msum[2 * t + 1 : 2 * t + 2] * rs / count_all
        ht = h_ref[inner, t * CA : (t + 1) * CA]
        pre = jnp.dot(ht, up[t], preferred_element_type=F32)
        dm = dym[t].reshape(pre.shape).astype(F32)
        dz = (sc * (dm - tot - (pre - mean) * cross)).astype(BF)
        du[t] = lax.dot_general(ht, dz, TN, preferred_element_type=F32)
        acc[:, t * CA : (t + 1) * CA] += lax.dot_general(dz, up[t], NT, preferred_element_type=F32)

    @pl.when(step == pl.num_programs(0) - 1)
    def _():
        mean, rs, sc, sh = coef(hst[...], hgb[...], count_all)
        hs[...] = jnp.zeros(hs.shape, F32)
        chunk = 2 * tall

        @pl.loop(0, (n_rows - 2 * tall) // chunk)
        def _(k):
            at = pl.ds(pl.multiple_of(k * chunk, chunk), chunk)
            v = hp[pl.ds(pl.multiple_of(tall + k * chunk, tall), chunk)]
            y = v * sc + sh
            s = sigm(y)
            g = acc[at] * (s * (1.0 + y * (1.0 - s)))
            dh[at] = g
            hs[0:1] += jnp.sum(g, axis=0, keepdims=True)
            hs[1:2] += jnp.sum(g * (v - mean) * rs, axis=0, keepdims=True)


def mask_back(mst, mgb, msum, hst, hgb, dym, h, hp, up, tall, count_all):
    lanes = 2 * BLK
    wide = TASKS * CA
    pixels = h.shape[0] - 2 * tall

    def two(n):
        return pl.BlockSpec((n, lanes), lambda c: (0, c))

    def whole(a):
        return pl.BlockSpec(a.shape, lambda c: (0,) * a.ndim)

    return pl.pallas_call(
        functools.partial(mask_back_kernel, tall, count_all),
        grid=(C // lanes,),
        in_specs=[
            two(2 * TASKS),
            two(2 * TASKS),
            two(2 * TASKS),
            whole(hst),
            whole(hgb),
            pl.BlockSpec(dym.shape[:3] + (lanes,), lambda c: (0, 0, 0, c)),
            whole(h),
            whole(hp),
            pl.BlockSpec((TASKS, CA, lanes), lambda c: (0, 0, c)),
        ],
        out_specs=[
            pl.BlockSpec((TASKS, CA, lanes), lambda c: (0, 0, c)),
            pl.BlockSpec((pixels, wide), lambda c: (0, 0)),
            pl.BlockSpec((2, wide), lambda c: (0, 0)),
        ],
        out_shape=[sds((TASKS, CA, C), F32), sds((pixels, wide), F32), sds((2, wide), F32)],
        scratch_shapes=[pltpu.VMEM((pixels, wide), F32)],
        compiler_params=params(),
        cost_estimate=cost(6 * pixels * C * wide, 8e6, 1e6),
        name="mask_back",
    )(mst, mgb, msum, hst, hgb, dym, h, hp, up)


def norm_back_kernel(
    batch, count_all, idx, st, gb, gs, dy, drows, dcols, z, zrows, zcols, x3, work
):
    height, tall, lanes = z.shape
    across = tall // (2 * batch)
    mean, rs, sc, _ = coef(st[...], gb[...], count_all)
    tot = gs[0:1] / count_all
    cross = gs[1:2] * rs / count_all

    def back(d, v):
        return sc * (d - tot - (v - mean) * cross)

    mask = side_mask(idx, 2 * batch, lanes, 0)
    flat = back(dcols[...].reshape(-1, lanes), zcols[...].reshape(-1, lanes))
    work[...] = flat.reshape(height + 2, 2 * batch, lanes) * mask[None]
    top, bottom = idx[3].astype(F32), idx[4].astype(F32)
    work[0] = work[0] * top
    work[height + 1] = work[height + 1] * bottom
    put_row(x3, 0, back(drows[0].astype(F32), zrows[0].astype(F32)) * top, work, batch, across)
    put_row(
        x3, height + 1, back(drows[1].astype(F32), zrows[1].astype(F32)) * bottom, work, batch, across
    )

    @pl.loop(0, height)
    def _(h):
        put_row(x3, h + 1, back(dy[h], z[h]), work, batch, across)


def norm_back(idx, st, gb, gs, dy, dhalo, z, zhalo, batch, count_all, name):
    height, tall, chans = z.shape
    lanes = 2 * BLK
    r = height + 2

    def two(n):
        return pl.BlockSpec((n, lanes), lambda c: (0, c))

    def three(a, b):
        return pl.BlockSpec((a, b, lanes), lambda c: (0, 0, c))

    field = [three(height, tall), three(2, tall), three(r, 2 * batch)]
    return pl.pallas_call(
        functools.partial(norm_back_kernel, batch, count_all),
        grid=(chans // lanes,),
        in_specs=[SM, two(2), two(2), two(2)] + field + field,
        out_specs=pl.BlockSpec((3, r, tall, lanes), lambda c: (0, 0, 0, c)),
        out_shape=sds((3, r, tall, chans), BF),
        scratch_shapes=[pltpu.VMEM((r, 2 * batch, lanes), F32)],
        compiler_params=params(),
        cost_estimate=cost(0, 10e6),
        name=name,
    )(idx, st, gb, gs, dy, *dhalo, z, *zhalo)


def first_back_kernel(
    batch, count_all, hst, hgb, hsum, st, gb, dh, hp, u3, part, z, down, dd, dy, gs, er, ec, low
):
    height, tall, lanes = z.shape

    @pl.when(pl.program_id(0) == 0)
    def _():
        mean, rs, sc, _ = coef(hst[...], hgb[...], count_all)
        tot = hsum[0:1] / count_all
        cross = hsum[1:2] * rs / count_all
        chunk = 2 * tall

        @pl.loop(0, height // 2)
        def _(k):
            at = pl.ds(pl.multiple_of(k * chunk, chunk), chunk)
            v = hp[pl.ds(pl.multiple_of(tall + k * chunk, tall), chunk)]
            low[at] = (sc * (dh[at] - tot - (v - mean) * cross)).astype(BF)

    u = u3[0, 1 : height + 1].reshape(height * tall, lanes)
    dd[...] = lax.dot_general(u, low[...], TN, preferred_element_type=F32)
    mean, rs, sc, sh = coef(st[...], gb[...], count_all)
    gs[...] = jnp.zeros(gs.shape, F32)
    rows = 4

    @pl.loop(0, height // rows)
    def _(k):
        at = pl.ds(pl.multiple_of(k * rows * tall, rows * tall), rows * tall)
        back = lax.dot_general(low[at], down[...], NT, preferred_element_type=F32)
        v = z[pl.ds(k * rows, rows)].reshape(rows * tall, lanes)
        y = v * sc + sh
        s = sigm(y)
        total = part[pl.ds(k * rows, rows)].reshape(rows * tall, lanes) + back
        g = total * (s * (1.0 + y * (1.0 - s)))
        dy[pl.ds(k * rows, rows)] = g.reshape(rows, tall, lanes)
        gs[0:1] += jnp.sum(g, axis=0, keepdims=True)
        gs[1:2] += jnp.sum(g * (v - mean) * rs, axis=0, keepdims=True)

    put_edges(dy, er, ec, batch)


def first_back(hst, hgb, hsum, st, gb, dh, hp, u3, part, z, down, batch, count_all):
    height, tall, chans = z.shape
    lanes = 2 * BLK
    wide = TASKS * CA

    def two(n):
        return pl.BlockSpec((n, lanes), lambda c: (0, c))

    def whole(a):
        return pl.BlockSpec(a.shape, lambda c: (0,) * a.ndim)

    field = pl.BlockSpec((height, tall, lanes), lambda c: (0, 0, c))
    return pl.pallas_call(
        functools.partial(first_back_kernel, batch, count_all),
        grid=(chans // lanes,),
        in_specs=[
            whole(hst),
            whole(hgb),
            whole(hsum),
            two(2),
            two(2),
            whole(dh),
            whole(hp),
            pl.BlockSpec((1, height + 2, tall, lanes), lambda c: (1, 0, 0, c)),
            field,
            field,
            pl.BlockSpec((lanes, wide), lambda c: (c, 0)),
        ],
        out_specs=[
            pl.BlockSpec((lanes, wide), lambda c: (c, 0)),
            field,
            two(2),
            pl.BlockSpec((2, tall, lanes), lambda c: (0, 0, c)),
            pl.BlockSpec((height, 2 * batch, lanes), lambda c: (0, 0, c)),
        ],
        out_shape=[
            sds((chans, wide), F32),
            sds((height, tall, chans), F32),
            sds((2, chans), F32),
            sds((2, tall, chans), BF),
            sds((height, 2 * batch, chans), F32),
        ],
        scratch_shapes=[pltpu.VMEM((height * tall, wide), BF)],
        compiler_params=params(),
        cost_estimate=cost(4 * height * tall * chans * wide, 12e6, 1e6),
        name="first_back",
    )(hst, hgb, hsum, st, gb, dh, hp, u3, part, z, down)


def flip_place(place, j):
    s = lax.bitwise_xor(place, j)
    return lax.shift_right_logical(s, 1) + 2 * lax.bitwise_and(s, 1)


def put_blocks(idx, grad, mine, other, m):
    low = grad.astype(BF)
    even = idx[2] == 0
    for i in range(NB):
        e = lax.bitwise_xor(idx[0], i)
        for j in range(NB):
            s = flip_place(idx[1], j)
            block = low[i * BLK : (i + 1) * BLK, j * BLK : (j + 1) * BLK]
            a, b = block[0:HB], block[HB:BLK]
            at = pl.ds(pl.multiple_of(m * HB, HB), HB)
            mine[e, s, at] = jnp.where(even, a, b)
            other[e, s, at] = jnp.where(even, b, a)


def put_in_order(grad, halves, m):
    low = grad.astype(BF)
    at = slice(m * HB, (m + 1) * HB)
    for i in range(NB):
        for j in range(NB):
            for h in range(2):
                row = i * BLK + h * HB
                halves[h, i * NB + j, at] = low[row : row + HB, j * BLK : (j + 1) * BLK]


def wgrad_kernel(n_extra, idx, x_hbm, g_hbm, *refs):
    mine_hbm, other_hbm, x3, g3, mine, other, sems, o_sems = refs[n_extra:]
    height, tall = x3.shape[1] - 2, x3.shape[2]
    g_copy = pltpu.make_async_copy(g_hbm.at[1, pl.ds(1, height)], g3, sems.at[3])
    x_copies = [pltpu.make_async_copy(x_hbm.at[k], x3.at[k], sems.at[k]) for k in range(3)]
    g_copy.start()
    for copy in x_copies:
        copy.start()
    g_copy.wait()
    outs = []

    def send(first, count):
        at = pl.ds(first, count)
        for k, (source, target) in enumerate(((mine, mine_hbm), (other, other_hbm))):
            copy = pltpu.make_async_copy(
                source.at[:, :, at], target.at[:, :, at], o_sems.at[len(outs)]
            )
            copy.start()
            outs.append(copy)

    g = g3[...].reshape(height * tall, C)
    for dx in range(3):
        x_copies[dx].wait()
        for dy in range(3):
            view = x3[dx, dy : dy + height].reshape(height * tall, C)
            grad = lax.dot_general(view, g, TN, preferred_element_type=F32)
            put_blocks(idx, grad, mine, other, 3 * dy + dx)
            send((3 * dy + dx) * HB, HB)

    if n_extra:
        ddown, dup = refs[:2]
        even = idx[2] == 0
        unit = BLK // 4

        def chunk(c):
            block, r = divmod(c, 4)
            t, block = divmod(block, 2 * NB)
            kind, n = divmod(block, NB)
            if kind == 0:
                return ddown[n * BLK + r * unit : n * BLK + (r + 1) * unit, t * CA : (t + 1) * CA]
            return dup[t, r * unit : (r + 1) * unit, n * BLK : (n + 1) * BLK]

        at = pl.ds(9 * HB, PROJ_ROWS)
        for n in range(NB * NB):
            e = lax.bitwise_xor(idx[0], n // NB)
            s = flip_place(idx[1], n % NB)
            a, b = [
                jnp.concatenate([chunk(6 * n + 3 * k + c) for c in range(3)], axis=0).astype(BF)
                for k in range(2)
            ]
            mine[e, s, at] = jnp.where(even, a, b)
            other[e, s, at] = jnp.where(even, b, a)
        send(9 * HB, PROJ_ROWS)

    for copy in outs:
        copy.wait()


def wgrad(idx, x3, g3, name, extra=()):
    r, tall = x3.shape[1], x3.shape[2]
    rows = 9 * HB + (PROJ_ROWS if extra else 0)
    blocks = (4, 4, rows, BLK)
    return pl.pallas_call(
        functools.partial(wgrad_kernel, len(extra)),
        in_specs=[SM, ANY, ANY] + [VM] * len(extra),
        out_specs=[ANY, ANY],
        out_shape=[sds(blocks, BF)] * 2,
        scratch_shapes=[
            pltpu.VMEM(x3.shape, BF),
            pltpu.VMEM((r - 2, tall, C), BF),
            pltpu.VMEM(blocks, BF),
            pltpu.VMEM(blocks, BF),
            pltpu.SemaphoreType.DMA((4,)),
            pltpu.SemaphoreType.DMA((20,)),
        ],
        compiler_params=params(),
        cost_estimate=cost(2 * 9 * C * C * (r - 2) * tall, 10e6),
        name=name,
    )(idx, x3, g3, *extra)


def task_wgrad_kernel(idx, se, so, go, halves):
    half, q = so.shape[2], so.shape[3]
    g = go[0, 0, 1 : half + 1].reshape(half * q, C)
    for dy in range(3):
        for dx in range(3):
            if dy == 1:
                view = so[0, dx]
            else:
                view = se[0, dx, dy // 2 : dy // 2 + half]
            grad = lax.dot_general(view.reshape(half * q, C), g, TN, preferred_element_type=F32)
            put_in_order(grad, halves, 3 * dy + dx)


def task_wgrad(idx, se, so, go):
    half, q = so.shape[2], so.shape[3]
    return pl.pallas_call(
        task_wgrad_kernel,
        grid=(TASKS,),
        in_specs=[
            SM,
            pl.BlockSpec((1,) + se.shape[1:], lambda t: (t, 0, 0, 0, 0)),
            pl.BlockSpec((1,) + so.shape[1:], lambda t: (t, 0, 0, 0, 0)),
            pl.BlockSpec((1, 1) + go.shape[2:], lambda t: (t, 1, 0, 0, 0)),
        ],
        out_specs=pl.BlockSpec((2, NB * NB, 9 * HB, BLK), lambda t: (0, 0, t, 0)),
        out_shape=sds((2, NB * NB, 9 * TASKS * HB, BLK), BF),
        compiler_params=params(),
        cost_estimate=cost(TASKS * 2 * 9 * C * C * half * q, 24e6),
        name="task_wgrad",
    )(idx, se, so, go)


def task_fwd_kernel(idx, se, so, mine, other, out, wv, sems):
    half, q = so.shape[2], so.shape[3]
    slot = task_weights(idx, (mine, other), wv, sems)
    acc = None
    for dy in range(3):
        for dx in range(3):
            if dy == 1:
                view = so[0, dx]
            else:
                view = se[0, dx, dy // 2 : dy // 2 + half]
            piece = jnp.dot(
                view.reshape(half * q, C), tap(wv.at[slot], 3 * dy + dx), preferred_element_type=F32
            )
            acc = piece if acc is None else acc + piece
    out[0] = (acc * 0.25).reshape(half, q, C).astype(BF)


def task_fwd(idx, se, so, pieces):
    half, q = so.shape[2], so.shape[3]
    return pl.pallas_call(
        task_fwd_kernel,
        grid=(TASKS,),
        in_specs=[
            SM,
            pl.BlockSpec((1,) + se.shape[1:], lambda t: (t, 0, 0, 0, 0)),
            pl.BlockSpec((1,) + so.shape[1:], lambda t: (t, 0, 0, 0, 0)),
            ANY,
            ANY,
        ],
        out_specs=pl.BlockSpec((1, half, q, C), lambda t: (t, 0, 0, 0)),
        out_shape=sds((TASKS, half, q, C), BF),
        scratch_shapes=[pltpu.VMEM((2,) + WEIGHTS, BF), pltpu.SemaphoreType.DMA((2, 2))],
        compiler_params=params(),
        cost_estimate=cost(TASKS * 2 * 9 * C * C * half * q, 20e6),
        name="task_fwd",
    )(idx, se, so, *pieces)


def shampoo_steps(grads, left, right, lroot, rroot, weight, rate):
    count = len(grads)
    low = [g.astype(BF) for g in grads]
    step = [jnp.dot(lroot(k).astype(BF), low[k], preferred_element_type=F32) for k in range(count)]
    ll = [lax.dot_general(g, g, NT, preferred_element_type=F32) for g in low]
    rr = [lax.dot_general(g, g, TN, preferred_element_type=F32) for g in low]
    step = [
        jnp.dot(step[k].astype(BF), rroot(k).astype(BF), preferred_element_type=F32)
        for k in range(count)
    ]
    keep, add = stat_decay, 1.0 - stat_decay
    return [
        (keep * left(k) + add * ll[k], keep * right(k) + add * rr[k], weight(k) - rate * step[k])
        for k in range(count)
    ]


def shampoo_kernel(n_prev, idx, mine, other, left, right, lroot, rroot, weight, *refs):
    gr, ln, rn, wn = refs[n_prev:]
    even = idx[2] == 0
    together = 3
    for first in range(0, mine.shape[0] // HB, together):
        places = range(first, first + together)
        grads = []
        for k in places:
            a, b = mine[k * HB : (k + 1) * HB], other[k * HB : (k + 1) * HB]
            grads.append(jnp.concatenate([jnp.where(even, a, b), jnp.where(even, b, a)], axis=0))
        state = [
            functools.partial(lambda ref, k: ref[0, first + k], ref)
            for ref in (left, right, lroot, rroot, weight)
        ]
        done = shampoo_steps(grads, *state, conv_rate)
        for k, g, (new_l, new_r, new_w) in zip(places, grads, done):
            gr[0, k] = g.astype(F32)
            ln[0, k], rn[0, k], wn[0, k] = new_l, new_r, new_w


def shampoo_conv(idx, mine, other, state, first, prev, begin=0, n=9):
    each = 9
    block = pl.BlockSpec((1, each, BLK, BLK), lambda k: (0, (first + begin) // each + k, 0, 0))
    half = pl.BlockSpec((each * HB, BLK), lambda k: (begin // each + k, 0))
    full = state[0].shape
    return pl.pallas_call(
        functools.partial(shampoo_kernel, len(prev)),
        grid=(n // each,),
        in_specs=[SM, half, half] + [block] * 5 + [ANY] * len(prev),
        out_specs=[block] * 4,
        out_shape=[sds(full, F32)] * 4,
        input_output_aliases={8 + k: k for k in range(len(prev))},
        compiler_params=params(),
        cost_estimate=cost(n * 8 * BLK**3, n * 9 * BLK * BLK * 4),
        name="shampoo_conv",
    )(idx, mine, other, *state, *prev)


def shampoo_proj_kernel(g, left, right, lroot, rroot, weight, gr, ln, rn, wn):
    gr[...] = g[...].astype(F32)
    kinds, count = g.shape[1], g.shape[2]
    for kind in range(kinds):
        grads = [g[0, kind, k] for k in range(count)]
        state = [
            functools.partial(lambda ref, k: ref[0, kind, k], ref)
            for ref in (left, right, lroot, rroot, weight)
        ]
        done = shampoo_steps(grads, *state, proj_rate)
        for k, (new_l, new_r, new_w) in enumerate(done):
            ln[0, kind, k], rn[0, kind, k], wn[0, kind, k] = new_l, new_r, new_w


def shampoo_proj(g, left, right, lroot, rroot, weight):
    block = pl.BlockSpec((1,) + g.shape[1:], lambda t: (t, 0, 0, 0, 0))
    return pl.pallas_call(
        shampoo_proj_kernel,
        grid=g.shape[:1],
        in_specs=[block] * 6,
        out_specs=[block] * 4,
        out_shape=[sds(g.shape, F32)] * 4,
        compiler_params=params(),
        cost_estimate=cost(24 * 8 * BLK**3, 24 * 9 * BLK * BLK * 4),
        name="shampoo_proj",
    )(g, left, right, lroot, rroot, weight)


def norm_step_kernel(gs1, gsum, dhs, norm, moment, gram, grad, moment_new, norm_new):
    off_down = 2 * C
    off_up = off_down + TASKS * CA
    for row in range(2):
        k = 1 - row
        at = slice(row, row + 1)
        grad[at, 0:C] = gs1[k : k + 1]
        grad[at, C : 2 * C] = gsum[6 + k : 7 + k]
        grad[at, off_down:off_up] = dhs[k : k + 1]
        for t in range(TASKS):
            grad[at, off_up + t * C : off_up + (t + 1) * C] = gsum[2 * t + k : 2 * t + k + 1]
    g = grad[...]
    new = moment_decay * moment[...] + (1.0 - moment_decay) * g * g
    moment_new[...] = new
    norm_new[...] = norm[...] - norm_rate * g / (jnp.sqrt(new) + 1e-08)
    row = lax.broadcasted_iota(jnp.int32, (TASKS, TASKS), 0)
    col = lax.broadcasted_iota(jnp.int32, (TASKS, TASKS), 1)
    value = jnp.zeros((TASKS, TASKS), F32)
    k = 8
    for t in range(TASKS):
        for s in range(t, TASKS):
            total = jnp.sum(gsum[k : k + 1], axis=1, keepdims=True)
            hit = ((row == t) & (col == s)) | ((row == s) & (col == t))
            value = jnp.where(hit, total, value)
            k += 1
    gram[...] = value


def norm_step(gs1, gsum, dhs, norm, moment):
    like = sds(norm.shape, F32)
    return pl.pallas_call(
        norm_step_kernel,
        in_specs=[VM] * 5,
        out_specs=[VM] * 4,
        out_shape=[sds((TASKS, TASKS), F32), like, like, like],
        compiler_params=params(),
        cost_estimate=cost(0, 1e5),
        name="norm_step",
    )(gs1, gsum, dhs, norm, moment)


def to_rows(field):
    b, h, w, c = field.shape
    split = field.reshape(b, h, w // 2, 2, c)
    return jnp.transpose(split, (1, 3, 0, 2, 4)).reshape(h, w * b, c)


def from_rows(field, b):
    h, tall, c = field.shape
    split = field.reshape(h, 2, b, tall // (2 * b), c)
    return jnp.transpose(split, (2, 0, 3, 1, 4)).reshape(b, h, tall // b, c)


def pooled_rows(field):
    b, h, w, c = field.shape
    return jnp.transpose(field, (1, 0, 2, 3)).reshape(h, b * w, c)


def shards(
    images,
    cot_shared,
    cot_tasks,
    depth_mask,
    nash_weights,
    conv_weight,
    conv_left,
    conv_right,
    conv_left_root,
    conv_right_root,
    proj_weight,
    proj_left,
    proj_right,
    proj_left_root,
    proj_right_root,
    norm_params,
    norm_moment,
):
    batch, tile_h, tile_w, _ = images.shape
    half_h, half_w = tile_h // 2, tile_w // 2
    tall = batch * tile_w
    q = batch * half_w
    ha, wa = lax.axis_index("ha"), lax.axis_index("wa")
    count_all = float(
        batch * tile_h * tile_w * lax.axis_size("img") * lax.axis_size("ha") * lax.axis_size("wa")
    )
    idx = jnp.stack(
        [
            lax.axis_index("img"),
            ha,
            wa % 2,
            ha > 0,
            ha < lax.axis_size("ha") - 1,
            wa > 0,
            wa < lax.axis_size("wa") - 1,
        ]
    ).astype(jnp.int32)

    halves = conv_weight[0].reshape(conv_weight.shape[1], 2, HB, BLK)
    own = lax.dynamic_index_in_dim(halves, wa % 2, axis=1, keepdims=False).astype(BF)
    g0, g1 = Gather(own[None, 0:9]), Gather(own[None, 9:18])
    g0.near()
    rows0 = jnp.stack(row_halo(edge_row(images, 0), edge_row(images, tile_h - 1)))
    g0.join(rows0)
    g0.far()
    g0.low()
    images = after(images, g0.line_low)
    off_down = 2 * C
    off_up = off_down + TASKS * CA
    gb1 = norm_params[:, 0:C]
    gb2 = norm_params[:, C : 2 * C]
    gbd = norm_params[:, off_down:off_up]
    gbu = jnp.transpose(norm_params[:, off_up:].reshape(2, TASKS, C), (1, 0, 2)).reshape(-1, C)
    proj_low = proj_weight.astype(BF)
    down = jnp.transpose(proj_low[:, 0].reshape(TASKS, C, CA), (1, 0, 2)).reshape(C, TASKS * CA)
    up = jnp.transpose(proj_low[:, 1], (0, 2, 1, 3)).reshape(TASKS, CA, C)

    image_rows = to_rows(images)
    edges = jnp.concatenate([images[:, :, 0], images[:, :, tile_w - 1]], axis=0)
    edges = jnp.transpose(edges, (1, 0, 2))
    x3 = shift_copies(idx, image_rows, rows0, halo_cols(edges, rows0, batch), batch)
    g0.high(g0.low_x, g0.low_y)
    g0.corner_a(x3)
    g1.near(g0.line_high)
    g0.corner_b(g0.high_x, g1.near_got)

    cot = pooled_rows(cot_shared.astype(F32) * 0.25)

    g1.join(g0.corner_high)
    g1.far()
    g1.low()
    w0 = g0.pieces()
    z1, s1, edges1 = conv(after(idx, g1.line_low), x3, w0, False, F32, "conv_first", batch)

    halo1 = halo(edges1, batch)
    s1 = after(s1, g1.line_high, g1.low_x, g1.low_y)
    wt_mine = lax.all_gather(after(own[18:], s1), ("img", "ha"), axis=0, tiled=False)
    g1.high(s1)

    cot_tasks = after(cot_tasks, z1)
    depth_pick = jnp.arange(TASKS) == 1
    scale = jnp.where(depth_pick, depth_mask.astype(F32)[..., None], 1.0) * nash_weights
    weighted = cot_tasks.astype(F32).reshape(batch, half_h, half_w, TASKS, C)
    weighted = (weighted * (scale * 0.25)[..., None]).astype(BF)
    grid = jnp.transpose(weighted, (3, 1, 0, 2, 4))
    top, bottom = row_halo(grid[:, 0:1], grid[:, half_h - 1 :])
    top = jnp.where(ha > 0, top, jnp.zeros_like(top))
    bottom = jnp.where(ha < lax.axis_size("ha") - 1, bottom, jnp.zeros_like(bottom))
    grid = jnp.concatenate([top, grid, bottom], axis=1)
    left, right = col_halo(grid[:, :, :, 0:1], grid[:, :, :, half_w - 1 :])
    grid = jnp.concatenate([left, grid, right], axis=3)
    go3 = jnp.stack([grid[:, :, :, k : k + half_w] for k in range(3)], axis=1)
    go3 = go3.reshape(TASKS, 3, half_h + 2, q, C)
    def s1_ha(dep):
        return halo1

    def s1_img(dep):
        g1.corner_a(dep, g1.high_x, g1.high_y)
        g1.corner_b(dep, g1.high_x, g1.high_y)
        return g1.high_x, g1.high_y

    s1 = sum_all(s1, ha=s1_ha, img=s1_img)
    w1 = g1.pieces(s1)
    u3, hp, hc, hs = mid(
        after(idx, *w1[8:14]), s1, gb1, z1, *halo1, down, batch, count_all
    )
    corners = tuple(swap(after(part, hs), "wa", 1) for part in w1[6:8])
    w1 = w1[:14] + corners
    hs = after(hs, *corners)
    kept = {}

    def s2_img(dep):
        kept["z2"], kept["s2"], kept["edges2"] = conv(
            idx, after(u3, dep), w1, False, F32, "conv_second", batch
        )
        return (kept["s2"],)

    hs = sum_all(hs, ("wa", "img", "ha"), img=s2_img)
    z2, s2 = kept["z2"], kept["s2"]
    halo2 = halo(kept["edges2"], batch)
    h, hcb, ms = hidden(hs, gbd, hp, hc, up, tall, count_all)

    def s3_img(dep):
        return halo2 + (go3,)

    s2m = sum_all(jnp.concatenate([s2, ms], axis=0), ("wa", "img", "ha"), img=s3_img)
    s2, ms = s2m[0:2], s2m[2:]
    se, so, pooled = attend(
        idx, s2, gb2, ms, gbu, z2, *halo2, h, hcb, up, batch, count_all
    )
    wt_mine = after(wt_mine, s2m)
    wt = (wt_mine, swap(wt_mine, "wa", 1))
    halves_t = task_wgrad(after(idx, wt[1]), se, so, go3)
    if lax.axis_size("wa") == 2:
        part_t = lax.psum_scatter(halves_t, "wa", scatter_dimension=0, tiled=True)[0]
    else:
        mine_t = lax.dynamic_index_in_dim(halves_t, wa % 2, keepdims=False)
        other_t = lax.dynamic_index_in_dim(halves_t, 1 - wa % 2, keepdims=False)
        part_t = add_low(mine_t, swap(other_t, "wa", 1))
    da = task_back(after(idx, halves_t), go3, wt)
    dym, dy2, gsum, *edges2 = attend_back(
        s2, gb2, ms, gbu, z2, h, up, da, cot, batch, count_all
    )

    grad_t = lax.psum_scatter(
        after(part_t, gsum), ("img", "ha"), scatter_dimension=0, tiled=True
    )

    dhalo2 = halo(edges2, batch)

    def run_task_fwd(dep):
        kept["task_out"] = task_fwd(after(idx, dep), se, so, wt)
        return (kept["task_out"],) + tuple(dhalo2)

    gsum = sum_all(gsum, ha=run_task_fwd)
    dup, dh, dhs = mask_back(ms, gbu, gsum[0:6], hs, gbd, dym, h, hp, up, tall, count_all)

    def run_second_back(dep):
        gs = after(gsum[6:8], dep)
        kept["z3"] = norm_back(
            idx, s2, gb2, gs, dy2, dhalo2, z2, halo2, batch, count_all, "second_back"
        )
        return (kept["z3"],)

    def run_conv_back(dep):
        kept["part"] = conv(idx, after(kept["z3"], dep), w1, True, F32, "conv_second_back")
        return (kept["part"],)

    dhs = sum_all(dhs, ha=run_second_back, img=run_conv_back)
    z3, part = kept["z3"], kept["part"]
    ddown, dy1, gs1, *edges1 = first_back(
        hs, gbd, dhs, s1, gb1, dh, hp, u3, part, z1, down, batch, count_all
    )
    dhalo1 = halo(edges1, batch)

    def run_wgrad_second(dep):
        kept["r1"] = Scatter(*wgrad(after(idx, dep), u3, z3, "wgrad_second", (ddown, dup)))
        return (kept["r1"].other,) + tuple(dhalo1)

    def run_wa(dep):
        kept["r1"].wa(dep)
        return ()

    gs1 = sum_all(gs1, ha=run_wgrad_second, img=run_wa)
    r1 = kept["r1"]
    r1.corner_sum(gs1)
    r1.corner_send()
    y3 = norm_back(
        after(idx, r1.corner), s1, gb1, gs1, dy1, dhalo1, z1, halo1, batch, count_all, "first_norm_back"
    )
    r0 = Scatter(*wgrad(idx, x3, y3, "wgrad_first"))
    state = (conv_left, conv_right, conv_left_root, conv_right_root, conv_weight)
    r0.wa(r1.to_x, r1.to_y)
    r1.high_sum(r0.mine)
    r1.high_send()
    r1.low_sum(*r1.high)
    r1.low_send()
    r0.corner_sum(*r1.low)
    r0.corner_send(r1.high_x, r1.high_y)
    r1.far_sum(r0.corner)
    r1.far_send()
    image_grad = conv(after(idx, r0.corner, r1.far), y3, w0, True, BF, "conv_first_back")
    image_grad = after(image_grad, r0.to_x, r0.to_y, r1.from_far)
    r1.near_sum(image_grad)
    r1.near_send()
    r0.high_sum(r1.near)
    r0.high_send()
    r0.low_sum(*r0.high)
    r0.low_send()
    r0.far_sum(*r0.low)
    r0.far_send()
    grad1, grad1_other = r1.finish(r0.far)
    gradt = after(grad_t[0], grad1)
    step = 2
    while step < lax.axis_size("wa"):
        gradt = add_low(gradt, swap(gradt, "wa", step))
        step *= 2
    gradt_other = swap(gradt, "wa", 1)
    new = shampoo_conv(after(idx, grad1), gradt, gradt_other, state, 18, (), 0)
    r0.near_sum(new[0])
    r0.near_send()
    proj = ring_gather(gather_proj_core(after(grad1[9 * HB :], r0.near)), "ha")
    new = shampoo_conv(after(idx, r0.near), gradt, gradt_other, state, 18, new, 9)
    grad0, grad0_other = r0.finish(new[0])
    proj_total = ring_gather(after(proj, grad0), "img")
    new = shampoo_conv(after(idx, grad0, proj), gradt, gradt_other, state, 18, new, 18)
    new = shampoo_conv(
        after(idx, new[0]), grad1[: 9 * HB], grad1_other[: 9 * HB], state, 9, new
    )
    new = shampoo_conv(idx, grad0, grad0_other, state, 0, new)
    proj_total = after(proj_total, new[0]).reshape(TASKS, 2, NB, BLK, BLK)
    proj_total, proj_left_new, proj_right_new, proj_weight_new = shampoo_proj(
        proj_total, proj_left, proj_right, proj_left_root, proj_right_root, proj_weight
    )
    conv_total, conv_left_new, conv_right_new, conv_weight_new = new

    image_grad = from_rows(image_grad, batch)
    task_out = jnp.transpose(
        kept["task_out"].reshape(TASKS, half_h, batch, half_w, C), (2, 1, 3, 0, 4)
    ).reshape(batch, half_h, half_w, TASKS * C)
    shared_out = jnp.transpose(
        pooled.reshape(half_h, batch, half_w, C), (1, 0, 2, 3)
    )

    gram, norm_grad, moment_new, norm_new = norm_step(gs1, gsum, dhs, norm_params, norm_moment)
    return (
        shared_out,
        task_out,
        image_grad,
        gram,
        conv_total,
        conv_left_new,
        conv_right_new,
        conv_weight_new,
        proj_total,
        proj_left_new,
        proj_right_new,
        proj_weight_new,
        norm_grad,
        moment_new,
        norm_new,
    )


def solution(mesh):
    tile = P("img", "ha", "wa", None)
    owned = P(("img", "ha"), None, None, None)
    return jax.shard_map(
        shards,
        mesh=mesh,
        in_specs=(tile, tile, tile, P("img", "ha", "wa"), P()) + (owned,) * 5 + (P(),) * 7,
        out_specs=(tile, tile, tile, P()) + (owned,) * 4 + (P(),) * 7,
        check_vma=False,
    )
```

```python
import functools

import jax
import jax.numpy as jnp
from jax import lax
from jax.experimental import pallas as pl
from jax.experimental.pallas import tpu as pltpu
from jax.sharding import PartitionSpec as P

C = 512
CA = 128
TASKS = 3
BLK = 128
HB = 64
NB = C // BLK
PROJ_ROWS = TASKS * 2 * NB * BLK // (2 * NB * NB)

eps_norm = 1e-05
conv_rate = 0.08
proj_rate = 0.2
norm_rate = 0.1
stat_decay = 0.9
moment_decay = 0.95

BF = jnp.bfloat16
F32 = jnp.float32
VM = pl.BlockSpec(memory_space=pltpu.VMEM)
SM = pl.BlockSpec(memory_space=pltpu.SMEM)
ANY = pl.BlockSpec(memory_space=pl.ANY)
VMEM_LIMIT = 56 * 1024 * 1024
NT = (((1,), (1,)), ((), ()))
TN = (((0,), (0,)), ((), ()))


def sds(shape, dtype):
    return jax.ShapeDtypeStruct(shape, dtype)


def params(**kw):
    return pltpu.CompilerParams(vmem_limit_bytes=VMEM_LIMIT, **kw)


def cost(flops, nbytes, trans=0):
    return pl.CostEstimate(
        flops=int(flops / 16), bytes_accessed=int(nbytes / 16), transcendentals=int(trans / 16)
    )


def pairs(axis, step):
    return [(i, i ^ step) for i in range(lax.axis_size(axis))]


def swap(value, axis, step):
    return lax.ppermute(value, axis, pairs(axis, step))


def sum_all(value, axes=("wa", "ha", "img"), **fillers):
    for axis in axes:
        count = lax.axis_size(axis)
        total = value
        if count <= 4:
            for step in range(1, count):
                total = total + swap(value, axis, step)
        else:
            step = 1
            while step < count:
                total = total + swap(total, axis, step)
                step *= 2
        if axis in fillers:
            total = after(total, *fillers[axis](value))
        value = total
    return value


def row_halo(first, last):
    count = lax.axis_size("ha")
    odd = lax.axis_index("ha") % 2 == 1
    got = []
    for shift in (0, 1):
        upper = [i for i in range(count) if i % 2 == shift and i + 1 < count]
        pairing = {i: i + 1 for i in upper} | {i + 1: i for i in upper}
        send = jnp.where(odd == (shift == 1), last, first)
        got.append(lax.ppermute(send, "ha", [(i, pairing.get(i, i)) for i in range(count)]))
    return jnp.where(odd, got[0], got[1]), jnp.where(odd, got[1], got[0])


def col_halo(left_edge, right_edge):
    count = lax.axis_size("wa")
    if count == 2:
        mine = jnp.where(lax.axis_index("wa") == 0, right_edge, left_edge)
        got = swap(mine, "wa", 1)
        none = jnp.zeros_like(got)
        first = lax.axis_index("wa") == 0
        return jnp.where(first, none, got), jnp.where(first, got, none)
    up = [(i, i + 1) for i in range(count - 1)]
    down = [(i + 1, i) for i in range(count - 1)]
    return lax.ppermute(right_edge, "wa", up), lax.ppermute(left_edge, "wa", down)


def halo(edges, batch):
    edge_rows, edge_cols = edges
    top, bottom = row_halo(edge_rows[0], edge_rows[1])
    rows = jnp.stack([top, bottom])
    return rows, halo_cols(edge_cols.astype(BF), rows, batch)


def after(value, *deps):
    return lax.optimization_barrier((value,) + deps)[0]


class Gather:
    def __init__(self, own):
        self.own = own

    def near(self, *deps):
        self.near_got = swap(after(self.own, *deps), "ha", 2)
        return self.near_got

    def join(self, *deps):
        self.line_low = after(jnp.concatenate([self.own, self.near_got], axis=0), *deps)
        return self.line_low

    def far(self, *deps):
        self.line_high = swap(after(self.line_low, *deps), "ha", 1)
        return self.line_high

    def low(self, *deps):
        low = after(self.line_low, *deps)
        self.low_x, self.low_y = swap(low, "img", 1), swap(low, "img", 2)
        return self.low_x, self.low_y

    def high(self, *deps):
        high = after(self.line_high, *deps)
        self.high_x, self.high_y = swap(high, "img", 1), swap(high, "img", 2)
        return self.high_x, self.high_y

    def corner_a(self, *deps):
        self.corner_low = swap(after(self.low_x, *deps), "img", 2)
        return self.corner_low

    def corner_b(self, *deps):
        self.corner_high = swap(after(self.high_y, *deps), "img", 1)
        return self.corner_high

    def pieces(self, *deps):
        mine = (
            self.line_low, self.line_high, self.low_x, self.high_x,
            self.low_y, self.high_y, self.corner_low, self.corner_high,
        )
        return mine + tuple(swap(after(part, *deps), "wa", 1) for part in mine)


def edge_row(field, h):
    return to_rows(field[:, h : h + 1])[0]


def halo_cols(edge_cols, rows, batch):
    tall, chans = rows.shape[1:]
    across = tall // (2 * batch)
    around = rows.reshape(2, 2, batch, across, chans)

    def edge(side):
        inner = edge_cols[:, side * batch : (side + 1) * batch]
        outer = around[:, side, :, (across - 1) * side]
        return jnp.concatenate([outer[0:1], inner, outer[1:2]], axis=0)

    return jnp.concatenate(col_halo(edge(0), edge(1)), axis=1).astype(F32)


def ring_gather(value, axis):
    count = lax.axis_size(axis)
    place = lax.axis_index(axis)
    value = value[None]
    if count == 4:
        value = jnp.concatenate([value] + [swap(value, axis, step) for step in (1, 2, 3)], axis=0)
        for step in (1, 2):
            parts = value.reshape((2, 2) + value.shape[1:])
            along = 1 if step == 1 else 0
            turned = jnp.flip(parts, along)
            value = jnp.where((place // step) % 2 == 0, parts, turned).reshape(value.shape)
        return value
    step = 1
    while step < count:
        came = swap(value, axis, step)
        first = (place // step) % 2 == 0
        value = jnp.concatenate(
            [jnp.where(first, value, came), jnp.where(first, came, value)], axis=0
        )
        step *= 2
    return value


def gather_proj_core(own):
    got = swap(own, "wa", 1)
    even = lax.axis_index("wa") % 2 == 0
    return jnp.stack([jnp.where(even, own, got), jnp.where(even, got, own)])


def add_low(*parts):
    total = parts[0].astype(F32)
    for part in parts[1:]:
        total = total + part.astype(F32)
    return total.astype(BF)


class Scatter:
    def __init__(self, mine, other):
        self.mine, self.other = mine, other

    def wa(self, *deps):
        self.came = swap(after(self.other, *deps), "wa", 1)
        return self.came

    def corner_sum(self, *deps):
        self.corner = add_low(self.mine[3], after(self.came, *deps)[3])
        return self.corner

    def corner_send(self, *deps):
        corner = after(self.corner, *deps)
        self.to_x = swap(corner[0:2], "img", 1)
        self.to_y = swap(corner[2:4], "img", 2)
        return self.to_x, self.to_y

    def high_sum(self, *deps):
        came = after(self.came, *deps)
        self.high = (
            add_low(self.mine[1][2:4], came[1][2:4], self.to_y),
            add_low(self.mine[2][2:4], came[2][2:4]),
        )
        return self.high

    def high_send(self, *deps):
        self.high_x = swap(after(self.high[0], *deps), "img", 1)
        self.high_y = swap(after(self.high[1], *deps), "img", 2)
        return self.high_x, self.high_y

    def low_sum(self, *deps):
        came = after(self.came, *deps)
        self.low = (
            add_low(self.mine[1][0:2], came[1][0:2]),
            add_low(self.mine[2][0:2], came[2][0:2], self.to_x),
        )
        return self.low

    def low_send(self, *deps):
        self.low_x = swap(after(self.low[0], *deps), "img", 1)
        self.low_y = swap(after(self.low[1], *deps), "img", 2)
        return self.low_x, self.low_y

    def far_sum(self, *deps):
        came = after(self.came, *deps)
        self.far = add_low(self.mine[0][2:4], came[0][2:4], self.high_x, self.high_y)
        return self.far

    def far_send(self, *deps):
        self.from_far = swap(after(self.far, *deps), "ha", 1)
        return self.from_far

    def near_sum(self, *deps):
        came = after(self.came, *deps)
        self.near = add_low(
            self.mine[0][1], came[0][1], self.low_x[1], self.low_y[1], self.from_far[1]
        )
        return self.near

    def near_send(self, *deps):
        self.from_near = swap(after(self.near, *deps), "ha", 2)
        return self.from_near

    def finish(self, *deps):
        total = add_low(
            after(self.mine[0][0], *deps), self.came[0][0], self.low_x[0], self.low_y[0], self.from_far[0], self.from_near
        )
        step = 2
        while step < lax.axis_size("wa"):
            total = add_low(total, swap(total, "wa", step))
            step *= 2
        return total, swap(total, "wa", 1)


def coef(sums, gb, count_all):
    mean = sums[0:1] / count_all
    var = sums[1:2] / count_all - mean * mean
    rs = lax.rsqrt(var + eps_norm)
    sc = gb[0:1] * rs
    return mean, rs, sc, gb[1:2] - mean * sc


def sigm(v):
    return pl.reciprocal(1.0 + jnp.exp(-v), approx=True)


def side_mask(idx, rows, lanes, count):
    row = lax.broadcasted_iota(jnp.int32, (rows, lanes), 0)
    return jnp.where(row < rows // 2, idx[5], idx[6]).astype(F32)


def col_block(cols, r, side, batch, across):
    lanes = cols.shape[-1]
    parts = [
        jnp.broadcast_to(cols[r, pl.ds(side * batch + b, 1), :], (across, lanes))
        for b in range(batch)
    ]
    return jnp.concatenate(parts, axis=0)


def shifted(even, odd, hl, hr, batch, across):
    lanes = even.shape[-1]
    shape = (batch, across, lanes)
    j = lax.broadcasted_iota(jnp.int32, shape, 1)
    lo = jnp.where(j == 0, hl.reshape(shape), pltpu.roll(odd.reshape(shape), 1, 1))
    hi = jnp.where(j == across - 1, hr.reshape(shape), pltpu.roll(even.reshape(shape), across - 1, 1))
    return lo.reshape(even.shape), hi.reshape(even.shape)


def put_row(x3, r, row, cols, batch, across):
    q = batch * across
    even, odd = row[0:q], row[q : 2 * q]
    hl = col_block(cols, r, 0, batch, across)
    hr = col_block(cols, r, 1, batch, across)
    lo, hi = shifted(even, odd, hl, hr, batch, across)
    x3[0, r] = jnp.concatenate([lo, even], axis=0).astype(BF)
    x3[1, r] = row.astype(BF)
    x3[2, r] = jnp.concatenate([odd, hi], axis=0).astype(BF)


def flip(s):
    return s // 2 + 2 * (s % 2)


WEIGHTS = (NB * NB, 9, 2, HB, BLK)


def weight_copies_rel(idx, pieces, wv, sems):
    rows = ([], [], [])
    count = len(pieces) // 2
    for half in range(2):
        parts = pieces[half * count : (half + 1) * count]
        h = lax.bitwise_xor(idx[2], half)
        for e in range(4):
            for k in range(2):
                src = parts[2 * e + k]
                for dy, copies in enumerate(rows):
                    taps = pl.ds(3 * dy, 3)
                    copies.append(
                        pltpu.make_async_copy(
                            src.at[:, taps],
                            wv.at[pl.ds(NB * e + 2 * k, 2), taps, h],
                            sems.at[dy, len(copies)],
                        )
                    )
    return rows


def weight_copies_task(idx, pieces, first, wv, sems):
    return [
        pltpu.make_async_copy(
            pieces[half].at[:, pl.ds(first, 9)],
            wv.at[:, :, lax.bitwise_xor(idx[2], half)],
            sems.at[half],
        )
        for half in range(2)
    ]


def tap(wv, m, idx=None):
    def block(i, j):
        if idx is not None:
            i, j = lax.bitwise_xor(idx[0], i), flip_place(idx[1], j)
        return wv[NB * i + j, m].reshape(BLK, BLK)

    rows = [jnp.concatenate([block(i, j) for j in range(NB)], axis=1) for i in range(NB)]
    return jnp.concatenate(rows, axis=0)


def put_edges(field, edge_rows, edge_cols, batch):
    height, tall = field.shape[0], field.shape[1]
    across = tall // (2 * batch)
    edge_rows[0] = field[0].astype(BF)
    edge_rows[1] = field[height - 1].astype(BF)

    @pl.loop(0, height)
    def _(h):
        for side in range(2):
            for b in range(batch):
                place = side * (tall // 2 + across - 1) + b * across
                edge_cols[h, side * batch + b : side * batch + b + 1] = field[h, place : place + 1]


def shift_kernel(batch, idx, x_ref, rows_ref, cols_ref, x3_ref, work):
    height, tall = x_ref.shape[0], x_ref.shape[1]
    across = tall // (2 * batch)
    top, bottom = idx[3].astype(F32), idx[4].astype(F32)
    work[...] = cols_ref[...]
    work[0] = work[0] * top
    work[height + 1] = work[height + 1] * bottom
    cols_ref = work
    put_row(x3_ref, 0, rows_ref[0].astype(F32) * top, cols_ref, batch, across)
    put_row(x3_ref, height + 1, rows_ref[1].astype(F32) * bottom, cols_ref, batch, across)

    @pl.loop(0, height)
    def _(h):
        put_row(x3_ref, h + 1, x_ref[h].astype(F32), cols_ref, batch, across)


def shift_copies(idx, field, rows, cols, batch):
    height, tall, chans = field.shape
    lanes = BLK
    return pl.pallas_call(
        functools.partial(shift_kernel, batch),
        grid=(chans // lanes,),
        in_specs=[
            SM,
            pl.BlockSpec((height, tall, lanes), lambda c: (0, 0, c)),
            pl.BlockSpec((2, tall, lanes), lambda c: (0, 0, c)),
            pl.BlockSpec((height + 2, 2 * batch, lanes), lambda c: (0, 0, c)),
        ],
        out_specs=pl.BlockSpec((3, height + 2, tall, lanes), lambda c: (0, 0, 0, c)),
        out_shape=sds((3, height + 2, tall, chans), BF),
        scratch_shapes=[pltpu.VMEM((height + 2, 2 * batch, lanes), F32)],
        compiler_params=params(),
        cost_estimate=cost(0, 8e6),
        name="shift_copies",
    )(idx, field, rows, cols)


def conv_kernel(n_pieces, batch, transposed, want_sums, idx_ref, x_hbm, *refs):
    pieces = refs[:n_pieces]
    o_hbm = refs[n_pieces]
    s_ref, er_ref, ec_ref = refs[n_pieces + 1 : n_pieces + 4] if want_sums else (None,) * 3
    wv, x_ref, acc_ref, o_ref, w_sems, x_sems, o_sems = refs[-7:]
    height, tall = x_ref.shape[1] - 2, x_ref.shape[2]
    step = height // 2
    rows = step * tall
    cut = ((0, step + 2), (step + 2, step))
    x_copies = [
        pltpu.make_async_copy(
            x_hbm.at[:, pl.ds(first, count)], x_ref.at[:, pl.ds(first, count)], x_sems.at[k]
        )
        for k, (first, count) in enumerate(cut)
    ]
    w_copies = weight_copies_rel(idx_ref, pieces, wv, w_sems)
    order = (2, 1, 0) if transposed else (0, 1, 2)
    x_copies[0].start()
    for dy in order:
        for copy in w_copies[dy]:
            copy.start()
    x_copies[1].start()

    def part_of(part, waits):
        for n, dy in enumerate(order):
            if waits:
                for copy in w_copies[dy]:
                    copy.wait()
                if n == 0:
                    x_copies[0].wait()
            acc = None
            for dx in range(3):
                if transposed:
                    view = x_ref[2 - dx, part * step + 2 - dy : (part + 1) * step + 2 - dy]
                    dims = NT
                else:
                    view = x_ref[dx, part * step + dy : (part + 1) * step + dy]
                    dims = (((1,), (0,)), ((), ()))
                piece = lax.dot_general(
                    view.reshape(rows, C), tap(wv, 3 * dy + dx, idx_ref), dims, preferred_element_type=F32
                )
                acc = piece if acc is None else acc + piece
            if n == 0:
                acc_ref[...] = acc
            elif n == 1:
                acc_ref[...] += acc
        total = acc_ref[...] + acc
        o_ref[part * step : (part + 1) * step] = total.reshape(step, tall, C).astype(o_ref.dtype)
        out = pltpu.make_async_copy(
            o_ref.at[pl.ds(part * step, step)], o_hbm.at[pl.ds(part * step, step)], o_sems.at[part]
        )
        out.start()
        if want_sums:
            first = jnp.sum(total, axis=0, keepdims=True)
            second = jnp.sum(total * total, axis=0, keepdims=True)
            if part == 0:
                s_ref[0:1], s_ref[1:2] = first, second
            else:
                s_ref[0:1] += first
                s_ref[1:2] += second
        return out

    first = part_of(0, True)
    x_copies[1].wait()
    second = part_of(1, False)
    if want_sums:
        put_edges(o_ref, er_ref, ec_ref, batch)
    first.wait()
    second.wait()


def conv(idx, x3, pieces, transposed, dtype, name, batch=0):
    want_sums = batch > 0
    height, tall = x3.shape[1] - 2, x3.shape[2]
    out_shape = [sds((height, tall, C), dtype)]
    if want_sums:
        out_shape += [sds((2, C), F32), sds((2, tall, C), BF), sds((height, 2 * batch, C), F32)]
    out = pl.pallas_call(
        functools.partial(conv_kernel, len(pieces), batch, transposed, want_sums),
        in_specs=[SM, ANY] + [ANY] * len(pieces),
        out_specs=[ANY] + [VM] * (len(out_shape) - 1),
        out_shape=out_shape,
        scratch_shapes=[
            pltpu.VMEM(WEIGHTS, BF),
            pltpu.VMEM(x3.shape, BF),
            pltpu.VMEM((height // 2 * tall, C), F32),
            pltpu.VMEM((height, tall, C), dtype),
            pltpu.SemaphoreType.DMA((3, 16)),
            pltpu.SemaphoreType.DMA((2,)),
            pltpu.SemaphoreType.DMA((2,)),
        ],
        compiler_params=params(),
        cost_estimate=cost(2 * 9 * C * C * height * tall, 10e6),
        name=name,
    )(idx, x3, *pieces)
    return (out[0], out[1], out[2:]) if want_sums else out[0]


def mid_kernel(batch, count_all, idx, st, gb, z_ref, rows_ref, cols_ref, d_ref, u3, hp, hc, hs, uc):
    height, tall, lanes = z_ref.shape
    across = tall // (2 * batch)
    step = pl.program_id(0)
    mean, rs, sc, sh = coef(st[...], gb[...], count_all)

    def act(v):
        y = v * sc + sh
        return y * sigm(y)

    mask = side_mask(idx, 2 * batch, lanes, 0)
    flat = act(cols_ref[...].reshape(-1, lanes)).reshape(height + 2, 2 * batch, lanes)
    uc[...] = flat * mask[None]
    uc[0] = uc[0] * idx[3].astype(F32)
    uc[height + 1] = uc[height + 1] * idx[4].astype(F32)
    put_row(u3, 0, act(rows_ref[0].astype(F32)) * idx[3].astype(F32), uc, batch, across)
    put_row(u3, height + 1, act(rows_ref[1].astype(F32)) * idx[4].astype(F32), uc, batch, across)

    @pl.loop(0, height)
    def _(h):
        put_row(u3, h + 1, act(z_ref[h]), uc, batch, across)

    @pl.when(step == 0)
    def _():
        hp[...] = jnp.zeros(hp.shape, F32)
        hc[...] = jnp.zeros(hc.shape, F32)

    hc[...] += jnp.dot(
        uc[...].reshape(-1, lanes).astype(BF), d_ref[...], preferred_element_type=F32
    )
    part = (height + 2) // 2
    size = part * tall

    @pl.loop(0, 2)
    def _(k):
        hp[pl.ds(pl.multiple_of(k * size, size), size)] += jnp.dot(
            u3[1, pl.ds(k * part, part)].reshape(size, lanes),
            d_ref[...],
            preferred_element_type=F32,
        )

    @pl.when(step == pl.num_programs(0) - 1)
    def _():
        inner = hp[tall : (height + 1) * tall]
        hs[0:1] = jnp.sum(inner, axis=0, keepdims=True)
        hs[1:2] = jnp.sum(inner * inner, axis=0, keepdims=True)


def mid(idx, st, gb, z, rows, cols, down, batch, count_all):
    height, tall, chans = z.shape
    lanes = 2 * BLK
    r = height + 2
    wide = TASKS * CA
    return pl.pallas_call(
        functools.partial(mid_kernel, batch, count_all),
        grid=(chans // lanes,),
        in_specs=[
            SM,
            pl.BlockSpec((2, lanes), lambda c: (0, c)),
            pl.BlockSpec((2, lanes), lambda c: (0, c)),
            pl.BlockSpec((height, tall, lanes), lambda c: (0, 0, c)),
            pl.BlockSpec((2, tall, lanes), lambda c: (0, 0, c)),
            pl.BlockSpec((r, 2 * batch, lanes), lambda c: (0, 0, c)),
            pl.BlockSpec((lanes, wide), lambda c: (c, 0)),
        ],
        out_specs=[
            pl.BlockSpec((3, r, tall, lanes), lambda c: (0, 0, 0, c)),
            pl.BlockSpec((r * tall, wide), lambda c: (0, 0)),
            pl.BlockSpec((r * 2 * batch, wide), lambda c: (0, 0)),
            pl.BlockSpec((2, wide), lambda c: (0, 0)),
        ],
        out_shape=[
            sds((3, r, tall, chans), BF),
            sds((r * tall, wide), F32),
            sds((r * 2 * batch, wide), F32),
            sds((2, wide), F32),
        ],
        scratch_shapes=[pltpu.VMEM((r, 2 * batch, lanes), F32)],
        compiler_params=params(),
        cost_estimate=cost(2 * r * tall * chans * wide, 10e6, 2e6),
        name="mid",
    )(idx, st, gb, z, rows, cols, down)


def hidden_kernel(tall, count_all, st, gb, hp, hc, up, h_ref, hcb, ms):
    mean, rs, sc, sh = coef(st[...], gb[...], count_all)
    yc = hc[...] * sc + sh
    hcb[...] = (yc * sigm(yc)).astype(BF)
    n_rows = hp.shape[0] // tall
    ms[...] = jnp.zeros(ms.shape, F32)

    def row(r):
        at = pl.ds(pl.multiple_of(r * tall, tall), tall)
        y = hp[at] * sc + sh
        h_ref[at] = (y * sigm(y)).astype(BF)

    @pl.loop(0, n_rows)
    def _(r):
        row(r)

    chunk = 4 * tall
    for t in range(TASKS):

        @pl.loop(0, (n_rows - 2) // 4)
        def _(k):
            at = pl.ds(pl.multiple_of(tall + k * chunk, tall), chunk)
            pre = jnp.dot(h_ref[at, t * CA : (t + 1) * CA], up[t], preferred_element_type=F32)
            ms[2 * t : 2 * t + 1] += jnp.sum(pre, axis=0, keepdims=True)
            ms[2 * t + 1 : 2 * t + 2] += jnp.sum(pre * pre, axis=0, keepdims=True)


def hidden(st, gb, hp, hc, up, tall, count_all):
    return pl.pallas_call(
        functools.partial(hidden_kernel, tall, count_all),
        in_specs=[VM] * 5,
        out_specs=[VM] * 3,
        out_shape=[sds(hp.shape, BF), sds(hc.shape, BF), sds((2 * TASKS, C), F32)],
        compiler_params=params(),
        cost_estimate=cost(2 * hp.shape[0] * CA * C * TASKS, 5e6, 2e6),
        name="hidden",
    )(st, gb, hp, hc, up)


def task_weights(idx, pieces, wv, sems):
    t = pl.program_id(0)
    slot = lax.rem(t, 2)

    def copies(task, place):
        return weight_copies_task(idx, pieces, task * 9, wv.at[place], sems.at[place])

    @pl.when(t == 0)
    def _():
        for copy in copies(0, 0):
            copy.start()

    for copy in copies(t, slot):
        copy.wait()

    @pl.when(t + 1 < pl.num_programs(0))
    def _():
        for copy in copies(t + 1, 1 - slot):
            copy.start()

    return slot


def task_kernel(idx, go, se, so, mine, other, da, out, wv, ws, sems):
    q = go.shape[3]
    half_h = go.shape[2] - 2
    slot = task_weights(idx, (mine, other), wv, sems)

    def add(a, b):
        return (a.astype(F32) + b.astype(F32)).astype(BF)

    for a in range(2):
        for k in range(2):
            taps = []
            for dx in range(3):
                if k == 0:
                    taps.append(add(tap(wv.at[slot], 3 * a + dx), tap(wv.at[slot], 3 * (a + 1) + dx)))
                else:
                    taps.append(tap(wv.at[slot], 3 * (2 if a == 0 else 0) + dx))
            ws[a, k, 0, 0] = add(taps[0], taps[1])
            ws[a, k, 0, 1] = taps[2]
            ws[a, k, 1, 0] = add(taps[1], taps[2])
            ws[a, k, 1, 1] = taps[0]
    for a in range(2):
        for bb in range(2):
            acc = None
            for k in range(2):
                for m in range(2):
                    ro = 0 if k == 0 else (-1 if a == 0 else 1)
                    co = 0 if m == 0 else (-1 if bb == 0 else 1)
                    view = go[0, co + 1, 1 + ro : 1 + ro + half_h].reshape(half_h * q, C)
                    piece = lax.dot_general(
                        view, ws[a, k, bb, m], NT, preferred_element_type=F32
                    )
                    acc = piece if acc is None else acc + piece
            da[0, :, a, bb] = acc.reshape(half_h, q, C).astype(BF)

    acc = None
    for dy in range(3):
        for dx in range(3):
            if dy == 1:
                view = so[0, dx]
            else:
                view = se[0, dx, dy // 2 : dy // 2 + half_h]
            piece = jnp.dot(
                view.reshape(half_h * q, C), tap(wv.at[slot], 3 * dy + dx), preferred_element_type=F32
            )
            acc = piece if acc is None else acc + piece
    out[0] = (acc * 0.25).reshape(half_h, q, C).astype(BF)


def task_convs(idx, go, se, so, pieces):
    half_h, q = go.shape[2] - 2, go.shape[3]
    back, out = pl.pallas_call(
        task_kernel,
        grid=(TASKS,),
        in_specs=[SM]
        + [pl.BlockSpec((1,) + a.shape[1:], lambda t: (t, 0, 0, 0, 0)) for a in (go, se, so)]
        + [ANY, ANY],
        out_specs=[
            pl.BlockSpec((1, half_h, 2, 2, q, C), lambda t: (t, 0, 0, 0, 0, 0)),
            pl.BlockSpec((1, half_h, q, C), lambda t: (t, 0, 0, 0)),
        ],
        out_shape=[sds((TASKS, half_h, 2, 2, q, C), BF), sds((TASKS, half_h, q, C), BF)],
        scratch_shapes=[
            pltpu.VMEM((2,) + WEIGHTS, BF),
            pltpu.VMEM((2, 2, 2, 2, C, C), BF),
            pltpu.SemaphoreType.DMA((2, 2)),
        ],
        compiler_params=params(),
        cost_estimate=cost(TASKS * 2 * 25 * C * C * half_h * q, 30e6),
        name="task_convs",
    )(idx, go, se, so, *pieces)
    return back.reshape(TASKS, 2 * half_h, 2 * q, C), out


def attend_kernel(
    batch, count_all, idx, st, gb, mst, mgb, z_ref, rows_ref, cols_ref, h_ref, hc_ref, up,
    se, so, pooled,
    ac, pre, prev,
):
    height, tall, lanes = z_ref.shape
    across = tall // (2 * batch)
    q = tall // 2
    _, _, sc, sh = coef(st[...], gb[...], count_all)
    mcoef = [
        coef(mst[2 * t : 2 * t + 2], mgb[2 * t : 2 * t + 2], count_all) for t in range(TASKS)
    ]
    mask = side_mask(idx, 2 * batch, lanes, 0)
    top, bottom = idx[3].astype(F32), idx[4].astype(F32)

    y = cols_ref[...].reshape(-1, lanes) * sc + sh
    pc = (y * sigm(y)).reshape(height + 2, 2 * batch, lanes) * mask[None]
    for t in range(TASKS):
        mc = jnp.dot(hc_ref[:, t * CA : (t + 1) * CA], up[t], preferred_element_type=F32)
        _, _, msc, msh = mcoef[t]
        mc = sigm(mc * msc + msh).reshape(height + 2, 2 * batch, lanes)
        ac[t] = (mc * pc).astype(BF).astype(F32)
        ac[t, 0] = ac[t, 0] * top
        ac[t, height + 1] = ac[t, height + 1] * bottom
        pre[t] = jnp.dot(
            h_ref[:, t * CA : (t + 1) * CA], up[t], preferred_element_type=F32
        ).reshape(height + 2, tall, lanes)

    def sums_of(r, p):
        out = []
        for t in range(TASKS):
            _, _, msc, msh = mcoef[t]
            a = (sigm(pre[t, r] * msc + msh) * p).astype(BF).astype(F32)
            even, odd = a[0:q], a[q : 2 * q]
            lo, hi = shifted(
                even,
                odd,
                col_block(ac.at[t], r, 0, batch, across),
                col_block(ac.at[t], r, 1, batch, across),
                batch,
                across,
            )
            out.append((lo + even, even + odd, odd + hi))
        return out

    def halo_row(r, place, scale):
        yy = rows_ref[place].astype(F32) * sc + sh
        return sums_of(r, yy * sigm(yy) * scale)

    def inner(h):
        yy = z_ref[h] * sc + sh
        p = yy * sigm(yy)
        return sums_of(h + 1, p), p[0:q] + p[q : 2 * q]

    first = halo_row(0, 0, top)
    for t in range(TASKS):
        for dx in range(3):
            prev[t, dx] = first[t][dx]

    @pl.loop(0, height // 2)
    def _(i):
        cs, pool_a = inner(2 * i)
        for t in range(TASKS):
            for dx in range(3):
                se[t, dx, i] = (prev[t, dx] + cs[t][dx]).astype(BF)
                prev[t, dx] = cs[t][dx]
        cs, pool_b = inner(2 * i + 1)
        for t in range(TASKS):
            for dx in range(3):
                so[t, dx, i] = (prev[t, dx] + cs[t][dx]).astype(BF)
                prev[t, dx] = cs[t][dx]
        pooled[i] = ((pool_a + pool_b) * 0.25).astype(BF)

    last = halo_row(height + 1, 1, bottom)
    for t in range(TASKS):
        for dx in range(3):
            se[t, dx, height // 2] = (prev[t, dx] + last[t][dx]).astype(BF)


def lane_blocks(lanes):
    def block(*lead):
        return pl.BlockSpec(lead + (lanes,), lambda c: (0,) * len(lead) + (c,))

    return block


def whole(a):
    return pl.BlockSpec(a.shape, lambda c: (0,) * a.ndim)


def attend(idx, st, gb, mst, mgb, z, rows, cols, h, hc, up, batch, count_all):
    height, tall, chans = z.shape
    lanes = BLK
    r, q, half = height + 2, tall // 2, height // 2
    block = lane_blocks(lanes)
    return pl.pallas_call(
        functools.partial(attend_kernel, batch, count_all),
        grid=(chans // lanes,),
        in_specs=[
            SM, block(2), block(2), block(2 * TASKS), block(2 * TASKS), block(height, tall), block(2, tall),
            block(r, 2 * batch), whole(h), whole(hc), block(TASKS, CA),
        ],
        out_specs=[block(TASKS, 3, half + 1, q), block(TASKS, 3, half, q), block(half, q)],
        out_shape=[
            sds((TASKS, 3, half + 1, q, chans), BF),
            sds((TASKS, 3, half, q, chans), BF),
            sds((half, q, chans), BF),
        ],
        scratch_shapes=[
            pltpu.VMEM((TASKS, r, 2 * batch, lanes), F32),
            pltpu.VMEM((TASKS, r, tall, lanes), F32),
            pltpu.VMEM((TASKS, 3, q, lanes), F32),
        ],
        compiler_params=params(),
        cost_estimate=cost(2 * r * tall * CA * chans * TASKS, 15e6, 6e6),
        name="attend",
    )(idx, st, gb, mst, mgb, z, rows, cols, h, hc, up)


def attend_back_kernel(
    batch, count_all, st, gb, mst, mgb, z_ref, h_ref, up, da, cot, dym, dy2, sums, er, ec, pre, acc
):
    height, tall, lanes = z_ref.shape
    mean, rs, sc, sh = coef(st[...], gb[...], count_all)
    mcoef = [
        coef(mst[2 * t : 2 * t + 2], mgb[2 * t : 2 * t + 2], count_all) for t in range(TASKS)
    ]
    for t in range(TASKS):
        pre[t] = jnp.dot(
            h_ref[tall : (height + 1) * tall, t * CA : (t + 1) * CA],
            up[t],
            preferred_element_type=F32,
        ).reshape(height, tall, lanes)
    acc[...] = jnp.zeros(acc.shape, F32)

    def add(k, value):
        acc[k] += jnp.sum(value.reshape(-1, 8, lanes), axis=0)

    @pl.loop(0, height)
    def _(h):
        z = z_ref[h]
        yy = z * sc + sh
        s = sigm(yy)
        p = yy * s
        shared = cot[h // 2]
        shared = jnp.concatenate([shared, shared], axis=0)
        branches = []
        for t in range(TASKS):
            mmean, _, msc, msh = mcoef[t]
            mp = pre[t, h]
            m = sigm(mp * msc + msh)
            br = m * da[t, h].astype(F32)
            branches.append(br)
            shared = shared + br
            dm = br * p * (1.0 - m)
            dym[t, h] = dm.astype(BF)
            add(2 * t, dm)
            add(2 * t + 1, dm * (mp - mmean))
        g2 = shared * (s * (1.0 + yy * (1.0 - s)))
        dy2[h] = g2
        add(6, g2)
        add(7, g2 * (z - mean))
        k = 8
        for t in range(TASKS):
            for s2 in range(t, TASKS):
                add(k, branches[t] * branches[s2])
                k += 1

    sums[...] = jnp.sum(acc[...], axis=1)
    for t in range(TASKS):
        sums[2 * t + 1 : 2 * t + 2] = sums[2 * t + 1 : 2 * t + 2] * mcoef[t][1]
    sums[7:8] = sums[7:8] * rs
    put_edges(dy2, er, ec, batch)


def attend_back(st, gb, mst, mgb, z, h, up, da, cot, batch, count_all):
    height, tall, chans = z.shape
    lanes = BLK
    block = lane_blocks(lanes)
    return pl.pallas_call(
        functools.partial(attend_back_kernel, batch, count_all),
        grid=(chans // lanes,),
        in_specs=[
            block(2), block(2), block(2 * TASKS), block(2 * TASKS), block(height, tall), whole(h),
            block(TASKS, CA), block(TASKS, height, tall), block(height // 2, tall // 2),
        ],
        out_specs=[
            block(TASKS, height, tall), block(height, tall), block(14), block(2, tall),
            block(height, 2 * batch),
        ],
        out_shape=[
            sds((TASKS, height, tall, chans), BF),
            sds((height, tall, chans), F32),
            sds((14, chans), F32),
            sds((2, tall, chans), BF),
            sds((height, 2 * batch, chans), F32),
        ],
        scratch_shapes=[
            pltpu.VMEM((TASKS, height, tall, lanes), F32),
            pltpu.VMEM((14, 8, lanes), F32),
        ],
        compiler_params=params(),
        cost_estimate=cost(2 * height * tall * CA * chans * TASKS, 15e6, 4e6),
        name="attend_back",
    )(st, gb, mst, mgb, z, h, up, da, cot)


def mask_back_kernel(
    tall, count_all, mst, mgb, msum, hst, hgb, dym, h_ref, hp, up, du, dh, hs, acc
):
    step = pl.program_id(0)
    n_rows = h_ref.shape[0]

    @pl.when(step == 0)
    def _():
        acc[...] = jnp.zeros(acc.shape, F32)

    inner = pl.ds(tall, n_rows - 2 * tall)
    for t in range(TASKS):
        mean, rs, sc, _ = coef(mst[2 * t : 2 * t + 2], mgb[2 * t : 2 * t + 2], count_all)
        tot = msum[2 * t : 2 * t + 1] / count_all
        cross = msum[2 * t + 1 : 2 * t + 2] * rs / count_all
        ht = h_ref[inner, t * CA : (t + 1) * CA]
        pre = jnp.dot(ht, up[t], preferred_element_type=F32)
        dm = dym[t].reshape(pre.shape).astype(F32)
        dz = (sc * (dm - tot - (pre - mean) * cross)).astype(BF)
        du[t] = lax.dot_general(ht, dz, TN, preferred_element_type=F32)
        acc[:, t * CA : (t + 1) * CA] += lax.dot_general(dz, up[t], NT, preferred_element_type=F32)

    @pl.when(step == pl.num_programs(0) - 1)
    def _():
        mean, rs, sc, sh = coef(hst[...], hgb[...], count_all)
        hs[...] = jnp.zeros(hs.shape, F32)
        chunk = 2 * tall

        @pl.loop(0, (n_rows - 2 * tall) // chunk)
        def _(k):
            at = pl.ds(pl.multiple_of(k * chunk, chunk), chunk)
            v = hp[pl.ds(pl.multiple_of(tall + k * chunk, tall), chunk)]
            y = v * sc + sh
            s = sigm(y)
            g = acc[at] * (s * (1.0 + y * (1.0 - s)))
            dh[at] = g
            hs[0:1] += jnp.sum(g, axis=0, keepdims=True)
            hs[1:2] += jnp.sum(g * (v - mean) * rs, axis=0, keepdims=True)


def mask_back(mst, mgb, msum, hst, hgb, dym, h, hp, up, tall, count_all):
    lanes = 2 * BLK
    wide = TASKS * CA
    pixels = h.shape[0] - 2 * tall

    def two(n):
        return pl.BlockSpec((n, lanes), lambda c: (0, c))

    def whole(a):
        return pl.BlockSpec(a.shape, lambda c: (0,) * a.ndim)

    return pl.pallas_call(
        functools.partial(mask_back_kernel, tall, count_all),
        grid=(C // lanes,),
        in_specs=[
            two(2 * TASKS),
            two(2 * TASKS),
            two(2 * TASKS),
            whole(hst),
            whole(hgb),
            pl.BlockSpec(dym.shape[:3] + (lanes,), lambda c: (0, 0, 0, c)),
            whole(h),
            whole(hp),
            pl.BlockSpec((TASKS, CA, lanes), lambda c: (0, 0, c)),
        ],
        out_specs=[
            pl.BlockSpec((TASKS, CA, lanes), lambda c: (0, 0, c)),
            pl.BlockSpec((pixels, wide), lambda c: (0, 0)),
            pl.BlockSpec((2, wide), lambda c: (0, 0)),
        ],
        out_shape=[sds((TASKS, CA, C), F32), sds((pixels, wide), F32), sds((2, wide), F32)],
        scratch_shapes=[pltpu.VMEM((pixels, wide), F32)],
        compiler_params=params(),
        cost_estimate=cost(6 * pixels * C * wide, 8e6, 1e6),
        name="mask_back",
    )(mst, mgb, msum, hst, hgb, dym, h, hp, up)


def norm_back_kernel(
    batch, count_all, idx, st, gb, gs, dy, drows, dcols, z, zrows, zcols, x3, work
):
    height, tall, lanes = z.shape
    across = tall // (2 * batch)
    mean, rs, sc, _ = coef(st[...], gb[...], count_all)
    tot = gs[0:1] / count_all
    cross = gs[1:2] * rs / count_all

    def back(d, v):
        return sc * (d - tot - (v - mean) * cross)

    mask = side_mask(idx, 2 * batch, lanes, 0)
    flat = back(dcols[...].reshape(-1, lanes), zcols[...].reshape(-1, lanes))
    work[...] = flat.reshape(height + 2, 2 * batch, lanes) * mask[None]
    top, bottom = idx[3].astype(F32), idx[4].astype(F32)
    work[0] = work[0] * top
    work[height + 1] = work[height + 1] * bottom
    put_row(x3, 0, back(drows[0].astype(F32), zrows[0].astype(F32)) * top, work, batch, across)
    put_row(
        x3, height + 1, back(drows[1].astype(F32), zrows[1].astype(F32)) * bottom, work, batch, across
    )

    @pl.loop(0, height)
    def _(h):
        put_row(x3, h + 1, back(dy[h], z[h]), work, batch, across)


def norm_back(idx, st, gb, gs, dy, dhalo, z, zhalo, batch, count_all, name):
    height, tall, chans = z.shape
    lanes = 2 * BLK
    r = height + 2

    def two(n):
        return pl.BlockSpec((n, lanes), lambda c: (0, c))

    def three(a, b):
        return pl.BlockSpec((a, b, lanes), lambda c: (0, 0, c))

    field = [three(height, tall), three(2, tall), three(r, 2 * batch)]
    return pl.pallas_call(
        functools.partial(norm_back_kernel, batch, count_all),
        grid=(chans // lanes,),
        in_specs=[SM, two(2), two(2), two(2)] + field + field,
        out_specs=pl.BlockSpec((3, r, tall, lanes), lambda c: (0, 0, 0, c)),
        out_shape=sds((3, r, tall, chans), BF),
        scratch_shapes=[pltpu.VMEM((r, 2 * batch, lanes), F32)],
        compiler_params=params(),
        cost_estimate=cost(0, 10e6),
        name=name,
    )(idx, st, gb, gs, dy, *dhalo, z, *zhalo)


def first_back_kernel(
    batch, count_all, hst, hgb, hsum, st, gb, dh, hp, u3, part, z, down, dd, dy, gs, er, ec, low
):
    height, tall, lanes = z.shape

    @pl.when(pl.program_id(0) == 0)
    def _():
        mean, rs, sc, _ = coef(hst[...], hgb[...], count_all)
        tot = hsum[0:1] / count_all
        cross = hsum[1:2] * rs / count_all
        chunk = 2 * tall

        @pl.loop(0, height // 2)
        def _(k):
            at = pl.ds(pl.multiple_of(k * chunk, chunk), chunk)
            v = hp[pl.ds(pl.multiple_of(tall + k * chunk, tall), chunk)]
            low[at] = (sc * (dh[at] - tot - (v - mean) * cross)).astype(BF)

    u = u3[0, 1 : height + 1].reshape(height * tall, lanes)
    dd[...] = lax.dot_general(u, low[...], TN, preferred_element_type=F32)
    mean, rs, sc, sh = coef(st[...], gb[...], count_all)
    gs[...] = jnp.zeros(gs.shape, F32)
    rows = 4

    @pl.loop(0, height // rows)
    def _(k):
        at = pl.ds(pl.multiple_of(k * rows * tall, rows * tall), rows * tall)
        back = lax.dot_general(low[at], down[...], NT, preferred_element_type=F32)
        v = z[pl.ds(k * rows, rows)].reshape(rows * tall, lanes)
        y = v * sc + sh
        s = sigm(y)
        total = part[pl.ds(k * rows, rows)].reshape(rows * tall, lanes) + back
        g = total * (s * (1.0 + y * (1.0 - s)))
        dy[pl.ds(k * rows, rows)] = g.reshape(rows, tall, lanes)
        gs[0:1] += jnp.sum(g, axis=0, keepdims=True)
        gs[1:2] += jnp.sum(g * (v - mean) * rs, axis=0, keepdims=True)

    put_edges(dy, er, ec, batch)


def first_back(hst, hgb, hsum, st, gb, dh, hp, u3, part, z, down, batch, count_all):
    height, tall, chans = z.shape
    lanes = 2 * BLK
    wide = TASKS * CA

    def two(n):
        return pl.BlockSpec((n, lanes), lambda c: (0, c))

    def whole(a):
        return pl.BlockSpec(a.shape, lambda c: (0,) * a.ndim)

    field = pl.BlockSpec((height, tall, lanes), lambda c: (0, 0, c))
    return pl.pallas_call(
        functools.partial(first_back_kernel, batch, count_all),
        grid=(chans // lanes,),
        in_specs=[
            whole(hst),
            whole(hgb),
            whole(hsum),
            two(2),
            two(2),
            whole(dh),
            whole(hp),
            pl.BlockSpec((1, height + 2, tall, lanes), lambda c: (1, 0, 0, c)),
            field,
            field,
            pl.BlockSpec((lanes, wide), lambda c: (c, 0)),
        ],
        out_specs=[
            pl.BlockSpec((lanes, wide), lambda c: (c, 0)),
            field,
            two(2),
            pl.BlockSpec((2, tall, lanes), lambda c: (0, 0, c)),
            pl.BlockSpec((height, 2 * batch, lanes), lambda c: (0, 0, c)),
        ],
        out_shape=[
            sds((chans, wide), F32),
            sds((height, tall, chans), F32),
            sds((2, chans), F32),
            sds((2, tall, chans), BF),
            sds((height, 2 * batch, chans), F32),
        ],
        scratch_shapes=[pltpu.VMEM((height * tall, wide), BF)],
        compiler_params=params(),
        cost_estimate=cost(4 * height * tall * chans * wide, 12e6, 1e6),
        name="first_back",
    )(hst, hgb, hsum, st, gb, dh, hp, u3, part, z, down)


def flip_place(place, j):
    s = lax.bitwise_xor(place, j)
    return lax.shift_right_logical(s, 1) + 2 * lax.bitwise_and(s, 1)


def put_blocks(idx, grad, mine, other, m):
    low = grad.astype(BF)
    even = idx[2] == 0
    for i in range(NB):
        e = lax.bitwise_xor(idx[0], i)
        for j in range(NB):
            s = flip_place(idx[1], j)
            block = low[i * BLK : (i + 1) * BLK, j * BLK : (j + 1) * BLK]
            a, b = block[0:HB], block[HB:BLK]
            at = pl.ds(pl.multiple_of(m * HB, HB), HB)
            mine[e, s, at] = jnp.where(even, a, b)
            other[e, s, at] = jnp.where(even, b, a)


def put_in_order(grad, halves, m):
    low = grad.astype(BF)
    at = slice(m * HB, (m + 1) * HB)
    for i in range(NB):
        for j in range(NB):
            for h in range(2):
                row = i * BLK + h * HB
                halves[h, i * NB + j, at] = low[row : row + HB, j * BLK : (j + 1) * BLK]


def wgrad_kernel(n_extra, idx, x_hbm, g_hbm, *refs):
    mine_hbm, other_hbm, x3, g3, mine, other, sems, o_sems = refs[n_extra:]
    height, tall = x3.shape[1] - 2, x3.shape[2]
    g_copy = pltpu.make_async_copy(g_hbm.at[1, pl.ds(1, height)], g3, sems.at[3])
    x_copies = [pltpu.make_async_copy(x_hbm.at[k], x3.at[k], sems.at[k]) for k in range(3)]
    g_copy.start()
    for copy in x_copies:
        copy.start()
    g_copy.wait()
    outs = []

    def send(first, count):
        at = pl.ds(first, count)
        for k, (source, target) in enumerate(((mine, mine_hbm), (other, other_hbm))):
            copy = pltpu.make_async_copy(
                source.at[:, :, at], target.at[:, :, at], o_sems.at[len(outs)]
            )
            copy.start()
            outs.append(copy)

    g = g3[...].reshape(height * tall, C)
    for dx in range(3):
        x_copies[dx].wait()
        for dy in range(3):
            view = x3[dx, dy : dy + height].reshape(height * tall, C)
            grad = lax.dot_general(view, g, TN, preferred_element_type=F32)
            put_blocks(idx, grad, mine, other, 3 * dy + dx)
            send((3 * dy + dx) * HB, HB)

    if n_extra:
        ddown, dup = refs[:2]
        even = idx[2] == 0
        unit = BLK // 4

        def chunk(c):
            block, r = divmod(c, 4)
            t, block = divmod(block, 2 * NB)
            kind, n = divmod(block, NB)
            if kind == 0:
                return ddown[n * BLK + r * unit : n * BLK + (r + 1) * unit, t * CA : (t + 1) * CA]
            return dup[t, r * unit : (r + 1) * unit, n * BLK : (n + 1) * BLK]

        at = pl.ds(9 * HB, PROJ_ROWS)
        for n in range(NB * NB):
            e = lax.bitwise_xor(idx[0], n // NB)
            s = flip_place(idx[1], n % NB)
            a, b = [
                jnp.concatenate([chunk(6 * n + 3 * k + c) for c in range(3)], axis=0).astype(BF)
                for k in range(2)
            ]
            mine[e, s, at] = jnp.where(even, a, b)
            other[e, s, at] = jnp.where(even, b, a)
        send(9 * HB, PROJ_ROWS)

    for copy in outs:
        copy.wait()


def wgrad(idx, x3, g3, name, extra=()):
    r, tall = x3.shape[1], x3.shape[2]
    rows = 9 * HB + (PROJ_ROWS if extra else 0)
    blocks = (4, 4, rows, BLK)
    return pl.pallas_call(
        functools.partial(wgrad_kernel, len(extra)),
        in_specs=[SM, ANY, ANY] + [VM] * len(extra),
        out_specs=[ANY, ANY],
        out_shape=[sds(blocks, BF)] * 2,
        scratch_shapes=[
            pltpu.VMEM(x3.shape, BF),
            pltpu.VMEM((r - 2, tall, C), BF),
            pltpu.VMEM(blocks, BF),
            pltpu.VMEM(blocks, BF),
            pltpu.SemaphoreType.DMA((4,)),
            pltpu.SemaphoreType.DMA((20,)),
        ],
        compiler_params=params(),
        cost_estimate=cost(2 * 9 * C * C * (r - 2) * tall, 10e6),
        name=name,
    )(idx, x3, g3, *extra)


def task_wgrad_kernel(idx, se, so, go, halves):
    half, q = so.shape[2], so.shape[3]
    g = go[0, 0, 1 : half + 1].reshape(half * q, C)
    for dy in range(3):
        for dx in range(3):
            if dy == 1:
                view = so[0, dx]
            else:
                view = se[0, dx, dy // 2 : dy // 2 + half]
            grad = lax.dot_general(view.reshape(half * q, C), g, TN, preferred_element_type=F32)
            put_in_order(grad, halves, 3 * dy + dx)


def task_wgrad(idx, se, so, go):
    half, q = so.shape[2], so.shape[3]
    return pl.pallas_call(
        task_wgrad_kernel,
        grid=(TASKS,),
        in_specs=[
            SM,
            pl.BlockSpec((1,) + se.shape[1:], lambda t: (t, 0, 0, 0, 0)),
            pl.BlockSpec((1,) + so.shape[1:], lambda t: (t, 0, 0, 0, 0)),
            pl.BlockSpec((1, 1) + go.shape[2:], lambda t: (t, 1, 0, 0, 0)),
        ],
        out_specs=pl.BlockSpec((2, NB * NB, 9 * HB, BLK), lambda t: (0, 0, t, 0)),
        out_shape=sds((2, NB * NB, 9 * TASKS * HB, BLK), BF),
        compiler_params=params(),
        cost_estimate=cost(TASKS * 2 * 9 * C * C * half * q, 24e6),
        name="task_wgrad",
    )(idx, se, so, go)


def shampoo_steps(grads, left, right, lroot, rroot, weight, rate):
    count = len(grads)
    low = [g.astype(BF) for g in grads]
    step = [jnp.dot(lroot(k).astype(BF), low[k], preferred_element_type=F32) for k in range(count)]
    ll = [lax.dot_general(g, g, NT, preferred_element_type=F32) for g in low]
    rr = [lax.dot_general(g, g, TN, preferred_element_type=F32) for g in low]
    step = [
        jnp.dot(step[k].astype(BF), rroot(k).astype(BF), preferred_element_type=F32)
        for k in range(count)
    ]
    keep, add = stat_decay, 1.0 - stat_decay
    return [
        (keep * left(k) + add * ll[k], keep * right(k) + add * rr[k], weight(k) - rate * step[k])
        for k in range(count)
    ]


def shampoo_kernel(n_prev, idx, mine, other, left, right, lroot, rroot, weight, *refs):
    gr, ln, rn, wn = refs[n_prev:]
    even = idx[2] == 0
    together = 3
    for first in range(0, mine.shape[0] // HB, together):
        places = range(first, first + together)
        grads = []
        for k in places:
            a, b = mine[k * HB : (k + 1) * HB], other[k * HB : (k + 1) * HB]
            grads.append(jnp.concatenate([jnp.where(even, a, b), jnp.where(even, b, a)], axis=0))
        state = [
            functools.partial(lambda ref, k: ref[0, first + k], ref)
            for ref in (left, right, lroot, rroot, weight)
        ]
        done = shampoo_steps(grads, *state, conv_rate)
        for k, g, (new_l, new_r, new_w) in zip(places, grads, done):
            gr[0, k] = g.astype(F32)
            ln[0, k], rn[0, k], wn[0, k] = new_l, new_r, new_w


def shampoo_conv(idx, mine, other, state, first, prev, begin=0, n=9):
    each = 9
    block = pl.BlockSpec((1, each, BLK, BLK), lambda k: (0, (first + begin) // each + k, 0, 0))
    half = pl.BlockSpec((each * HB, BLK), lambda k: (begin // each + k, 0))
    full = state[0].shape
    return pl.pallas_call(
        functools.partial(shampoo_kernel, len(prev)),
        grid=(n // each,),
        in_specs=[SM, half, half] + [block] * 5 + [ANY] * len(prev),
        out_specs=[block] * 4,
        out_shape=[sds(full, F32)] * 4,
        input_output_aliases={8 + k: k for k in range(len(prev))},
        compiler_params=params(),
        cost_estimate=cost(n * 8 * BLK**3, n * 9 * BLK * BLK * 4),
        name="shampoo_conv",
    )(idx, mine, other, *state, *prev)


def shampoo_proj_kernel(g, left, right, lroot, rroot, weight, gr, ln, rn, wn):
    gr[...] = g[...].astype(F32)
    kinds, count = g.shape[1], g.shape[2]
    for kind in range(kinds):
        grads = [g[0, kind, k] for k in range(count)]
        state = [
            functools.partial(lambda ref, k: ref[0, kind, k], ref)
            for ref in (left, right, lroot, rroot, weight)
        ]
        done = shampoo_steps(grads, *state, proj_rate)
        for k, (new_l, new_r, new_w) in enumerate(done):
            ln[0, kind, k], rn[0, kind, k], wn[0, kind, k] = new_l, new_r, new_w


def shampoo_proj(g, left, right, lroot, rroot, weight):
    block = pl.BlockSpec((1,) + g.shape[1:], lambda t: (t, 0, 0, 0, 0))
    return pl.pallas_call(
        shampoo_proj_kernel,
        grid=g.shape[:1],
        in_specs=[block] * 6,
        out_specs=[block] * 4,
        out_shape=[sds(g.shape, F32)] * 4,
        compiler_params=params(),
        cost_estimate=cost(24 * 8 * BLK**3, 24 * 9 * BLK * BLK * 4),
        name="shampoo_proj",
    )(g, left, right, lroot, rroot, weight)


def norm_step_kernel(gs1, gsum, dhs, norm, moment, gram, grad, moment_new, norm_new):
    off_down = 2 * C
    off_up = off_down + TASKS * CA
    for row in range(2):
        k = 1 - row
        at = slice(row, row + 1)
        grad[at, 0:C] = gs1[k : k + 1]
        grad[at, C : 2 * C] = gsum[6 + k : 7 + k]
        grad[at, off_down:off_up] = dhs[k : k + 1]
        for t in range(TASKS):
            grad[at, off_up + t * C : off_up + (t + 1) * C] = gsum[2 * t + k : 2 * t + k + 1]
    g = grad[...]
    new = moment_decay * moment[...] + (1.0 - moment_decay) * g * g
    moment_new[...] = new
    norm_new[...] = norm[...] - norm_rate * g / (jnp.sqrt(new) + 1e-08)
    row = lax.broadcasted_iota(jnp.int32, (TASKS, TASKS), 0)
    col = lax.broadcasted_iota(jnp.int32, (TASKS, TASKS), 1)
    value = jnp.zeros((TASKS, TASKS), F32)
    k = 8
    for t in range(TASKS):
        for s in range(t, TASKS):
            total = jnp.sum(gsum[k : k + 1], axis=1, keepdims=True)
            hit = ((row == t) & (col == s)) | ((row == s) & (col == t))
            value = jnp.where(hit, total, value)
            k += 1
    gram[...] = value


def norm_step(gs1, gsum, dhs, norm, moment):
    like = sds(norm.shape, F32)
    return pl.pallas_call(
        norm_step_kernel,
        in_specs=[VM] * 5,
        out_specs=[VM] * 4,
        out_shape=[sds((TASKS, TASKS), F32), like, like, like],
        compiler_params=params(),
        cost_estimate=cost(0, 1e5),
        name="norm_step",
    )(gs1, gsum, dhs, norm, moment)


def to_rows(field):
    b, h, w, c = field.shape
    split = field.reshape(b, h, w // 2, 2, c)
    return jnp.transpose(split, (1, 3, 0, 2, 4)).reshape(h, w * b, c)


def from_rows(field, b):
    h, tall, c = field.shape
    split = field.reshape(h, 2, b, tall // (2 * b), c)
    return jnp.transpose(split, (2, 0, 3, 1, 4)).reshape(b, h, tall // b, c)


def pooled_rows(field):
    b, h, w, c = field.shape
    return jnp.transpose(field, (1, 0, 2, 3)).reshape(h, b * w, c)


def shards(
    images,
    cot_shared,
    cot_tasks,
    depth_mask,
    nash_weights,
    conv_weight,
    conv_left,
    conv_right,
    conv_left_root,
    conv_right_root,
    proj_weight,
    proj_left,
    proj_right,
    proj_left_root,
    proj_right_root,
    norm_params,
    norm_moment,
):
    batch, tile_h, tile_w, _ = images.shape
    half_h, half_w = tile_h // 2, tile_w // 2
    tall = batch * tile_w
    q = batch * half_w
    ha, wa = lax.axis_index("ha"), lax.axis_index("wa")
    count_all = float(
        batch * tile_h * tile_w * lax.axis_size("img") * lax.axis_size("ha") * lax.axis_size("wa")
    )
    idx = jnp.stack(
        [
            lax.axis_index("img"),
            ha,
            wa % 2,
            ha > 0,
            ha < lax.axis_size("ha") - 1,
            wa > 0,
            wa < lax.axis_size("wa") - 1,
        ]
    ).astype(jnp.int32)

    halves = conv_weight[0].reshape(conv_weight.shape[1], 2, HB, BLK)
    own = lax.dynamic_index_in_dim(halves, wa % 2, axis=1, keepdims=False).astype(BF)
    g0, g1 = Gather(own[None, 0:9]), Gather(own[None, 9:18])
    g0.near()
    rows0 = jnp.stack(row_halo(edge_row(images, 0), edge_row(images, tile_h - 1)))
    g0.join(rows0)
    g0.far()
    g0.low()
    images = after(images, g0.line_low)
    off_down = 2 * C
    off_up = off_down + TASKS * CA
    gb1 = norm_params[:, 0:C]
    gb2 = norm_params[:, C : 2 * C]
    gbd = norm_params[:, off_down:off_up]
    gbu = jnp.transpose(norm_params[:, off_up:].reshape(2, TASKS, C), (1, 0, 2)).reshape(-1, C)
    proj_low = proj_weight.astype(BF)
    down = jnp.transpose(proj_low[:, 0].reshape(TASKS, C, CA), (1, 0, 2)).reshape(C, TASKS * CA)
    up = jnp.transpose(proj_low[:, 1], (0, 2, 1, 3)).reshape(TASKS, CA, C)

    image_rows = to_rows(images)
    edges = jnp.concatenate([images[:, :, 0], images[:, :, tile_w - 1]], axis=0)
    edges = jnp.transpose(edges, (1, 0, 2))
    x3 = shift_copies(idx, image_rows, rows0, halo_cols(edges, rows0, batch), batch)
    g0.high(g0.low_x, g0.low_y)
    g0.corner_a(x3)
    g1.near(g0.line_high)
    g0.corner_b(g0.high_x, g1.near_got)

    cot = pooled_rows(cot_shared.astype(F32) * 0.25)

    g1.join(g0.corner_high)
    g1.far()
    g1.low()
    w0 = g0.pieces()
    z1, s1, edges1 = conv(after(idx, g1.line_low), x3, w0, False, F32, "conv_first", batch)

    halo1 = halo(edges1, batch)
    s1 = after(s1, g1.line_high, g1.low_x, g1.low_y)
    wt_mine = lax.all_gather(after(own[18:], s1), ("img", "ha"), axis=0, tiled=False)
    g1.high(s1)

    cot_tasks = after(cot_tasks, z1)
    depth_pick = jnp.arange(TASKS) == 1
    scale = jnp.where(depth_pick, depth_mask.astype(F32)[..., None], 1.0) * nash_weights
    weighted = cot_tasks.astype(F32).reshape(batch, half_h, half_w, TASKS, C)
    weighted = (weighted * (scale * 0.25)[..., None]).astype(BF)
    grid = jnp.transpose(weighted, (3, 1, 0, 2, 4))
    top, bottom = row_halo(grid[:, 0:1], grid[:, half_h - 1 :])
    top = jnp.where(ha > 0, top, jnp.zeros_like(top))
    bottom = jnp.where(ha < lax.axis_size("ha") - 1, bottom, jnp.zeros_like(bottom))
    grid = jnp.concatenate([top, grid, bottom], axis=1)
    left, right = col_halo(grid[:, :, :, 0:1], grid[:, :, :, half_w - 1 :])
    grid = jnp.concatenate([left, grid, right], axis=3)
    go3 = jnp.stack([grid[:, :, :, k : k + half_w] for k in range(3)], axis=1)
    go3 = go3.reshape(TASKS, 3, half_h + 2, q, C)
    def s1_ha(dep):
        return halo1

    def s1_img(dep):
        g1.corner_a(dep, g1.high_x, g1.high_y)
        g1.corner_b(dep, g1.high_x, g1.high_y)
        return g1.high_x, g1.high_y

    s1 = sum_all(s1, ha=s1_ha, img=s1_img)
    w1 = g1.pieces(s1)
    u3, hp, hc, hs = mid(
        after(idx, *w1[8:14]), s1, gb1, z1, *halo1, down, batch, count_all
    )
    corners = tuple(swap(after(part, hs), "wa", 1) for part in w1[6:8])
    w1 = w1[:14] + corners
    hs = after(hs, *corners)
    kept = {}

    def s2_img(dep):
        kept["z2"], kept["s2"], kept["edges2"] = conv(
            idx, after(u3, dep), w1, False, F32, "conv_second", batch
        )
        return (kept["s2"],)

    hs = sum_all(hs, ("wa", "img", "ha"), img=s2_img)
    z2, s2 = kept["z2"], kept["s2"]
    halo2 = halo(kept["edges2"], batch)
    h, hcb, ms = hidden(hs, gbd, hp, hc, up, tall, count_all)

    def s3_img(dep):
        return halo2 + (go3,)

    s2m = sum_all(jnp.concatenate([s2, ms], axis=0), ("wa", "img", "ha"), img=s3_img)
    s2, ms = s2m[0:2], s2m[2:]
    se, so, pooled = attend(
        idx, s2, gb2, ms, gbu, z2, *halo2, h, hcb, up, batch, count_all
    )
    wt_mine = after(wt_mine, pooled)
    wt = (wt_mine, swap(wt_mine, "wa", 1))
    halves_t = after(task_wgrad(after(idx, wt_mine), se, so, go3), wt[1])
    if lax.axis_size("wa") == 2:
        part_t = lax.psum_scatter(halves_t, "wa", scatter_dimension=0, tiled=True)[0]
    else:
        mine_t = lax.dynamic_index_in_dim(halves_t, wa % 2, keepdims=False)
        other_t = lax.dynamic_index_in_dim(halves_t, 1 - wa % 2, keepdims=False)
        part_t = add_low(mine_t, swap(other_t, "wa", 1))
    da, task_out = task_convs(after(idx, halves_t), go3, se, so, wt)
    dym, dy2, gsum, *edges2 = attend_back(
        s2, gb2, ms, gbu, z2, h, up, da, cot, batch, count_all
    )

    grad_t = lax.psum_scatter(
        after(part_t, gsum), ("img", "ha"), scatter_dimension=0, tiled=True
    )

    dhalo2 = halo(edges2, batch)

    def with_halo(dep):
        return dhalo2

    gsum = sum_all(gsum, ha=with_halo)
    dup, dh, dhs = mask_back(ms, gbu, gsum[0:6], hs, gbd, dym, h, hp, up, tall, count_all)

    def run_second_back(dep):
        gs = after(gsum[6:8], dep)
        kept["z3"] = norm_back(
            idx, s2, gb2, gs, dy2, dhalo2, z2, halo2, batch, count_all, "second_back"
        )
        return (kept["z3"],)

    def run_conv_back(dep):
        kept["part"] = conv(idx, after(kept["z3"], dep), w1, True, F32, "conv_second_back")
        return (kept["part"],)

    dhs = sum_all(dhs, ha=run_second_back, img=run_conv_back)
    z3, part = kept["z3"], kept["part"]
    ddown, dy1, gs1, *edges1 = first_back(
        hs, gbd, dhs, s1, gb1, dh, hp, u3, part, z1, down, batch, count_all
    )
    dhalo1 = halo(edges1, batch)

    def run_wgrad_second(dep):
        kept["r1"] = Scatter(*wgrad(after(idx, dep), u3, z3, "wgrad_second", (ddown, dup)))
        return (kept["r1"].other,) + tuple(dhalo1)

    def run_wa(dep):
        kept["r1"].wa(dep)
        return ()

    gs1 = sum_all(gs1, ha=run_wgrad_second, img=run_wa)
    r1 = kept["r1"]
    r1.corner_sum(gs1)
    r1.corner_send()
    y3 = norm_back(
        after(idx, r1.corner), s1, gb1, gs1, dy1, dhalo1, z1, halo1, batch, count_all, "first_norm_back"
    )
    r0 = Scatter(*wgrad(idx, x3, y3, "wgrad_first"))
    state = (conv_left, conv_right, conv_left_root, conv_right_root, conv_weight)
    r0.wa(r1.to_x, r1.to_y)
    r1.high_sum(r0.mine)
    r1.high_send()
    r1.low_sum(*r1.high)
    r1.low_send()
    r0.corner_sum(*r1.low)
    r0.corner_send(r1.high_x, r1.high_y)
    r1.far_sum(r0.corner)
    r1.far_send()
    image_grad = conv(after(idx, r0.corner, r1.far), y3, w0, True, BF, "conv_first_back")
    image_grad = after(image_grad, r0.to_x, r0.to_y, r1.from_far)
    r1.near_sum(image_grad)
    r1.near_send()
    r0.high_sum(r1.near)
    r0.high_send()
    r0.low_sum(*r0.high)
    r0.low_send()
    r0.far_sum(*r0.low)
    r0.far_send()
    grad1, grad1_other = r1.finish(r0.far)
    gradt = after(grad_t[0], grad1)
    step = 2
    while step < lax.axis_size("wa"):
        gradt = add_low(gradt, swap(gradt, "wa", step))
        step *= 2
    gradt_other = swap(gradt, "wa", 1)
    new = shampoo_conv(after(idx, grad1), gradt, gradt_other, state, 18, (), 0)
    r0.near_sum(new[0])
    r0.near_send()
    new = shampoo_conv(after(idx, r0.near), gradt, gradt_other, state, 18, new, 9)
    new = shampoo_conv(after(idx, new[0]), gradt, gradt_other, state, 18, new, 18)
    grad0, grad0_other = r0.finish(new[0])
    proj = ring_gather(gather_proj_core(after(grad1[9 * HB :], grad0)), "ha")
    new = shampoo_conv(
        after(idx, grad0), grad1[: 9 * HB], grad1_other[: 9 * HB], state, 9, new
    )
    proj_total = ring_gather(after(proj, new[0]), "img")
    new = shampoo_conv(after(idx, proj), grad0, grad0_other, state, 0, new)
    proj_total = after(proj_total, new[0]).reshape(TASKS, 2, NB, BLK, BLK)
    proj_total, proj_left_new, proj_right_new, proj_weight_new = shampoo_proj(
        proj_total, proj_left, proj_right, proj_left_root, proj_right_root, proj_weight
    )
    conv_total, conv_left_new, conv_right_new, conv_weight_new = new

    image_grad = from_rows(image_grad, batch)
    task_out = jnp.transpose(
        task_out.reshape(TASKS, half_h, batch, half_w, C), (2, 1, 3, 0, 4)
    ).reshape(batch, half_h, half_w, TASKS * C)
    shared_out = jnp.transpose(
        pooled.reshape(half_h, batch, half_w, C), (1, 0, 2, 3)
    )

    gram, norm_grad, moment_new, norm_new = norm_step(gs1, gsum, dhs, norm_params, norm_moment)
    return (
        shared_out,
        task_out,
        image_grad,
        gram,
        conv_total,
        conv_left_new,
        conv_right_new,
        conv_weight_new,
        proj_total,
        proj_left_new,
        proj_right_new,
        proj_weight_new,
        norm_grad,
        moment_new,
        norm_new,
    )


def solution(mesh):
    tile = P("img", "ha", "wa", None)
    owned = P(("img", "ha"), None, None, None)
    return jax.shard_map(
        shards,
        mesh=mesh,
        in_specs=(tile, tile, tile, P("img", "ha", "wa"), P()) + (owned,) * 5 + (P(),) * 7,
        out_specs=(tile, tile, tile, P()) + (owned,) * 4 + (P(),) * 7,
        check_vma=False,
    )
```
